32 devices in a mesh: rep: 2 (over y), ep: 4 (over z), tp: 2 (over x), sub: 2 (over core).
Axes of the slice: x: 2, y: 2, z: 4, core: 2. Of those that a mesh axis runs over, the one named last changes fastest.
Arguments:
- grad_values: bfloat16 [2048, 3584], P(('rep', 'ep', 'tp'), 'sub'), parts along dimension 0, may hold values from -6 to 6
- grad_scales: float32 [2048, 28], P(('rep', 'ep', 'tp'), 'sub'), parts along dimension 0, may hold values from 0.2 to 2
- expert_ids: int32 [2048, 1], P(('rep', 'ep', 'tp')), parts along dimension 0, may hold values from 0 to 3; in each aligned block of 128 rows (0 to 127, 128 to 255, ...) at most 36 rows name the same one
- route_weights: float32 [2048, 1], P(('rep', 'ep', 'tp')), parts along dimension 0, may hold values from 0.2 to 1
- w_gate: bfloat16 [4, 3584, 1024], P('ep', 'sub', 'tp'), may hold values from -0.1875 to 0.1875
- w_up: bfloat16 [4, 3584, 1024], P('ep', 'sub', 'tp'), may hold values from -0.1875 to 0.1875
- w_down: bfloat16 [4, 1024, 3584], P('ep', 'tp', 'sub'), may hold values from -0.09375 to 0.09375
- pre_acts: bfloat16 [8, 2, 288, 1024], P(('rep', 'ep'), None, None, 'tp'), parts along dimension 0, may hold values from -6 to 6
- latent_partials: bfloat16 [2, 2048, 512], P('tp', ('rep', 'ep'), 'sub'), parts along dimension 1, may hold values from -6 to 6
- latent: bfloat16 [2048, 512], P(('rep', 'ep', 'tp'), 'sub'), parts along dimension 0, may hold values from -120 to 120
- latent_gain: float32 [512], P('sub'), may hold values from 0.25 to 1.75
Outputs:
- grad_input: bfloat16 [2048, 3584], P(('rep', 'ep', 'tp'), 'sub'), parts along dimension 0
- d_latent: bfloat16 [2048, 512], P(('rep', 'ep', 'tp'), 'sub'), parts along dimension 0
The draws below stay inside these ranges and needn't reach their ends.
There are 2 independent parts, one for each index of `rep`. The reference program is written for one: setup_inputs(seed, part) draws one part's arguments, and reference() takes and returns one part's arrays. A program takes and returns all parts, laid end to end along the dimension named above; an argument that names none is the same for every part. Nothing has to cross between parts.
Inputs may be any that keep to these rules, and one draw needn't show every extreme that they name: `expert_ids`: among the routes of the tokens of one index pair of ep and tp, no expert is named more than 36 times.
All inputs are finite; a program needn't handle non-finite values.
Results may differ from the reference program's by a relative error of at most 0.0066.
Values may be sent and summed in bfloat16 or wider, within the bound.
No kernel may reach another device: no remote copies, remote signals or barrier semaphores. Data moves between devices by JAX's collectives and lax.ppermute only.
A program may use at most 64 MiB of HBM per device.

```python
import math
import jax
import jax.numpy as jnp
import numpy as np
from jax import lax

D = 3584
FF = 1024
LAT = 512
TOP = 1
TOK_DEV = 128
EXPERTS = 4
MOST = 36
SLOTS = 288
TOKENS = 1024
N_EP = 4
N_TP = 2


def draw_latent(key, part):
    key = jax.random.fold_in(key, 7)
    value_key, row_key, column_key = jax.random.split(key, 3)
    raw_values = jax.random.truncated_normal(value_key, -3.0, 3.0, (TOKENS, LAT), jnp.float32)
    row_scale = jnp.exp(jax.random.uniform(row_key, (TOKENS, 1), jnp.float32, 0.0, math.log(10.0)))
    column_scale = jnp.exp(jax.random.uniform(column_key, (1, LAT), jnp.float32, 0.0, math.log(4.0)))
    return (raw_values * row_scale * column_scale).astype(jnp.bfloat16)


def shard_levels(rng, shape, pieces, smallest, top_value):
    def one(axis_at, shards_of):
        draws = jax.random.uniform(jax.random.fold_in(jax.random.fold_in(rng, 6), axis_at), (shards_of,), jnp.float32, smallest / len(pieces), top_value / len(pieces))
        return jnp.repeat(jnp.exp(draws), shape[axis_at] // shards_of).reshape((-1,) + (1,) * (len(shape) - axis_at - 1))

    gain = one(*pieces[0])
    for cut in pieces[1:]:
        gain = gain * one(*cut)
    return gain


def shared_out(key, own, number, rows, amount, top, limit, lean):
    sequence = jax.random.permutation(key, amount)
    heavy_load, common = portions_of(amount, rows * top, limit, lean, True), portions_of(amount, rows * top, limit, lean, False)
    places = jnp.arange(amount)

    def named(lengths, turn):
        used = int((lengths > 0).sum())
        fixed = max(1, used // 4)
        shifted = fixed + (places - fixed + turn * (used - fixed)) % max(1, amount - fixed)
        return jnp.zeros((amount,), jnp.int32).at[sequence[jnp.where(places < fixed, places, shifted)]].set(jnp.asarray(lengths, jnp.int32))

    lengths = jnp.where(number % 4 == 0, named(heavy_load, number // 4), named(common, number - number // 4 - 1))
    mixed = jax.random.permutation(jax.random.fold_in(own, 3), amount)
    donor, receiver = mixed[0:amount // 2 * 2:2], mixed[1:amount // 2 * 2:2]
    margin = jnp.minimum(lengths[donor] - 1, limit - lengths[receiver]) // 2
    margin = jnp.where((donor == sequence[0]) | (receiver == sequence[0]) | (lengths[receiver] == 0), 0, jnp.maximum(margin, 0))
    shifted = jax.random.randint(jax.random.fold_in(own, 4), (amount // 2,), 0, 1 << 20) % (margin + 1)
    lengths = lengths.at[donor].add(-shifted).at[receiver].add(shifted)
    items = jnp.searchsorted(jnp.cumsum(lengths), jnp.arange(rows * top), side="right").astype(jnp.int32)
    table = items.reshape(top, rows).T
    table = table[jax.random.permutation(jax.random.fold_in(own, 1), rows)]
    turn = jax.random.randint(jax.random.fold_in(own, 2), (rows, 1), 0, top)
    return jnp.take_along_axis(table, (jnp.arange(top)[None, :] + turn) % top, axis=1)


def portions_of(count, total, limit, slope, full):
    weights = [(1 << 20) // math.isqrt(standing ** slope) + 1 for standing in range(1, count + 1)]
    largest = limit if full else min(limit, max(-(-total // count), total * weights[0] // sum(weights)))
    least = 1 if total - largest >= count - 1 else 0
    given, surplus = [largest] + [least] * (count - 1), total - largest - least * (count - 1)
    while surplus > 0:
        free = [i for i in range(1, count) if given[i] < largest] or [i for i in range(1, count) if given[i] < limit]
        pool, remaining = sum([weights[i] for i in free]), surplus
        for i in free:
            more = min(limit - given[i], max(1, remaining * weights[i] // pool), surplus)
            given[i] = given[i] + more
            surplus = surplus - more
    return np.array(given)


def bell_draw(own_key, shape, scale, most, cuts=(), held_as=jnp.bfloat16):
    values = scale * jax.random.normal(own_key, shape, jnp.float32)
    if cuts:
        values = values * shard_levels(own_key, shape, cuts, -0.22, 0.18)
    return jnp.clip(values, -most, most).astype(held_as)


def setup_inputs(seed: int = 0, part: int = 0) -> dict:
    key_of = jax.random.split(jax.random.key(seed), 12)
    part_splits = jax.random.split(jax.random.fold_in(key_of[11], part), 12)
    grad_values = bell_draw(part_splits[0], (TOKENS, D), 1.0, 6.0, ((0, 8), (1, 2)))
    grad_scales = jnp.clip(jnp.exp(math.log(2.0) - 2.3025851 * jax.random.uniform(part_splits[1], (TOKENS, D // 128), jnp.float32) ** shard_levels(part_splits[1], (TOKENS, D // 128), ((0, 8), (1, 2)), -0.2, 0.2)), 0.2, 2.0)
    expert_ids_keys = jax.random.split(jax.random.fold_in(part_splits[2], 1), TOKENS // TOK_DEV)
    expert_ids_turns = jax.random.permutation(jax.random.fold_in(part_splits[2], 3), TOKENS // TOK_DEV)
    expert_ids = jax.vmap(lambda own, number: shared_out(jax.random.fold_in(part_splits[2], 2), own, number, TOK_DEV, EXPERTS, TOP, MOST, 2))(expert_ids_keys, expert_ids_turns).reshape((TOKENS, TOP))
    route_weights = jnp.clip(0.2 + 0.8 * jax.random.uniform(part_splits[3], (TOKENS, TOP), jnp.float32) ** shard_levels(part_splits[3], (TOKENS, TOP), ((0, 8),), -0.2, 0.2), 0.2, 1.0)
    w_gate = bell_draw(key_of[4], (EXPERTS, D, FF), FF ** -0.5, 0.1875, ((0, 4), (1, 2), (2, 2)))
    w_up = bell_draw(key_of[5], (EXPERTS, D, FF), FF ** -0.5, 0.1875, ((0, 4), (1, 2), (2, 2)))
    w_down = bell_draw(key_of[6], (EXPERTS, FF, D), D ** -0.5, 0.09375, ((0, 4), (1, 2), (2, 2)))
    pre_acts = bell_draw(part_splits[7], (EXPERTS, 2, SLOTS, FF), 1.5, 6.0, ((0, 4), (3, 2)))
    latent_partials = bell_draw(part_splits[8], (N_TP, TOKENS, LAT), 1.0, 6.0, ((0, 2), (1, 4), (2, 2)))
    latent = draw_latent(jax.random.fold_in(jax.random.fold_in(key_of[11], part), 71), part)
    latent_gain = jnp.clip(1.0 + 0.15 * jax.random.normal(key_of[10], (LAT,), jnp.float32), 0.25, 1.75)
    return {"grad_values": grad_values, "grad_scales": grad_scales, "expert_ids": expert_ids, "route_weights": route_weights, "w_gate": w_gate, "w_up": w_up, "w_down": w_down, "pre_acts": pre_acts, "latent_partials": latent_partials, "latent": latent, "latent_gain": latent_gain}


def reference(grad_values, grad_scales, expert_ids, route_weights, w_gate, w_up, w_down, pre_acts, latent_partials, latent, latent_gain):
    scaled = (grad_values.astype(jnp.float32).reshape(TOKENS, D // 128, 128) * grad_scales[:, :, None]).reshape(TOKENS, D)
    weighted = (scaled[:, None, :] * route_weights[:, :, None]).astype(jnp.bfloat16).reshape(TOKENS * TOP, D)
    flat_ids = expert_ids.reshape(-1).astype(jnp.int32)
    onehot = (flat_ids[:, None] == jnp.arange(EXPERTS, dtype=jnp.int32)[None, :]).astype(jnp.int32)
    per_device = onehot.reshape(N_EP * N_TP, TOK_DEV * TOP, EXPERTS)
    earlier = jnp.cumsum(per_device, axis=1) - per_device
    position = lax.optimization_barrier(jnp.sum(earlier * per_device, axis=2)).reshape(-1).astype(jnp.int32)
    source = (jnp.arange(TOKENS * TOP, dtype=jnp.int32) // (TOK_DEV * TOP)).astype(jnp.int32)
    slot_index = (source * MOST + position).astype(jnp.int32)
    expert_in = jnp.zeros((EXPERTS, SLOTS, D), jnp.bfloat16).at[flat_ids, slot_index].set(weighted)
    block_width = FF // N_TP

    def one_expert(operands):
        rows, gate_weight, up_weight, down_weight, saved = operands
        hidden_grad = jnp.einsum('sd,fd->sf', rows.astype(jnp.float32), down_weight.astype(jnp.float32), precision=lax.Precision.HIGHEST)
        gate_pre = saved[0].astype(jnp.float32)
        up_pre = saved[1].astype(jnp.float32)
        sigmoid_gate = jax.nn.sigmoid(gate_pre)
        up_grad = (hidden_grad * gate_pre * sigmoid_gate).astype(jnp.bfloat16)
        gate_grad = (hidden_grad * up_pre * sigmoid_gate * (1.0 + gate_pre * (1.0 - sigmoid_gate))).astype(jnp.bfloat16)
        gate_blocks = gate_grad.astype(jnp.float32).reshape(SLOTS, N_TP, block_width)
        up_blocks = up_grad.astype(jnp.float32).reshape(SLOTS, N_TP, block_width)
        gate_matrix = gate_weight.astype(jnp.float32).reshape(D, N_TP, block_width)
        up_matrix = up_weight.astype(jnp.float32).reshape(D, N_TP, block_width)
        partial_value = jnp.einsum('sbf,dbf->bsd', gate_blocks, gate_matrix, precision=lax.Precision.HIGHEST)
        partial_value = partial_value + jnp.einsum('sbf,dbf->bsd', up_blocks, up_matrix, precision=lax.Precision.HIGHEST)
        rounded = lax.optimization_barrier(partial_value.astype(jnp.bfloat16))
        return lax.optimization_barrier(jnp.sum(rounded.astype(jnp.float32), axis=0))
    expert_out = lax.map(one_expert, (expert_in, w_gate, w_up, w_down, pre_acts))
    picked = expert_out[flat_ids, slot_index]
    grad_input = lax.optimization_barrier(jnp.sum(picked.reshape(TOKENS, TOP, D), axis=1)).astype(jnp.bfloat16)
    latent_grad = lax.optimization_barrier(jnp.sum(latent_partials.astype(jnp.float32), axis=0))
    values = latent.astype(jnp.float32)
    inverse_rms = lax.rsqrt(lax.optimization_barrier(jnp.mean(values * values, axis=1, keepdims=True)) + 1e-06)
    gained = latent_grad * latent_gain[None, :]
    cross = lax.optimization_barrier(jnp.sum(gained * values, axis=1, keepdims=True))
    d_latent = (inverse_rms * gained - values * inverse_rms ** 3 * cross / LAT).astype(jnp.bfloat16)
    return (grad_input, d_latent)
```

```python
import functools

import jax
import jax.numpy as jnp
from jax import lax
from jax.experimental import pallas as pl
from jax.experimental.pallas import tpu as pltpu
from jax.sharding import PartitionSpec as P

LAT = 512
NT = (((1,), (1,)), ((), ()))
TN = (((0,), (0,)), ((), ()))
VMEM = pl.BlockSpec(memory_space=pltpu.VMEM)
VMEM_LIMIT = 32 * 1024 * 1024


def dot(a, b, dims, precision=None):
    return lax.dot_general(a, b, dims, precision=precision, preferred_element_type=jnp.float32)


def swap(value, axis, step):
    count = lax.axis_size(axis)
    return lax.ppermute(value, axis, [(i, i ^ step) for i in range(count)])


def call(kernel, outs, *args, flops=0, name=None):
    read = sum(a.size * a.dtype.itemsize for a in args)
    written = sum(o.size * o.dtype.itemsize for o in outs)
    return pl.pallas_call(
        kernel,
        out_shape=outs,
        in_specs=[VMEM] * len(args),
        out_specs=[VMEM] * len(outs),
        compiler_params=pltpu.CompilerParams(vmem_limit_bytes=VMEM_LIMIT),
        cost_estimate=pl.CostEstimate(flops=flops, bytes_accessed=read + written, transcendentals=0),
        name=name,
    )(*args)


def pack_kernel(wide, most, ids_ref, weights_ref, scales_ref, grad_ref, *outs):
    blocks, place_ref = outs[:-1], outs[-1]
    tokens, width = grad_ref.shape
    half, scale_half = width // 2, scales_ref.shape[0] // 2
    rows = blocks[0].shape[0]
    me = lax.axis_index("ep")
    ids = ids_ref[...]
    expert = lax.broadcasted_iota(jnp.int32, (max(8, wide), tokens), 0)
    named = expert == ids
    before = lax.broadcasted_iota(jnp.int32, (tokens, tokens), 0) < lax.broadcasted_iota(
        jnp.int32, (tokens, tokens), 1
    )
    earlier = jnp.dot(
        named.astype(jnp.bfloat16), before.astype(jnp.bfloat16), preferred_element_type=jnp.float32
    )
    position = jnp.sum(jnp.where(named, earlier, 0.0), axis=0, keepdims=True).astype(jnp.int32)
    row = lax.broadcasted_iota(jnp.int32, (rows, tokens), 0)
    for k in range(wide):
        local = jnp.where(ids == (me ^ k), position, -2 * rows)
        low, high = row == local, row - most == local
        low_place, high_place = low.astype(jnp.bfloat16), high.astype(jnp.bfloat16)
        place_ref[0, k] = low_place
        place_ref[1, k] = high_place
        placed = jnp.dot(low_place, grad_ref[:, :half], preferred_element_type=jnp.float32)
        placed += jnp.dot(high_place, grad_ref[:, half:], preferred_element_type=jnp.float32)
        scale = dot(low.astype(jnp.float32), scales_ref[:scale_half], NT, lax.Precision.HIGHEST)
        scale += dot(high.astype(jnp.float32), scales_ref[scale_half:], NT, lax.Precision.HIGHEST)
        weight = jnp.sum(jnp.where(low | high, weights_ref[...], 0.0), axis=1, keepdims=True)
        for b in range(scale_half):
            part = slice(b * 128, (b + 1) * 128)
            blocks[k][:, part] = (placed[:, part] * scale[:, b : b + 1] * weight).astype(
                jnp.bfloat16
            )


def hidden_kernel(most, narrow, *refs):
    blocks, (down_ref, sum_ref, sent_ref) = refs[:-3], refs[-3:]
    half = down_ref.shape[1] // 2
    values = [b[...].astype(jnp.float32) for b in blocks]
    low = jnp.concatenate([v[:most] for v in values], axis=0).astype(jnp.bfloat16)
    high = jnp.concatenate([v[most : 2 * most] for v in values], axis=0).astype(jnp.bfloat16)
    total = dot(low, down_ref[:, :half], NT) + dot(high, down_ref[:, half:], NT)
    sum_ref[...] = total
    sent_ref[...] = total.astype(jnp.bfloat16)


def back_kernel(most, sum_ref, other_ref, pre_ref, gate_ref, up_ref, *outs):
    half = gate_ref.shape[0] // 2
    hidden = sum_ref[...] + other_ref[...].astype(jnp.float32)
    gate_pre = pre_ref[0].astype(jnp.float32)
    up_pre = pre_ref[1].astype(jnp.float32)
    sig = 1.0 / (1.0 + jnp.exp(-gate_pre))
    up_grad = (hidden * gate_pre * sig).astype(jnp.bfloat16)
    gate_grad = (hidden * up_pre * sig * (1.0 + gate_pre * (1.0 - sig))).astype(jnp.bfloat16)
    low = dot(gate_grad, gate_ref[:half], NT) + dot(up_grad, up_ref[:half], NT)
    high = dot(gate_grad, gate_ref[half:], NT) + dot(up_grad, up_ref[half:], NT)
    for i, out in enumerate(outs):
        part = slice(i * most, (i + 1) * most)
        pieces = [low[part], high[part]]
        spare = out.shape[0] - 2 * most
        if spare:
            pieces.append(jnp.zeros((spare, half), jnp.float32))
        out[...] = jnp.concatenate(pieces, axis=0).astype(jnp.bfloat16)


def unpack_kernel(wide, place_ref, *refs):
    blocks, out_ref = refs[:-1], refs[-1]
    half = out_ref.shape[1] // 2
    for side in range(2):
        total = None
        for k in range(wide):
            if k == 0:
                rows = blocks[0][...].astype(jnp.float32)
                for other in blocks[wide:]:
                    rows += other[...].astype(jnp.float32)
                rows = rows.astype(jnp.bfloat16)
            else:
                rows = blocks[k][...]
            term = dot(place_ref[side, k], rows, TN)
            total = term if total is None else total + term
        out_ref[:, side * half : (side + 1) * half] = total.astype(jnp.bfloat16)


def local(
    grad_values,
    grad_scales,
    expert_ids,
    route_weights,
    w_gate,
    w_up,
    w_down,
    pre_acts,
    latent_partials,
    latent,
    latent_gain,
):
    wide, narrow = lax.axis_size("ep"), lax.axis_size("tp")
    me, lane = lax.axis_index("ep"), lax.axis_index("tp")
    tokens, width = grad_values.shape
    half = width // 2
    slots, hidden_width = pre_acts.shape[2:]
    most = slots // (wide * narrow)
    rows = -(-2 * most // 8) * 8
    f32, bf16 = jnp.float32, jnp.bfloat16
    block = jax.ShapeDtypeStruct((rows, half), bf16)

    packed = call(
        functools.partial(pack_kernel, wide, most),
        [block] * wide + [jax.ShapeDtypeStruct((2, wide, rows, tokens), bf16)],
        expert_ids.reshape(1, tokens),
        route_weights.reshape(1, tokens),
        grad_scales.T,
        grad_values,
        name="pack",
    )
    place = packed[wide]
    order = list(range(wide - 1, 0, -1))
    arrived = {0: packed[0]}
    for k in order:
        arrived[k] = swap(packed[k], "ep", k)

    share = tokens
    partials = latent_partials.reshape(narrow, share, latent_partials.shape[2])
    own_grad = lax.dynamic_index_in_dim(partials, lane, 0, keepdims=False).astype(f32)
    for j in range(1, narrow):
        own_grad += swap(
            lax.dynamic_index_in_dim(partials, lane ^ j, 0, keepdims=False), "tp", j
        ).astype(f32)

    values = latent.astype(f32)
    gained = own_grad * latent_gain[None, :]
    sums = jnp.stack([jnp.sum(values * values, axis=1), jnp.sum(gained * values, axis=1)])
    for step in range(1, lax.axis_size("sub")):
        sums = sums + swap(sums, "sub", step)
    inverse_rms = lax.rsqrt(sums[0] / LAT + 1e-06)[:, None]
    d_latent = (inverse_rms * gained - values * inverse_rms**3 * sums[1][:, None] / LAT).astype(
        bf16
    )

    groups = [list(range(i, min(i + 4, wide))) for i in range(0, wide, 4)]
    returned = {}
    own = []
    for group in groups:
        taken = []
        for k in group:
            taken += [arrived[k]] + [swap(arrived[k], "tp", j) for j in range(1, narrow)]
        count = len(group) * narrow * most
        summed, sent = call(
            functools.partial(hidden_kernel, most, narrow),
            [
                jax.ShapeDtypeStruct((count, hidden_width), f32),
                jax.ShapeDtypeStruct((count, hidden_width), bf16),
            ],
            *taken,
            w_down[0],
            flops=2 * count * width * hidden_width,
            name="hidden",
        )
        received = swap(sent, "sub", 1)
        pre = jnp.concatenate(
            [
                lax.dynamic_slice_in_dim(
                    pre_acts[0], ((me ^ k) * narrow + (lane ^ j)) * most, most, axis=1
                )
                for k in group
                for j in range(narrow)
            ],
            axis=1,
        )
        products = call(
            functools.partial(back_kernel, most),
            [block] * (len(group) * narrow),
            summed,
            received,
            pre,
            w_gate[0],
            w_up[0],
            flops=4 * count * width * hidden_width,
            name="back",
        )
        for at, k in enumerate(group):
            mine = products[at * narrow]
            others = [swap(products[at * narrow + j], "tp", j) for j in range(1, narrow)]
            if k == 0:
                returned[0] = mine
                own = others
            else:
                total = mine.astype(f32)
                for other in others:
                    total += other.astype(f32)
                returned[k] = swap(total.astype(bf16), "ep", k)
    (grad_input,) = call(
        functools.partial(unpack_kernel, wide),
        [jax.ShapeDtypeStruct((tokens, width), bf16)],
        place,
        *[returned[k] for k in range(wide)],
        *own,
        name="unpack",
    )
    return (grad_input, d_latent)


def solution(mesh):
    placed = (
        P(("rep", "ep", "tp"), "sub"),
        P(("rep", "ep", "tp"), "sub"),
        P(("rep", "ep", "tp"), None),
        P(("rep", "ep", "tp"), None),
        P("ep", "sub", "tp"),
        P("ep", "sub", "tp"),
        P("ep", "tp", "sub"),
        P(("rep", "ep"), None, None, "tp"),
        P("tp", ("rep", "ep"), "sub"),
        P(("rep", "ep", "tp"), "sub"),
        P("sub"),
    )
    return jax.shard_map(
        local,
        mesh=mesh,
        in_specs=placed,
        out_specs=(P(("rep", "ep", "tp"), "sub"), P(("rep", "ep", "tp"), "sub")),
        check_vma=False,
    )
```

```python
import functools

import jax
import jax.numpy as jnp
from jax import lax
from jax.experimental import pallas as pl
from jax.experimental.pallas import tpu as pltpu
from jax.sharding import PartitionSpec as P

LAT = 512
NT = (((1,), (1,)), ((), ()))
TN = (((0,), (0,)), ((), ()))
VMEM = pl.BlockSpec(memory_space=pltpu.VMEM)
ANY = pl.BlockSpec(memory_space=pl.ANY)
HBM = pl.BlockSpec(memory_space=pltpu.HBM)
EXTRA = 16
VMEM_LIMIT = 20 * 1024 * 1024


def dot(a, b, dims, precision=None):
    return lax.dot_general(a, b, dims, precision=precision, preferred_element_type=jnp.float32)


def swap(value, axis, step):
    count = lax.axis_size(axis)
    return lax.ppermute(value, axis, [(i, i ^ step) for i in range(count)])


def call(kernel, outs, *args, cost=0, name=None, specs=None, scratch=(), limit=VMEM_LIMIT, earlier=()):
    specs = (specs or [VMEM] * len(args)) + [ANY] * len(earlier)
    if earlier:
        taken, body = len(args), kernel

        def kernel(*refs):
            body(*refs[:taken], *refs[taken + len(earlier) :])

    return pl.pallas_call(
        kernel,
        out_shape=outs,
        in_specs=specs,
        out_specs=[VMEM] * len(outs),
        scratch_shapes=scratch,
        compiler_params=pltpu.CompilerParams(vmem_limit_bytes=limit),
        cost_estimate=pl.CostEstimate(flops=0, bytes_accessed=cost, transcendentals=0),
        name=name,
    )(*args, *earlier)


def after(value, earlier, cost=0):
    return pl.pallas_call(
        lambda value_ref, earlier_ref, out_ref: None,
        out_shape=jax.ShapeDtypeStruct(value.shape, value.dtype),
        in_specs=[ANY, ANY],
        out_specs=ANY,
        input_output_aliases={0: 0},
        cost_estimate=pl.CostEstimate(flops=0, bytes_accessed=cost, transcendentals=0),
        name="after",
    )(value, earlier)


def fill(block_ref, most, low, high, weights_ref, scales_ref, grad_ref):
    half, scale_half = grad_ref.shape[1] // 2, scales_ref.shape[0] // 2
    placed = jnp.dot(
        low.astype(jnp.bfloat16), grad_ref[:, :half], preferred_element_type=jnp.float32
    )
    placed += jnp.dot(
        high.astype(jnp.bfloat16), grad_ref[:, half:], preferred_element_type=jnp.float32
    )
    scale = dot(low.astype(jnp.float32), scales_ref[:scale_half], NT, lax.Precision.HIGHEST)
    scale += dot(high.astype(jnp.float32), scales_ref[scale_half:], NT, lax.Precision.HIGHEST)
    weight = jnp.sum(jnp.where(low | high, weights_ref[...], 0.0), axis=1, keepdims=True)
    for b in range(scale_half):
        part = slice(b * 128, (b + 1) * 128)
        block_ref[:, part] = (placed[:, part] * scale[:, b : b + 1] * weight).astype(jnp.bfloat16)


def pack_kernel(wide, most, order, *refs):
    given, partial_ref, refs = refs[:4], refs[4], refs[5:]
    blocks, (place_ref, *held, share_ref) = refs[: len(order)], refs[len(order) : -3]
    ids_ref, sems, share_sems = refs[-3:]
    held = [ids_ref] + held
    lane = lax.axis_index("tp")
    shares = [
        pltpu.make_async_copy(partial_ref.at[lane ^ j], share_ref.at[j], share_sems.at[j])
        for j in range(partial_ref.shape[0])
    ]
    copies = [
        pltpu.make_async_copy(source, target, sems.at[i])
        for i, (source, target) in enumerate(zip(given, held))
    ]
    for copy in copies + shares:
        copy.start()
    copies[0].wait()
    weights_ref, scales_ref, grad_ref = held[1:]
    tokens, rows = grad_ref.shape[0], blocks[0].shape[0]
    me = lax.axis_index("ep")
    ids = ids_ref[...]
    expert = lax.broadcasted_iota(jnp.int32, (max(8, wide), tokens), 0)
    named = expert == ids
    before = lax.broadcasted_iota(jnp.int32, (tokens, tokens), 0) < lax.broadcasted_iota(
        jnp.int32, (tokens, tokens), 1
    )
    earlier = jnp.dot(
        named.astype(jnp.bfloat16), before.astype(jnp.bfloat16), preferred_element_type=jnp.float32
    )
    position = jnp.sum(jnp.where(named, earlier, 0.0), axis=0, keepdims=True).astype(jnp.int32)
    row = lax.broadcasted_iota(jnp.int32, (rows, tokens), 0)
    found = []
    for k in range(wide):
        local = jnp.where(ids == (me ^ k), position, -2 * rows)
        found.append((row == local, row - most == local))
        place_ref[0, k] = found[k][0].astype(jnp.bfloat16)
        place_ref[1, k] = found[k][1].astype(jnp.bfloat16)
    for copy in copies[1:]:
        copy.wait()
    for block_ref, k in zip(blocks, order):
        fill(block_ref, most, *found[k], weights_ref, scales_ref, grad_ref)
    for copy in shares:
        copy.wait()


def pack_more_kernel(most, order, place_ref, weights_ref, scales_ref, grad_ref, *blocks):
    for block_ref, k in zip(blocks, order):
        low, high = place_ref[0, k] != 0, place_ref[1, k] != 0
        fill(block_ref, most, low, high, weights_ref, scales_ref, grad_ref)


def hidden_kernel(most, extra, *refs):
    blocks, (down_ref, sum_ref, sent_ref) = refs[:-3], refs[-3:]
    half = down_ref.shape[1] // 2
    count = sum_ref.shape[0]
    if extra:
        blocks, row_sums = blocks[:-1], blocks[-1][...]
        high = row_sums.astype(jnp.bfloat16).astype(jnp.float32)
        spare = jnp.zeros((EXTRA - 4, row_sums.shape[1]), jnp.float32)
        tail = jnp.concatenate([high, row_sums - high, spare], axis=0)
        sent_ref[count:, :] = jnp.zeros((EXTRA, sent_ref.shape[1]), jnp.bfloat16)
        sent_ref[count:, : row_sums.shape[1]] = tail.astype(jnp.bfloat16)
    values = [b[...].astype(jnp.float32) for b in blocks]
    low = jnp.concatenate([v[:most] for v in values], axis=0).astype(jnp.bfloat16)
    high = jnp.concatenate([v[most : 2 * most] for v in values], axis=0).astype(jnp.bfloat16)
    total = dot(low, down_ref[:, :half], NT) + dot(high, down_ref[:, half:], NT)
    sum_ref[...] = total
    sent_ref[:count, :] = total.astype(jnp.bfloat16)


def by_xor(value, most, narrow, lane):
    step = 1
    while step < narrow:
        pieces = [value[i * most : (i + step) * most] for i in range(0, narrow, step)]
        turned = [pieces[i ^ 1] for i in range(len(pieces))]
        value = jnp.where((lane & step) != 0, jnp.concatenate(turned, axis=0), value)
        step *= 2
    return value


def back_kernel(most, narrow, group, sum_ref, other_ref, pre_ref, gate_ref, up_ref, *outs):
    half = gate_ref.shape[0] // 2
    me, lane = lax.axis_index("ep"), lax.axis_index("tp")
    hidden = sum_ref[...] + other_ref[: sum_ref.shape[0], :].astype(jnp.float32)
    gate_pre, up_pre = [
        jnp.concatenate(
            [by_xor(pre_ref[i, me ^ k].astype(jnp.float32), most, narrow, lane) for k in group],
            axis=0,
        )
        for i in range(2)
    ]
    sig = 1.0 / (1.0 + jnp.exp(-gate_pre))
    up_grad = (hidden * gate_pre * sig).astype(jnp.bfloat16)
    gate_grad = (hidden * up_pre * sig * (1.0 + gate_pre * (1.0 - sig))).astype(jnp.bfloat16)
    low = dot(gate_grad, gate_ref[:half], NT) + dot(up_grad, up_ref[:half], NT)
    high = dot(gate_grad, gate_ref[half:], NT) + dot(up_grad, up_ref[half:], NT)
    for i, out in enumerate(outs):
        part = slice(i * most, (i + 1) * most)
        pieces = [low[part], high[part]]
        spare = out.shape[0] - 2 * most
        if spare:
            pieces.append(jnp.zeros((spare, half), jnp.float32))
        out[...] = jnp.concatenate(pieces, axis=0).astype(jnp.bfloat16)


def unpack_kernel(wide, place_ref, *refs):
    blocks, out_ref = refs[:-1], refs[-1]
    half = out_ref.shape[1] // 2
    for side in range(2):
        total = None
        for k in range(wide):
            if k == 0:
                rows = blocks[0][...].astype(jnp.float32)
                for other in blocks[wide:]:
                    rows += other[...].astype(jnp.float32)
                rows = rows.astype(jnp.bfloat16)
            else:
                rows = blocks[k][...]
            term = dot(place_ref[side, k], rows, TN)
            total = term if total is None else total + term
        out_ref[:, side * half : (side + 1) * half] = total.astype(jnp.bfloat16)


def groups_of(wide):
    left = list(range(wide - 1, -1, -1))
    if wide < 4:
        return [left]
    return [[left[0], left[-1]]] + [left[i : min(i + 2, wide - 1)] for i in range(1, wide - 1, 2)]


def local(
    grad_values,
    grad_scales,
    expert_ids,
    route_weights,
    w_gate,
    w_up,
    w_down,
    pre_acts,
    latent_partials,
    latent,
    latent_gain,
):
    wide, narrow = lax.axis_size("ep"), lax.axis_size("tp")
    tokens, width = grad_values.shape
    half = width // 2
    slots, hidden_width = pre_acts.shape[2:]
    most = slots // (wide * narrow)
    rows = -(-2 * most // 8) * 8
    f32, bf16 = jnp.float32, jnp.bfloat16
    block = jax.ShapeDtypeStruct((rows, half), bf16)

    groups = groups_of(wide)
    order, more = groups[0], [k for group in groups[1:] for k in reversed(group)]
    packed = call(
        functools.partial(pack_kernel, wide, most, order),
        [block] * len(order)
        + [
            jax.ShapeDtypeStruct((2, wide, rows, tokens), bf16),
            jax.ShapeDtypeStruct((1, tokens), f32),
            jax.ShapeDtypeStruct((grad_scales.shape[1], tokens), f32),
            jax.ShapeDtypeStruct((tokens, width), bf16),
            jax.ShapeDtypeStruct((narrow, tokens, latent.shape[1]), bf16),
        ],
        expert_ids.reshape(1, tokens),
        route_weights.reshape(1, tokens),
        grad_scales.T,
        grad_values,
        latent_partials.reshape(narrow, tokens, latent.shape[1]),
        specs=[HBM] * 5,
        scratch=[
            pltpu.VMEM((1, tokens), jnp.int32),
            pltpu.SemaphoreType.DMA((4,)),
            pltpu.SemaphoreType.DMA((narrow,)),
        ],
        limit=None,
        name="pack",
    )
    place, *fillers, shares = packed[len(order) :]
    packed = dict(zip(order, packed))
    if more:
        blocks = call(
            functools.partial(pack_more_kernel, most, more),
            [block] * len(more),
            place,
            *fillers,
            cost=1 << 25,
            name="pack_more",
        )
        packed.update(zip(more, blocks))

    def across(k, rows_of_k):
        return [rows_of_k] + [swap(rows_of_k, "tp", j) for j in range(1, narrow)]

    taken = {0: across(0, packed[0])}
    first = groups[0][0]
    arrived = {}
    for k in order + more:
        if k:
            arrived[k] = swap(packed[k], "ep", k)
            if len(groups) > 1 and k == groups[1][0]:
                arrived[k] = after(arrived[k], place, 1 << 25)
    pre = pre_acts.reshape(2, wide, narrow * most, hidden_width)
    latent_parts = [shares[0]] + [
        swap(after(shares[j], taken[0][-1]), "tp", j) for j in range(1, narrow)
    ]

    returned = {}
    own = []
    values = latent.astype(f32)
    received, products, moved = None, None, None
    for group in groups:
        for k in group:
            if k == 0:
                continue
            taken[k] = across(k, arrived[k])
        count = len(group) * narrow * most
        extra = group is groups[-1]
        if extra:
            if received is not None:
                latent_parts[-1] = after(latent_parts[-1], summed)
            own_grad = sum(part.astype(f32) for part in latent_parts)
            gained = own_grad * latent_gain[None, :]
            row_sums = jnp.stack(
                [jnp.sum(values * values, axis=1), jnp.sum(gained * values, axis=1)]
            )
        summed, sent = call(
            functools.partial(hidden_kernel, most, extra),
            [
                jax.ShapeDtypeStruct((count, hidden_width), f32),
                jax.ShapeDtypeStruct((count + (EXTRA if extra else 0), hidden_width), bf16),
            ],
            *[rows_of_k for k in group for rows_of_k in taken[k]],
            *([row_sums] if extra else []),
            w_down[0],
            name="hidden",
            earlier=products[:1] if products else [arrived[g[0]] for g in groups[1:2]],
        )
        received = swap(sent, "sub", 1)
        products = call(
            functools.partial(back_kernel, most, narrow, group),
            [block] * (len(group) * narrow),
            summed,
            received,
            pre,
            w_gate[0],
            w_up[0],
            name="back",
            earlier=(moved,) if moved is not None else (),
        )
        for at, k in enumerate(group):
            mine = products[at * narrow]
            if k == 0:
                returned[0] = mine
                own = products[1 + at * narrow : (at + 1) * narrow]
            else:
                others = [swap(products[at * narrow + j], "tp", j) for j in range(1, narrow)]
                total = mine.astype(f32)
                for other in others:
                    total += other.astype(f32)
                moved = total.astype(bf16)
                returned[k] = swap(moved, "ep", k)
                last = moved if k == group[0] else last
    own = [swap(after(value, last), "tp", j + 1) for j, value in enumerate(own)]
    tail = received[count : count + 4, :tokens].astype(f32)
    row_sums = row_sums + tail[:2] + tail[2:]
    inverse_rms = lax.rsqrt(row_sums[0] / LAT + 1e-06)[:, None]
    d_latent = (
        inverse_rms * gained - values * inverse_rms**3 * row_sums[1][:, None] / LAT
    ).astype(bf16)
    (grad_input,) = call(
        functools.partial(unpack_kernel, wide),
        [jax.ShapeDtypeStruct((tokens, width), bf16)],
        place,
        *[returned[k] for k in range(wide)],
        *own,
        name="unpack",
    )
    return (grad_input, d_latent)


def solution(mesh):
    placed = (
        P(("rep", "ep", "tp"), "sub"),
        P(("rep", "ep", "tp"), "sub"),
        P(("rep", "ep", "tp"), None),
        P(("rep", "ep", "tp"), None),
        P("ep", "sub", "tp"),
        P("ep", "sub", "tp"),
        P("ep", "tp", "sub"),
        P(("rep", "ep"), None, None, "tp"),
        P("tp", ("rep", "ep"), "sub"),
        P(("rep", "ep", "tp"), "sub"),
        P("sub"),
    )
    return jax.shard_map(
        local,
        mesh=mesh,
        in_specs=placed,
        out_specs=(P(("rep", "ep", "tp"), "sub"), P(("rep", "ep", "tp"), "sub")),
        check_vma=False,
    )
```

```python
import functools

import jax
import jax.numpy as jnp
from jax import lax
from jax.experimental import pallas as pl
from jax.experimental.pallas import tpu as pltpu
from jax.sharding import PartitionSpec as P

LAT = 512
NT = (((1,), (1,)), ((), ()))
TN = (((0,), (0,)), ((), ()))
VMEM = pl.BlockSpec(memory_space=pltpu.VMEM)
ANY = pl.BlockSpec(memory_space=pl.ANY)
HBM = pl.BlockSpec(memory_space=pltpu.HBM)
EXTRA = 16
VMEM_LIMIT = 20 * 1024 * 1024


def dot(a, b, dims, precision=None):
    return lax.dot_general(a, b, dims, precision=precision, preferred_element_type=jnp.float32)


def swap(value, axis, step):
    count = lax.axis_size(axis)
    return lax.ppermute(value, axis, [(i, i ^ step) for i in range(count)])


def pinned(*arrays):
    return [pltpu.with_memory_space_constraint(array, pltpu.HBM) for array in arrays]


def like(array):
    return pltpu.VMEM(array.shape, array.dtype)


def call(kernel, outs, *args, cost=0, name=None, specs=None, scratch=(), earlier=()):
    specs = (specs or [VMEM] * len(args)) + [ANY] * len(earlier)
    if earlier:
        taken, body = len(args), kernel

        def kernel(*refs):
            body(*refs[:taken], *refs[taken + len(earlier) :])

    return pl.pallas_call(
        kernel,
        out_shape=outs,
        in_specs=specs,
        out_specs=[VMEM] * len(outs),
        scratch_shapes=scratch,
        compiler_params=pltpu.CompilerParams(vmem_limit_bytes=VMEM_LIMIT),
        cost_estimate=pl.CostEstimate(flops=0, bytes_accessed=cost, transcendentals=0),
        name=name,
    )(*args, *earlier)


def after(value, earlier, cost=0):
    return pl.pallas_call(
        lambda value_ref, earlier_ref, out_ref: None,
        out_shape=jax.ShapeDtypeStruct(value.shape, value.dtype),
        in_specs=[ANY, ANY],
        out_specs=ANY,
        input_output_aliases={0: 0},
        cost_estimate=pl.CostEstimate(flops=0, bytes_accessed=cost, transcendentals=0),
        name="after",
    )(value, earlier)


def fill(block_ref, most, low, high, weights_ref, scales_ref, grad_ref):
    half, scale_half = grad_ref.shape[1] // 2, scales_ref.shape[0] // 2
    placed = jnp.dot(
        low.astype(jnp.bfloat16), grad_ref[:, :half], preferred_element_type=jnp.float32
    )
    placed += jnp.dot(
        high.astype(jnp.bfloat16), grad_ref[:, half:], preferred_element_type=jnp.float32
    )
    scale = dot(low.astype(jnp.float32), scales_ref[:scale_half], NT, lax.Precision.HIGHEST)
    scale += dot(high.astype(jnp.float32), scales_ref[scale_half:], NT, lax.Precision.HIGHEST)
    weight = jnp.sum(jnp.where(low | high, weights_ref[...], 0.0), axis=1, keepdims=True)
    for b in range(scale_half):
        part = slice(b * 128, (b + 1) * 128)
        block_ref[:, part] = (placed[:, part] * scale[:, b : b + 1] * weight).astype(jnp.bfloat16)


def fetch(sources, targets, sems, first=0):
    copies = [
        pltpu.make_async_copy(source, target, sems.at[first + i])
        for i, (source, target) in enumerate(zip(sources, targets))
    ]
    for copy in copies:
        copy.start()
    return copies


def pack_kernel(wide, most, order, *refs):
    given, refs = refs[:4], refs[4:]
    blocks, (place_ref, *held) = refs[: len(order)], refs[len(order) : -2]
    ids_ref, sems = refs[-2:]
    held = [ids_ref] + held
    copies = fetch(given, held, sems)
    copies[0].wait()
    weights_ref, scales_ref, grad_ref = held[1:]
    tokens, rows = grad_ref.shape[0], blocks[0].shape[0]
    me = lax.axis_index("ep")
    ids = ids_ref[...]
    expert = lax.broadcasted_iota(jnp.int32, (max(8, wide), tokens), 0)
    named = expert == ids
    before = lax.broadcasted_iota(jnp.int32, (tokens, tokens), 0) < lax.broadcasted_iota(
        jnp.int32, (tokens, tokens), 1
    )
    earlier = jnp.dot(
        named.astype(jnp.bfloat16), before.astype(jnp.bfloat16), preferred_element_type=jnp.float32
    )
    position = jnp.sum(jnp.where(named, earlier, 0.0), axis=0, keepdims=True).astype(jnp.int32)
    row = lax.broadcasted_iota(jnp.int32, (rows, tokens), 0)
    found = []
    for k in range(wide):
        local = jnp.where(ids == (me ^ k), position, -2 * rows)
        found.append((row == local, row - most == local))
        place_ref[0, k] = found[k][0].astype(jnp.bfloat16)
        place_ref[1, k] = found[k][1].astype(jnp.bfloat16)
    for copy in copies[1:]:
        copy.wait()
    for block_ref, k in zip(blocks, order):
        fill(block_ref, most, *found[k], weights_ref, scales_ref, grad_ref)


def pack_more_kernel(most, order, place_ref, weights_ref, scales_ref, grad_ref, partial_ref, *refs):
    taken = (len(refs) - 3 - len(order)) // 2
    given, blocks, (share_ref, *held) = refs[:taken], refs[taken : -taken - 3], refs[-taken - 3 : -2]
    sems, share_sems = refs[-2:]
    lane, count = lax.axis_index("tp"), partial_ref.shape[0]
    copies = fetch(
        [partial_ref.at[lane ^ j] for j in range(count)],
        [share_ref.at[j] for j in range(count)],
        share_sems,
    )
    copies += fetch(given, held, sems)
    for block_ref, k in zip(blocks, order):
        low, high = place_ref[0, k] != 0, place_ref[1, k] != 0
        fill(block_ref, most, low, high, weights_ref, scales_ref, grad_ref)
    for copy in copies:
        copy.wait()


def hidden_kernel(most, extra, *refs):
    blocks, (down_ref, sum_ref, sent_ref) = refs[:-3], refs[-3:]
    half = down_ref.shape[1] // 2
    count = sum_ref.shape[0]
    if extra:
        blocks, row_sums = blocks[:-1], blocks[-1][...]
        high = row_sums.astype(jnp.bfloat16).astype(jnp.float32)
        spare = jnp.zeros((EXTRA - 4, row_sums.shape[1]), jnp.float32)
        tail = jnp.concatenate([high, row_sums - high, spare], axis=0)
        sent_ref[count:, :] = jnp.zeros((EXTRA, sent_ref.shape[1]), jnp.bfloat16)
        sent_ref[count:, : row_sums.shape[1]] = tail.astype(jnp.bfloat16)
    values = [b[...].astype(jnp.float32) for b in blocks]
    low = jnp.concatenate([v[:most] for v in values], axis=0).astype(jnp.bfloat16)
    high = jnp.concatenate([v[most : 2 * most] for v in values], axis=0).astype(jnp.bfloat16)
    total = dot(low, down_ref[:, :half], NT) + dot(high, down_ref[:, half:], NT)
    sum_ref[...] = total
    sent_ref[:count, :] = total.astype(jnp.bfloat16)


def by_xor(value, most, narrow, lane):
    step = 1
    while step < narrow:
        pieces = [value[i * most : (i + step) * most] for i in range(0, narrow, step)]
        turned = [pieces[i ^ 1] for i in range(len(pieces))]
        value = jnp.where((lane & step) != 0, jnp.concatenate(turned, axis=0), value)
        step *= 2
    return value


def back_kernel(most, narrow, group, sum_ref, other_ref, pre_ref, gate_ref, up_ref, *outs):
    half = gate_ref.shape[0] // 2
    me, lane = lax.axis_index("ep"), lax.axis_index("tp")
    hidden = sum_ref[...] + other_ref[: sum_ref.shape[0], :].astype(jnp.float32)
    gate_pre, up_pre = [
        jnp.concatenate(
            [by_xor(pre_ref[i, me ^ k].astype(jnp.float32), most, narrow, lane) for k in group],
            axis=0,
        )
        for i in range(2)
    ]
    sig = 1.0 / (1.0 + jnp.exp(-gate_pre))
    up_grad = (hidden * gate_pre * sig).astype(jnp.bfloat16)
    gate_grad = (hidden * up_pre * sig * (1.0 + gate_pre * (1.0 - sig))).astype(jnp.bfloat16)
    low = dot(gate_grad, gate_ref[:half], NT) + dot(up_grad, up_ref[:half], NT)
    high = dot(gate_grad, gate_ref[half:], NT) + dot(up_grad, up_ref[half:], NT)
    for i, out in enumerate(outs):
        part = slice(i * most, (i + 1) * most)
        pieces = [low[part], high[part]]
        spare = out.shape[0] - 2 * most
        if spare:
            pieces.append(jnp.zeros((spare, half), jnp.float32))
        out[...] = jnp.concatenate(pieces, axis=0).astype(jnp.bfloat16)


def unpack_kernel(wide, place_ref, *refs):
    blocks, out_ref = refs[:-1], refs[-1]
    half = out_ref.shape[1] // 2
    for side in range(2):
        total = None
        for k in range(wide):
            if k == 0:
                rows = blocks[0][...].astype(jnp.float32)
                for other in blocks[wide:]:
                    rows += other[...].astype(jnp.float32)
                rows = rows.astype(jnp.bfloat16)
            else:
                rows = blocks[k][...]
            term = dot(place_ref[side, k], rows, TN)
            total = term if total is None else total + term
        out_ref[:, side * half : (side + 1) * half] = total.astype(jnp.bfloat16)


def groups_of(wide):
    left = list(range(wide - 1, -1, -1))
    if wide < 4:
        return [left]
    return [[left[0], left[-1]]] + [left[i : min(i + 2, wide - 1)] for i in range(1, wide - 1, 2)]


def local(
    grad_values,
    grad_scales,
    expert_ids,
    route_weights,
    w_gate,
    w_up,
    w_down,
    pre_acts,
    latent_partials,
    latent,
    latent_gain,
):
    wide, narrow = lax.axis_size("ep"), lax.axis_size("tp")
    tokens, width = grad_values.shape
    half = width // 2
    slots, hidden_width = pre_acts.shape[2:]
    most = slots // (wide * narrow)
    rows = -(-2 * most // 8) * 8
    f32, bf16 = jnp.float32, jnp.bfloat16
    block = pltpu.VMEM((rows, half), bf16)
    groups = groups_of(wide)
    order, more = groups[0], [k for group in groups[1:] for k in reversed(group)]
    packed = call(
        functools.partial(pack_kernel, wide, most, order),
        [block] * len(order)
        + [
            pltpu.VMEM((2, wide, rows, tokens), bf16),
            pltpu.VMEM((1, tokens), f32),
            pltpu.VMEM((grad_scales.shape[1], tokens), f32),
            pltpu.VMEM((tokens, width), bf16),
        ],
        *pinned(
            expert_ids.reshape(1, tokens),
            route_weights.reshape(1, tokens),
            grad_scales.T,
            grad_values,
        ),
        specs=[HBM] * 4,
        scratch=[pltpu.VMEM((1, tokens), jnp.int32), pltpu.SemaphoreType.DMA((4,))],
        name="pack",
    )
    place, *fillers = packed[len(order) :]
    packed = dict(zip(order, packed))
    partials = latent_partials.reshape(narrow, tokens, latent.shape[1])
    fetched = [
        w_down[0],
        pre_acts.reshape(2, wide, narrow * most, hidden_width),
        w_gate[0],
        w_up[0],
        latent,
        latent_gain.reshape(1, -1),
    ]
    blocks = call(
        functools.partial(pack_more_kernel, most, more),
        [block] * len(more) + [like(partials)] + [like(array) for array in fetched],
        place,
        *fillers,
        *pinned(partials, *fetched),
        specs=[VMEM] * 4 + [HBM] * (1 + len(fetched)),
        scratch=[
            pltpu.SemaphoreType.DMA((len(fetched),)),
            pltpu.SemaphoreType.DMA((narrow,)),
        ],
        cost=1 << 25,
        name="pack_more",
    )
    packed.update(zip(more, blocks))
    shares, down, pre, gate, up, latent, latent_gain = blocks[len(more) :]

    def across(k, rows_of_k):
        return [rows_of_k] + [swap(rows_of_k, "tp", j) for j in range(1, narrow)]

    taken = {0: across(0, packed[0])}
    first = groups[0][0]
    arrived = {}
    for k in order + more:
        if k:
            arrived[k] = swap(packed[k], "ep", k)
            if len(groups) > 1 and k == groups[1][0]:
                arrived[k] = after(arrived[k], packed[first], 1 << 25)
    latent_parts = [shares[0]] + [
        swap(after(shares[j], taken[0][-1]), "tp", j) for j in range(1, narrow)
    ]

    returned = {}
    own = []
    values = latent.astype(f32)
    received, products, moved = None, None, None
    for group in groups:
        for k in group:
            if k == 0:
                continue
            taken[k] = across(k, arrived[k])
        count = len(group) * narrow * most
        extra = group is groups[-1]
        if extra:
            if received is not None:
                latent_parts[-1] = after(latent_parts[-1], summed)
            own_grad = sum(part.astype(f32) for part in latent_parts)
            gained = own_grad * latent_gain
            row_sums = jnp.stack(
                [jnp.sum(values * values, axis=1), jnp.sum(gained * values, axis=1)]
            )
        summed, sent = call(
            functools.partial(hidden_kernel, most, extra),
            [
                pltpu.VMEM((count, hidden_width), f32),
                pltpu.VMEM((count + (EXTRA if extra else 0), hidden_width), bf16),
            ],
            *[rows_of_k for k in group for rows_of_k in taken[k]],
            *([row_sums] if extra else []),
            down,
            name="hidden",
            earlier=products[:1] if products else [arrived[g[0]] for g in groups[1:2]],
        )
        received = swap(sent, "sub", 1)
        products = call(
            functools.partial(back_kernel, most, narrow, group),
            [block] * (len(group) * narrow),
            summed,
            received,
            pre,
            gate,
            up,
            name="back",
            earlier=(moved,) if moved is not None else (),
        )
        for at, k in enumerate(group):
            mine = products[at * narrow]
            if k == 0:
                returned[0] = mine
                own = products[1 + at * narrow : (at + 1) * narrow]
            else:
                others = [swap(products[at * narrow + j], "tp", j) for j in range(1, narrow)]
                if k == group[0]:
                    others[0] = after(others[0], mine, 1 << 24)
                total = mine.astype(f32)
                for other in others:
                    total += other.astype(f32)
                moved = total.astype(bf16)
                returned[k] = swap(moved, "ep", k)
                last = moved if k == group[0] else last
    own = [swap(after(value, last), "tp", j + 1) for j, value in enumerate(own)]
    tail = received[count : count + 4, :tokens].astype(f32)
    row_sums = row_sums + tail[:2] + tail[2:]
    inverse_rms = lax.rsqrt(row_sums[0] / LAT + 1e-06)[:, None]
    d_latent = (
        inverse_rms * gained - values * inverse_rms**3 * row_sums[1][:, None] / LAT
    ).astype(bf16)
    (grad_input,) = call(
        functools.partial(unpack_kernel, wide),
        [jax.ShapeDtypeStruct((tokens, width), bf16)],
        place,
        *[returned[k] for k in range(wide)],
        *own,
        name="unpack",
    )
    return (grad_input, d_latent)


def solution(mesh):
    placed = (
        P(("rep", "ep", "tp"), "sub"),
        P(("rep", "ep", "tp"), "sub"),
        P(("rep", "ep", "tp"), None),
        P(("rep", "ep", "tp"), None),
        P("ep", "sub", "tp"),
        P("ep", "sub", "tp"),
        P("ep", "tp", "sub"),
        P(("rep", "ep"), None, None, "tp"),
        P("tp", ("rep", "ep"), "sub"),
        P(("rep", "ep", "tp"), "sub"),
        P("sub"),
    )
    return jax.shard_map(
        local,
        mesh=mesh,
        in_specs=placed,
        out_specs=(P(("rep", "ep", "tp"), "sub"), P(("rep", "ep", "tp"), "sub")),
        check_vma=False,
    )
```

```python
import functools

import jax
import jax.numpy as jnp
from jax import lax
from jax.experimental import pallas as pl
from jax.experimental.pallas import tpu as pltpu
from jax.sharding import PartitionSpec as P

LAT = 512
NT = (((1,), (1,)), ((), ()))
TN = (((0,), (0,)), ((), ()))
VMEM = pl.BlockSpec(memory_space=pltpu.VMEM)
ANY = pl.BlockSpec(memory_space=pl.ANY)
HBM = pl.BlockSpec(memory_space=pltpu.HBM)
EXTRA = 16
VMEM_LIMIT = 20 * 1024 * 1024


def dot(a, b, dims, precision=None):
    return lax.dot_general(a, b, dims, precision=precision, preferred_element_type=jnp.float32)


def swap(value, axis, step):
    count = lax.axis_size(axis)
    return lax.ppermute(value, axis, [(i, i ^ step) for i in range(count)])


def pinned(*arrays):
    return [pltpu.with_memory_space_constraint(array, pltpu.HBM) for array in arrays]


def like(array):
    return pltpu.VMEM(array.shape, array.dtype)


def call(kernel, outs, *args, cost=0, name=None, specs=None, scratch=(), earlier=()):
    specs = (specs or [VMEM] * len(args)) + [ANY] * len(earlier)
    if earlier:
        taken, body = len(args), kernel

        def kernel(*refs):
            body(*refs[:taken], *refs[taken + len(earlier) :])

    return pl.pallas_call(
        kernel,
        out_shape=outs,
        in_specs=specs,
        out_specs=[VMEM] * len(outs),
        scratch_shapes=scratch,
        compiler_params=pltpu.CompilerParams(vmem_limit_bytes=VMEM_LIMIT),
        cost_estimate=pl.CostEstimate(flops=0, bytes_accessed=cost, transcendentals=0),
        name=name,
    )(*args, *earlier)


def after(value, earlier, cost=0):
    return pl.pallas_call(
        lambda value_ref, earlier_ref, out_ref: None,
        out_shape=jax.ShapeDtypeStruct(value.shape, value.dtype),
        in_specs=[ANY, ANY],
        out_specs=ANY,
        input_output_aliases={0: 0},
        compiler_params=pltpu.CompilerParams(vmem_limit_bytes=1 << 17),
        cost_estimate=pl.CostEstimate(flops=0, bytes_accessed=cost, transcendentals=0),
        name="after",
    )(value, earlier)


def fill(block_ref, most, low, high, weights_ref, scales_ref, grad_ref):
    half, scale_half = grad_ref.shape[1] // 2, scales_ref.shape[0] // 2
    placed = jnp.dot(
        low.astype(jnp.bfloat16), grad_ref[:, :half], preferred_element_type=jnp.float32
    )
    placed += jnp.dot(
        high.astype(jnp.bfloat16), grad_ref[:, half:], preferred_element_type=jnp.float32
    )
    scale = dot(low.astype(jnp.float32), scales_ref[:scale_half], NT, lax.Precision.HIGHEST)
    scale += dot(high.astype(jnp.float32), scales_ref[scale_half:], NT, lax.Precision.HIGHEST)
    weight = jnp.sum(jnp.where(low | high, weights_ref[...], 0.0), axis=1, keepdims=True)
    for b in range(scale_half):
        part = slice(b * 128, (b + 1) * 128)
        block_ref[:, part] = (placed[:, part] * scale[:, b : b + 1] * weight).astype(jnp.bfloat16)


def fetch(sources, targets, sems, first=0):
    copies = [
        pltpu.make_async_copy(source, target, sems.at[first + i])
        for i, (source, target) in enumerate(zip(sources, targets))
    ]
    for copy in copies:
        copy.start()
    return copies


def pack_kernel(wide, most, order, *refs):
    given, refs = refs[:4], refs[4:]
    blocks, (place_ref, *held) = refs[: len(order)], refs[len(order) : -2]
    ids_ref, sems = refs[-2:]
    held = [ids_ref] + held
    copies = fetch(given, held, sems)
    copies[0].wait()
    weights_ref, scales_ref, grad_ref = held[1:]
    tokens, rows = grad_ref.shape[0], blocks[0].shape[0]
    me = lax.axis_index("ep")
    ids = ids_ref[...]
    expert = lax.broadcasted_iota(jnp.int32, (max(8, wide), tokens), 0)
    named = expert == ids
    before = lax.broadcasted_iota(jnp.int32, (tokens, tokens), 0) < lax.broadcasted_iota(
        jnp.int32, (tokens, tokens), 1
    )
    earlier = jnp.dot(
        named.astype(jnp.bfloat16), before.astype(jnp.bfloat16), preferred_element_type=jnp.float32
    )
    position = jnp.sum(jnp.where(named, earlier, 0.0), axis=0, keepdims=True).astype(jnp.int32)
    row = lax.broadcasted_iota(jnp.int32, (rows, tokens), 0)
    found = []
    for k in range(wide):
        local = jnp.where(ids == (me ^ k), position, -2 * rows)
        found.append((row == local, row - most == local))
        place_ref[0, k] = found[k][0].astype(jnp.bfloat16)
        place_ref[1, k] = found[k][1].astype(jnp.bfloat16)
    for copy in copies[1:]:
        copy.wait()
    for block_ref, k in zip(blocks, order):
        fill(block_ref, most, *found[k], weights_ref, scales_ref, grad_ref)


def pack_more_kernel(most, order, place_ref, weights_ref, scales_ref, grad_ref, partial_ref, *refs):
    taken = (len(refs) - 3 - len(order)) // 2
    given, blocks, (share_ref, *held) = refs[:taken], refs[taken : -taken - 3], refs[-taken - 3 : -2]
    sems, share_sems = refs[-2:]
    lane, count = lax.axis_index("tp"), partial_ref.shape[0]
    copies = fetch(
        [partial_ref.at[lane ^ j] for j in range(count)],
        [share_ref.at[j] for j in range(count)],
        share_sems,
    )
    copies += fetch(given, held, sems)
    for block_ref, k in zip(blocks, order):
        low, high = place_ref[0, k] != 0, place_ref[1, k] != 0
        fill(block_ref, most, low, high, weights_ref, scales_ref, grad_ref)
    for copy in copies:
        copy.wait()


def hidden_kernel(most, extra, *refs):
    blocks, (down_ref, sum_ref, sent_ref) = refs[:-3], refs[-3:]
    half = down_ref.shape[1] // 2
    count = sum_ref.shape[0]
    if extra:
        blocks, row_sums = blocks[:-1], blocks[-1][...]
        high = row_sums.astype(jnp.bfloat16).astype(jnp.float32)
        spare = jnp.zeros((EXTRA - 4, row_sums.shape[1]), jnp.float32)
        tail = jnp.concatenate([high, row_sums - high, spare], axis=0)
        sent_ref[count:, :] = jnp.zeros((EXTRA, sent_ref.shape[1]), jnp.bfloat16)
        sent_ref[count:, : row_sums.shape[1]] = tail.astype(jnp.bfloat16)
    values = [b[...].astype(jnp.float32) for b in blocks]
    low = jnp.concatenate([v[:most] for v in values], axis=0).astype(jnp.bfloat16)
    high = jnp.concatenate([v[most : 2 * most] for v in values], axis=0).astype(jnp.bfloat16)
    total = dot(low, down_ref[:, :half], NT) + dot(high, down_ref[:, half:], NT)
    sum_ref[...] = total
    sent_ref[:count, :] = total.astype(jnp.bfloat16)


def by_xor(value, most, narrow, lane):
    step = 1
    while step < narrow:
        pieces = [value[i * most : (i + step) * most] for i in range(0, narrow, step)]
        turned = [pieces[i ^ 1] for i in range(len(pieces))]
        value = jnp.where((lane & step) != 0, jnp.concatenate(turned, axis=0), value)
        step *= 2
    return value


def back_kernel(most, narrow, group, sum_ref, other_ref, pre_ref, gate_ref, up_ref, *outs):
    half = gate_ref.shape[0] // 2
    me, lane = lax.axis_index("ep"), lax.axis_index("tp")
    hidden = sum_ref[...] + other_ref[: sum_ref.shape[0], :].astype(jnp.float32)
    gate_pre, up_pre = [
        jnp.concatenate(
            [by_xor(pre_ref[i, me ^ k].astype(jnp.float32), most, narrow, lane) for k in group],
            axis=0,
        )
        for i in range(2)
    ]
    sig = 1.0 / (1.0 + jnp.exp(-gate_pre))
    up_grad = (hidden * gate_pre * sig).astype(jnp.bfloat16)
    gate_grad = (hidden * up_pre * sig * (1.0 + gate_pre * (1.0 - sig))).astype(jnp.bfloat16)
    low = dot(gate_grad, gate_ref[:half], NT) + dot(up_grad, up_ref[:half], NT)
    high = dot(gate_grad, gate_ref[half:], NT) + dot(up_grad, up_ref[half:], NT)
    for i, out in enumerate(outs):
        part = slice(i * most, (i + 1) * most)
        pieces = [low[part], high[part]]
        spare = out.shape[0] - 2 * most
        if spare:
            pieces.append(jnp.zeros((spare, half), jnp.float32))
        out[...] = jnp.concatenate(pieces, axis=0).astype(jnp.bfloat16)


def unpack_kernel(wide, place_ref, *refs):
    blocks, out_ref = refs[:-1], refs[-1]
    half = out_ref.shape[1] // 2
    for side in range(2):
        total = None
        for k in range(wide):
            if k == 0:
                rows = blocks[0][...].astype(jnp.float32)
                for other in blocks[wide:]:
                    rows += other[...].astype(jnp.float32)
                rows = rows.astype(jnp.bfloat16)
            else:
                rows = blocks[k][...]
            term = dot(place_ref[side, k], rows, TN)
            total = term if total is None else total + term
        out_ref[:, side * half : (side + 1) * half] = total.astype(jnp.bfloat16)


def groups_of(wide):
    left = list(range(wide - 1, -1, -1))
    if wide < 4:
        return [left]
    return [[left[0], left[-1]]] + [left[i : min(i + 2, wide - 1)] for i in range(1, wide - 1, 2)]


def local(
    grad_values,
    grad_scales,
    expert_ids,
    route_weights,
    w_gate,
    w_up,
    w_down,
    pre_acts,
    latent_partials,
    latent,
    latent_gain,
):
    wide, narrow = lax.axis_size("ep"), lax.axis_size("tp")
    tokens, width = grad_values.shape
    half = width // 2
    slots, hidden_width = pre_acts.shape[2:]
    most = slots // (wide * narrow)
    rows = -(-2 * most // 8) * 8
    f32, bf16 = jnp.float32, jnp.bfloat16
    block = pltpu.VMEM((rows, half), bf16)
    groups = groups_of(wide)
    order, more = groups[0], [k for group in groups[1:] for k in reversed(group)]
    packed = call(
        functools.partial(pack_kernel, wide, most, order),
        [block] * len(order)
        + [
            pltpu.VMEM((2, wide, rows, tokens), bf16),
            pltpu.VMEM((1, tokens), f32),
            pltpu.VMEM((grad_scales.shape[1], tokens), f32),
            pltpu.VMEM((tokens, width), bf16),
        ],
        *pinned(
            expert_ids.reshape(1, tokens),
            route_weights.reshape(1, tokens),
            grad_scales.T,
            grad_values,
        ),
        specs=[HBM] * 4,
        scratch=[pltpu.VMEM((1, tokens), jnp.int32), pltpu.SemaphoreType.DMA((4,))],
        name="pack",
    )
    place, *fillers = packed[len(order) :]
    packed = dict(zip(order, packed))
    partials = latent_partials.reshape(narrow, tokens, latent.shape[1])
    fetched = [
        w_down[0],
        pre_acts.reshape(2, wide, narrow * most, hidden_width),
        w_gate[0],
        w_up[0],
        latent,
        latent_gain.reshape(1, -1),
    ]
    blocks = call(
        functools.partial(pack_more_kernel, most, more),
        [block] * len(more) + [like(partials)] + [like(array) for array in fetched],
        place,
        *fillers,
        *pinned(partials, *fetched),
        specs=[VMEM] * 4 + [HBM] * (1 + len(fetched)),
        scratch=[
            pltpu.SemaphoreType.DMA((len(fetched),)),
            pltpu.SemaphoreType.DMA((narrow,)),
        ],
        cost=1 << 25,
        name="pack_more",
    )
    packed.update(zip(more, blocks))
    shares, down, pre, gate, up, latent, latent_gain = blocks[len(more) :]

    def across(k, rows_of_k):
        return [rows_of_k] + [swap(rows_of_k, "tp", j) for j in range(1, narrow)]

    taken = {0: across(0, packed[0])}
    first = groups[0][0]
    arrived = {}
    for k in order + more:
        if k:
            arrived[k] = swap(packed[k], "ep", k)
            if len(groups) > 1 and k == groups[1][0]:
                arrived[k] = after(arrived[k], packed[first], 1 << 25)
    latent_parts = [shares[0]] + [
        swap(after(shares[j], taken[0][-1]), "tp", j) for j in range(1, narrow)
    ]

    returned = {}
    own = []
    values = latent.astype(f32)
    received, products, moved = None, None, None
    for group in groups:
        for k in group:
            if k == 0:
                continue
            taken[k] = across(k, arrived[k])
        count = len(group) * narrow * most
        extra = group is groups[-1]
        if extra:
            if received is not None:
                latent_parts[-1] = after(latent_parts[-1], summed)
            own_grad = sum(part.astype(f32) for part in latent_parts)
            gained = own_grad * latent_gain
            row_sums = jnp.stack(
                [jnp.sum(values * values, axis=1), jnp.sum(gained * values, axis=1)]
            )
        summed, sent = call(
            functools.partial(hidden_kernel, most, extra),
            [
                pltpu.VMEM((count, hidden_width), f32),
                pltpu.VMEM((count + (EXTRA if extra else 0), hidden_width), bf16),
            ],
            *[rows_of_k for k in group for rows_of_k in taken[k]],
            *([row_sums] if extra else []),
            down,
            name="hidden",
            earlier=products[:1] if products else [arrived[g[0]] for g in groups[1:2]],
        )
        received = swap(sent, "sub", 1)
        products = call(
            functools.partial(back_kernel, most, narrow, group),
            [block] * (len(group) * narrow),
            summed,
            received,
            pre,
            gate,
            up,
            name="back",
            earlier=(moved,) if moved is not None else (),
        )
        for at, k in enumerate(group):
            mine = products[at * narrow]
            if k == 0:
                returned[0] = mine
                own = products[1 + at * narrow : (at + 1) * narrow]
            else:
                others = [swap(products[at * narrow + j], "tp", j) for j in range(1, narrow)]
                if k == group[0]:
                    others[0] = after(others[0], mine, 1 << 24)
                total = mine.astype(f32)
                for other in others:
                    total += other.astype(f32)
                moved = total.astype(bf16)
                returned[k] = swap(moved, "ep", k)
                last = moved if k == group[0] else last
    own = [swap(after(value, last), "tp", j + 1) for j, value in enumerate(own)]
    tail = received[count : count + 4, :tokens].astype(f32)
    row_sums = row_sums + tail[:2] + tail[2:]
    inverse_rms = lax.rsqrt(row_sums[0] / LAT + 1e-06)[:, None]
    d_latent = (
        inverse_rms * gained - values * inverse_rms**3 * row_sums[1][:, None] / LAT
    ).astype(bf16)
    (grad_input,) = call(
        functools.partial(unpack_kernel, wide),
        [jax.ShapeDtypeStruct((tokens, width), bf16)],
        place,
        *[returned[k] for k in range(wide)],
        *own,
        name="unpack",
    )
    return (grad_input, d_latent)


def solution(mesh):
    placed = (
        P(("rep", "ep", "tp"), "sub"),
        P(("rep", "ep", "tp"), "sub"),
        P(("rep", "ep", "tp"), None),
        P(("rep", "ep", "tp"), None),
        P("ep", "sub", "tp"),
        P("ep", "sub", "tp"),
        P("ep", "tp", "sub"),
        P(("rep", "ep"), None, None, "tp"),
        P("tp", ("rep", "ep"), "sub"),
        P(("rep", "ep", "tp"), "sub"),
        P("sub"),
    )
    return jax.shard_map(
        local,
        mesh=mesh,
        in_specs=placed,
        out_specs=(P(("rep", "ep", "tp"), "sub"), P(("rep", "ep", "tp"), "sub")),
        check_vma=False,
    )
```

```python
import functools

import jax
import jax.numpy as jnp
from jax import lax
from jax.experimental import pallas as pl
from jax.experimental.pallas import tpu as pltpu
from jax.sharding import PartitionSpec as P

LAT = 512
NT = (((1,), (1,)), ((), ()))
TN = (((0,), (0,)), ((), ()))
VMEM = pl.BlockSpec(memory_space=pltpu.VMEM)
ANY = pl.BlockSpec(memory_space=pl.ANY)
HBM = pl.BlockSpec(memory_space=pltpu.HBM)
EXTRA = 16
VMEM_LIMIT = 20 * 1024 * 1024


def dot(a, b, dims, precision=None):
    return lax.dot_general(a, b, dims, precision=precision, preferred_element_type=jnp.float32)


def swap(value, axis, step, what):
    count = lax.axis_size(axis)
    with jax.named_scope(f"{what}_{axis}"):
        return lax.ppermute(value, axis, [(i, i ^ step) for i in range(count)])


def pinned(*arrays):
    return [pltpu.with_memory_space_constraint(array, pltpu.HBM) for array in arrays]


def like(array):
    return pltpu.VMEM(array.shape, array.dtype)


def call(kernel, outs, *args, cost=0, name=None, specs=None, scratch=(), earlier=()):
    specs = (specs or [VMEM] * len(args)) + [ANY] * len(earlier)
    if earlier:
        taken, body = len(args), kernel

        def kernel(*refs):
            body(*refs[:taken], *refs[taken + len(earlier) :])

    return pl.pallas_call(
        kernel,
        out_shape=outs,
        in_specs=specs,
        out_specs=[VMEM] * len(outs),
        scratch_shapes=scratch,
        compiler_params=pltpu.CompilerParams(vmem_limit_bytes=VMEM_LIMIT),
        cost_estimate=pl.CostEstimate(flops=cost, bytes_accessed=0, transcendentals=0),
        name=name,
    )(*args, *earlier)


def after(value, earlier, cost=0):
    return pl.pallas_call(
        lambda value_ref, earlier_ref, out_ref: None,
        out_shape=jax.ShapeDtypeStruct(value.shape, value.dtype),
        in_specs=[ANY, ANY],
        out_specs=ANY,
        input_output_aliases={0: 0},
        compiler_params=pltpu.CompilerParams(vmem_limit_bytes=1 << 17),
        cost_estimate=pl.CostEstimate(flops=cost, bytes_accessed=0, transcendentals=0),
        name="after",
    )(value, earlier)


def fill(block_ref, most, low, high, weights_ref, scales_ref, grad_ref):
    half, scale_half = grad_ref.shape[1] // 2, scales_ref.shape[0] // 2
    placed = jnp.dot(
        low.astype(jnp.bfloat16), grad_ref[:, :half], preferred_element_type=jnp.float32
    )
    placed += jnp.dot(
        high.astype(jnp.bfloat16), grad_ref[:, half:], preferred_element_type=jnp.float32
    )
    scale = dot(low.astype(jnp.float32), scales_ref[:scale_half], NT, lax.Precision.HIGHEST)
    scale += dot(high.astype(jnp.float32), scales_ref[scale_half:], NT, lax.Precision.HIGHEST)
    weight = jnp.sum(jnp.where(low | high, weights_ref[...], 0.0), axis=1, keepdims=True)
    for b in range(scale_half):
        part = slice(b * 128, (b + 1) * 128)
        block_ref[:, part] = (placed[:, part] * scale[:, b : b + 1] * weight).astype(jnp.bfloat16)


def fetch(sources, targets, sems, first=0):
    copies = [
        pltpu.make_async_copy(source, target, sems.at[first + i])
        for i, (source, target) in enumerate(zip(sources, targets))
    ]
    for copy in copies:
        copy.start()
    return copies


def pack_kernel(wide, most, order, *refs):
    given, refs = refs[:4], refs[4:]
    blocks, (place_ref, *held) = refs[: len(order)], refs[len(order) : -2]
    ids_ref, sems = refs[-2:]
    held = [ids_ref] + held
    copies = fetch(given, held, sems)
    copies[0].wait()
    weights_ref, scales_ref, grad_ref = held[1:]
    tokens, rows = grad_ref.shape[0], blocks[0].shape[0]
    me = lax.axis_index("ep")
    ids = ids_ref[...]
    expert = lax.broadcasted_iota(jnp.int32, (max(8, wide), tokens), 0)
    named = expert == ids
    before = lax.broadcasted_iota(jnp.int32, (tokens, tokens), 0) < lax.broadcasted_iota(
        jnp.int32, (tokens, tokens), 1
    )
    earlier = jnp.dot(
        named.astype(jnp.bfloat16), before.astype(jnp.bfloat16), preferred_element_type=jnp.float32
    )
    position = jnp.sum(jnp.where(named, earlier, 0.0), axis=0, keepdims=True).astype(jnp.int32)
    row = lax.broadcasted_iota(jnp.int32, (rows, tokens), 0)
    found = []
    for k in range(wide):
        local = jnp.where(ids == (me ^ k), position, -2 * rows)
        found.append((row == local, row - most == local))
        place_ref[0, k] = found[k][0].astype(jnp.bfloat16)
        place_ref[1, k] = found[k][1].astype(jnp.bfloat16)
    for copy in copies[1:]:
        copy.wait()
    for block_ref, k in zip(blocks, order):
        fill(block_ref, most, *found[k], weights_ref, scales_ref, grad_ref)


def pack_more_kernel(most, order, place_ref, weights_ref, scales_ref, grad_ref, partial_ref, *refs):
    taken = (len(refs) - 3 - len(order)) // 2
    given, blocks, (share_ref, *held) = refs[:taken], refs[taken : -taken - 3], refs[-taken - 3 : -2]
    sems, share_sems = refs[-2:]
    lane, count = lax.axis_index("tp"), partial_ref.shape[0]
    copies = fetch(
        [partial_ref.at[lane ^ j] for j in range(count)],
        [share_ref.at[j] for j in range(count)],
        share_sems,
    )
    copies += fetch(given, held, sems)
    for block_ref, k in zip(blocks, order):
        low, high = place_ref[0, k] != 0, place_ref[1, k] != 0
        fill(block_ref, most, low, high, weights_ref, scales_ref, grad_ref)
    for copy in copies:
        copy.wait()


def hidden_kernel(most, extra, *refs):
    blocks, (down_ref, sum_ref, sent_ref) = refs[:-3], refs[-3:]
    half = down_ref.shape[1] // 2
    count = sum_ref.shape[0]
    if extra:
        blocks, row_sums = blocks[:-1], blocks[-1][...]
        high = row_sums.astype(jnp.bfloat16).astype(jnp.float32)
        spare = jnp.zeros((EXTRA - 4, row_sums.shape[1]), jnp.float32)
        tail = jnp.concatenate([high, row_sums - high, spare], axis=0)
        sent_ref[count:, :] = jnp.zeros((EXTRA, sent_ref.shape[1]), jnp.bfloat16)
        sent_ref[count:, : row_sums.shape[1]] = tail.astype(jnp.bfloat16)
    values = [b[...].astype(jnp.float32) for b in blocks]
    low = jnp.concatenate([v[:most] for v in values], axis=0).astype(jnp.bfloat16)
    high = jnp.concatenate([v[most : 2 * most] for v in values], axis=0).astype(jnp.bfloat16)
    total = dot(low, down_ref[:, :half], NT) + dot(high, down_ref[:, half:], NT)
    sum_ref[...] = total
    sent_ref[:count, :] = total.astype(jnp.bfloat16)


def by_xor(value, most, narrow, lane):
    step = 1
    while step < narrow:
        pieces = [value[i * most : (i + step) * most] for i in range(0, narrow, step)]
        turned = [pieces[i ^ 1] for i in range(len(pieces))]
        value = jnp.where((lane & step) != 0, jnp.concatenate(turned, axis=0), value)
        step *= 2
    return value


def back_kernel(most, narrow, group, sum_ref, other_ref, pre_ref, gate_ref, up_ref, *outs):
    half = gate_ref.shape[0] // 2
    me, lane = lax.axis_index("ep"), lax.axis_index("tp")
    hidden = sum_ref[...] + other_ref[: sum_ref.shape[0], :].astype(jnp.float32)
    gate_pre, up_pre = [
        jnp.concatenate(
            [by_xor(pre_ref[i, me ^ k].astype(jnp.float32), most, narrow, lane) for k in group],
            axis=0,
        )
        for i in range(2)
    ]
    sig = 1.0 / (1.0 + jnp.exp(-gate_pre))
    up_grad = (hidden * gate_pre * sig).astype(jnp.bfloat16)
    gate_grad = (hidden * up_pre * sig * (1.0 + gate_pre * (1.0 - sig))).astype(jnp.bfloat16)
    low = dot(gate_grad, gate_ref[:half], NT) + dot(up_grad, up_ref[:half], NT)
    high = dot(gate_grad, gate_ref[half:], NT) + dot(up_grad, up_ref[half:], NT)
    for i, out in enumerate(outs):
        part = slice(i * most, (i + 1) * most)
        pieces = [low[part], high[part]]
        spare = out.shape[0] - 2 * most
        if spare:
            pieces.append(jnp.zeros((spare, half), jnp.float32))
        out[...] = jnp.concatenate(pieces, axis=0).astype(jnp.bfloat16)


def unpack_kernel(wide, place_ref, *refs):
    blocks, out_ref = refs[:-1], refs[-1]
    half = out_ref.shape[1] // 2
    for side in range(2):
        total = None
        for k in range(wide):
            if k == 0:
                rows = blocks[0][...].astype(jnp.float32)
                for other in blocks[wide:]:
                    rows += other[...].astype(jnp.float32)
                rows = rows.astype(jnp.bfloat16)
            else:
                rows = blocks[k][...]
            term = dot(place_ref[side, k], rows, TN)
            total = term if total is None else total + term
        out_ref[:, side * half : (side + 1) * half] = total.astype(jnp.bfloat16)


def groups_of(wide):
    if wide < 4:
        return [list(range(wide - 1, -1, -1))]
    left = list(range(wide - 2, 1, -1))
    return [[wide - 1, 1, 0]] + [left[i : i + 2] for i in range(0, len(left), 2)]


def local(
    grad_values,
    grad_scales,
    expert_ids,
    route_weights,
    w_gate,
    w_up,
    w_down,
    pre_acts,
    latent_partials,
    latent,
    latent_gain,
):
    wide, narrow = lax.axis_size("ep"), lax.axis_size("tp")
    tokens, width = grad_values.shape
    half = width // 2
    slots, hidden_width = pre_acts.shape[2:]
    most = slots // (wide * narrow)
    rows = -(-2 * most // 8) * 8
    f32, bf16 = jnp.float32, jnp.bfloat16
    block = pltpu.VMEM((rows, half), bf16)
    groups = groups_of(wide)
    order, more = groups[0], [k for group in groups[1:] for k in group]
    packed = call(
        functools.partial(pack_kernel, wide, most, order),
        [block] * len(order)
        + [
            pltpu.VMEM((2, wide, rows, tokens), bf16),
            pltpu.VMEM((1, tokens), f32),
            pltpu.VMEM((grad_scales.shape[1], tokens), f32),
            pltpu.VMEM((tokens, width), bf16),
        ],
        *pinned(
            expert_ids.reshape(1, tokens),
            route_weights.reshape(1, tokens),
            grad_scales.T,
            grad_values,
        ),
        specs=[HBM] * 4,
        scratch=[pltpu.VMEM((1, tokens), jnp.int32), pltpu.SemaphoreType.DMA((4,))],
        name="pack",
    )
    place, *fillers = packed[len(order) :]
    packed = dict(zip(order, packed))
    partials = latent_partials.reshape(narrow, tokens, latent.shape[1])
    fetched = [
        w_down[0],
        pre_acts.reshape(2, wide, narrow * most, hidden_width),
        w_gate[0],
        w_up[0],
        latent,
        latent_gain.reshape(1, -1),
    ]
    blocks = call(
        functools.partial(pack_more_kernel, most, more),
        [block] * len(more) + [like(partials)] + [like(array) for array in fetched],
        place,
        *fillers,
        *pinned(partials, *fetched),
        specs=[VMEM] * 4 + [HBM] * (1 + len(fetched)),
        scratch=[
            pltpu.SemaphoreType.DMA((len(fetched),)),
            pltpu.SemaphoreType.DMA((narrow,)),
        ],
        cost=1 << 25,
        name="pack_more",
    )
    packed.update(zip(more, blocks))
    shares, down, pre, gate, up, latent, latent_gain = blocks[len(more) :]

    def across(k, rows_of_k):
        return [rows_of_k] + [swap(rows_of_k, "tp", j, f"rows{k}") for j in range(1, narrow)]

    taken = {0: across(0, packed[0])}
    first = groups[0][0]
    arrived = {}
    for k in order + more:
        if k:
            arrived[k] = swap(packed[k], "ep", k, f"rows{k}")
            if len(groups) > 1 and k == groups[1][0]:
                arrived[k] = after(arrived[k], packed[first], 1 << 31)
    latent_parts = [shares[0]] + [
        swap(shares[j], "tp", j, "latent") for j in range(1, narrow)
    ]

    returned = {}
    own = []
    values = latent.astype(f32)
    received, products, moved = None, None, None
    for group in groups:
        for k in group:
            if k == 0:
                continue
            taken[k] = across(k, arrived[k])
            if received is not None:
                taken[k][-1] = after(taken[k][-1], products[0])
            elif k != first and narrow > 1:
                taken[k][-1] = after(taken[k][-1], packed[first], 1 << 31)
        count = len(group) * narrow * most
        extra = group is groups[-1]
        if extra:
            if received is not None:
                latent_parts[-1] = after(latent_parts[-1], summed, 1 << 30)
            own_grad = sum(part.astype(f32) for part in latent_parts)
            gained = own_grad * latent_gain
            row_sums = jnp.stack(
                [jnp.sum(values * values, axis=1), jnp.sum(gained * values, axis=1)]
            )
        summed, sent = call(
            functools.partial(hidden_kernel, most, extra),
            [
                pltpu.VMEM((count, hidden_width), f32),
                pltpu.VMEM((count + (EXTRA if extra else 0), hidden_width), bf16),
            ],
            *[rows_of_k for k in group for rows_of_k in taken[k]],
            *([row_sums] if extra else []),
            down,
            name="hidden",
            earlier=products[:1] if products else (),
        )
        received = swap(sent, "sub", 1, f"hidden{group[0]}")
        if moved is not None:
            received = after(received, moved)
        products = call(
            functools.partial(back_kernel, most, narrow, group),
            [block] * (len(group) * narrow),
            summed,
            received,
            pre,
            gate,
            up,
            name="back",
        )
        for at, k in enumerate(group):
            mine = products[at * narrow]
            if k == 0:
                returned[0] = mine
                own = products[1 + at * narrow : (at + 1) * narrow]
                continue
            others = products[at * narrow + 1 : (at + 1) * narrow]
            if k != group[0]:
                others = [after(other, moved) for other in others]
            others = [swap(other, "tp", j + 1, f"back{k}") for j, other in enumerate(others)]
            total = mine.astype(f32)
            for other in others:
                total += other.astype(f32)
            total = total.astype(bf16)
            returned[k] = swap(total, "ep", k, f"back{k}")
            if k == group[0]:
                moved = total
    own = [swap(after(value, moved), "tp", j + 1, "back0") for j, value in enumerate(own)]
    tail = received[count : count + 4, :tokens].astype(f32)
    row_sums = row_sums + tail[:2] + tail[2:]
    inverse_rms = lax.rsqrt(row_sums[0] / LAT + 1e-06)[:, None]
    d_latent = (
        inverse_rms * gained - values * inverse_rms**3 * row_sums[1][:, None] / LAT
    ).astype(bf16)
    (grad_input,) = call(
        functools.partial(unpack_kernel, wide),
        [jax.ShapeDtypeStruct((tokens, width), bf16)],
        place,
        *[returned[k] for k in range(wide)],
        *own,
        name="unpack",
    )
    return (grad_input, d_latent)


def solution(mesh):
    placed = (
        P(("rep", "ep", "tp"), "sub"),
        P(("rep", "ep", "tp"), "sub"),
        P(("rep", "ep", "tp"), None),
        P(("rep", "ep", "tp"), None),
        P("ep", "sub", "tp"),
        P("ep", "sub", "tp"),
        P("ep", "tp", "sub"),
        P(("rep", "ep"), None, None, "tp"),
        P("tp", ("rep", "ep"), "sub"),
        P(("rep", "ep", "tp"), "sub"),
        P("sub"),
    )
    return jax.shard_map(
        local,
        mesh=mesh,
        in_specs=placed,
        out_specs=(P(("rep", "ep", "tp"), "sub"), P(("rep", "ep", "tp"), "sub")),
        check_vma=False,
    )
```

```python
import functools

import jax
import jax.numpy as jnp
from jax import lax
from jax.experimental import pallas as pl
from jax.experimental.pallas import tpu as pltpu
from jax.sharding import PartitionSpec as P

LAT = 512
NT = (((1,), (1,)), ((), ()))
TN = (((0,), (0,)), ((), ()))
VMEM = pl.BlockSpec(memory_space=pltpu.VMEM)
ANY = pl.BlockSpec(memory_space=pl.ANY)
HBM = pl.BlockSpec(memory_space=pltpu.HBM)
EXTRA = 16
VMEM_LIMIT = 20 * 1024 * 1024


def dot(a, b, dims, precision=None):
    return lax.dot_general(a, b, dims, precision=precision, preferred_element_type=jnp.float32)


def swap(value, axis, step, what):
    count = lax.axis_size(axis)
    with jax.named_scope(f"{what}_{axis}"):
        return lax.ppermute(value, axis, [(i, i ^ step) for i in range(count)])


def pinned(*arrays):
    return [pltpu.with_memory_space_constraint(array, pltpu.HBM) for array in arrays]


def like(array):
    return pltpu.VMEM(array.shape, array.dtype)


def call(kernel, outs, *args, cost=0, name=None, specs=None, scratch=(), earlier=()):
    specs = (specs or [VMEM] * len(args)) + [ANY] * len(earlier)
    if earlier:
        taken, body = len(args), kernel

        def kernel(*refs):
            body(*refs[:taken], *refs[taken + len(earlier) :])

    return pl.pallas_call(
        kernel,
        out_shape=outs,
        in_specs=specs,
        out_specs=[VMEM] * len(outs),
        scratch_shapes=scratch,
        compiler_params=pltpu.CompilerParams(vmem_limit_bytes=VMEM_LIMIT),
        cost_estimate=pl.CostEstimate(flops=cost, bytes_accessed=0, transcendentals=0),
        name=name,
    )(*args, *earlier)


def after(value, earlier, cost=0):
    return pl.pallas_call(
        lambda value_ref, earlier_ref, out_ref: None,
        out_shape=jax.ShapeDtypeStruct(value.shape, value.dtype),
        in_specs=[ANY, ANY],
        out_specs=ANY,
        input_output_aliases={0: 0},
        compiler_params=pltpu.CompilerParams(vmem_limit_bytes=1 << 17),
        cost_estimate=pl.CostEstimate(flops=cost, bytes_accessed=0, transcendentals=0),
        name="after",
    )(value, earlier)


def fill(block_ref, most, low, high, weights_ref, scales_ref, grad_ref):
    half, scale_half = grad_ref.shape[1] // 2, scales_ref.shape[0] // 2
    placed = jnp.dot(
        low.astype(jnp.bfloat16), grad_ref[:, :half], preferred_element_type=jnp.float32
    )
    placed += jnp.dot(
        high.astype(jnp.bfloat16), grad_ref[:, half:], preferred_element_type=jnp.float32
    )
    scale = dot(low.astype(jnp.float32), scales_ref[:scale_half], NT, lax.Precision.HIGHEST)
    scale += dot(high.astype(jnp.float32), scales_ref[scale_half:], NT, lax.Precision.HIGHEST)
    weight = jnp.sum(jnp.where(low | high, weights_ref[...], 0.0), axis=1, keepdims=True)
    for b in range(scale_half):
        part = slice(b * 128, (b + 1) * 128)
        block_ref[:, part] = (placed[:, part] * scale[:, b : b + 1] * weight).astype(jnp.bfloat16)


def fetch(sources, targets, sems, first=0):
    copies = [
        pltpu.make_async_copy(source, target, sems.at[first + i])
        for i, (source, target) in enumerate(zip(sources, targets))
    ]
    for copy in copies:
        copy.start()
    return copies


def pack_kernel(wide, most, order, *refs):
    given, refs = refs[:4], refs[4:]
    blocks, (place_ref, *held) = refs[: len(order)], refs[len(order) : -2]
    ids_ref, sems = refs[-2:]
    held = [ids_ref] + held
    copies = fetch(given, held, sems)
    copies[0].wait()
    weights_ref, scales_ref, grad_ref = held[1:]
    tokens, rows = grad_ref.shape[0], blocks[0].shape[0]
    me = lax.axis_index("ep")
    ids = ids_ref[...]
    expert = lax.broadcasted_iota(jnp.int32, (max(8, wide), tokens), 0)
    named = expert == ids
    before = lax.broadcasted_iota(jnp.int32, (tokens, tokens), 0) < lax.broadcasted_iota(
        jnp.int32, (tokens, tokens), 1
    )
    earlier = jnp.dot(
        named.astype(jnp.bfloat16), before.astype(jnp.bfloat16), preferred_element_type=jnp.float32
    )
    position = jnp.sum(jnp.where(named, earlier, 0.0), axis=0, keepdims=True).astype(jnp.int32)
    row = lax.broadcasted_iota(jnp.int32, (rows, tokens), 0)
    found = []
    for k in range(wide):
        local = jnp.where(ids == (me ^ k), position, -2 * rows)
        found.append((row == local, row - most == local))
        place_ref[0, k] = found[k][0].astype(jnp.bfloat16)
        place_ref[1, k] = found[k][1].astype(jnp.bfloat16)
    for copy in copies[1:]:
        copy.wait()
    for block_ref, k in zip(blocks, order):
        fill(block_ref, most, *found[k], weights_ref, scales_ref, grad_ref)


def pack_more_kernel(most, order, place_ref, weights_ref, scales_ref, grad_ref, partial_ref, *refs):
    taken = (len(refs) - 3 - len(order)) // 2
    given, blocks, (share_ref, *held) = refs[:taken], refs[taken : -taken - 3], refs[-taken - 3 : -2]
    sems, share_sems = refs[-2:]
    lane, count = lax.axis_index("tp"), partial_ref.shape[0]
    copies = fetch(
        [partial_ref.at[lane ^ j] for j in range(count)],
        [share_ref.at[j] for j in range(count)],
        share_sems,
    )
    copies += fetch(given, held, sems)
    for block_ref, k in zip(blocks, order):
        low, high = place_ref[0, k] != 0, place_ref[1, k] != 0
        fill(block_ref, most, low, high, weights_ref, scales_ref, grad_ref)
    for copy in copies:
        copy.wait()


def hidden_kernel(most, extra, *refs):
    blocks, (down_ref, sum_ref, sent_ref) = refs[:-3], refs[-3:]
    half = down_ref.shape[1] // 2
    count = sum_ref.shape[0]
    if extra:
        blocks, row_sums = blocks[:-1], blocks[-1][...]
        high = row_sums.astype(jnp.bfloat16).astype(jnp.float32)
        spare = jnp.zeros((EXTRA - 4, row_sums.shape[1]), jnp.float32)
        tail = jnp.concatenate([high, row_sums - high, spare], axis=0)
        sent_ref[count:, :] = jnp.zeros((EXTRA, sent_ref.shape[1]), jnp.bfloat16)
        sent_ref[count:, : row_sums.shape[1]] = tail.astype(jnp.bfloat16)
    values = [b[...].astype(jnp.float32) for b in blocks]
    low = jnp.concatenate([v[:most] for v in values], axis=0).astype(jnp.bfloat16)
    high = jnp.concatenate([v[most : 2 * most] for v in values], axis=0).astype(jnp.bfloat16)
    total = dot(low, down_ref[:, :half], NT) + dot(high, down_ref[:, half:], NT)
    sum_ref[...] = total
    sent_ref[:count, :] = total.astype(jnp.bfloat16)


def by_xor(value, most, narrow, lane):
    step = 1
    while step < narrow:
        pieces = [value[i * most : (i + step) * most] for i in range(0, narrow, step)]
        turned = [pieces[i ^ 1] for i in range(len(pieces))]
        value = jnp.where((lane & step) != 0, jnp.concatenate(turned, axis=0), value)
        step *= 2
    return value


def back_kernel(most, narrow, group, sum_ref, other_ref, pre_ref, gate_ref, up_ref, *outs):
    half = gate_ref.shape[0] // 2
    me, lane = lax.axis_index("ep"), lax.axis_index("tp")
    hidden = sum_ref[...] + other_ref[: sum_ref.shape[0], :].astype(jnp.float32)
    gate_pre, up_pre = [
        jnp.concatenate(
            [by_xor(pre_ref[i, me ^ k].astype(jnp.float32), most, narrow, lane) for k in group],
            axis=0,
        )
        for i in range(2)
    ]
    sig = 1.0 / (1.0 + jnp.exp(-gate_pre))
    up_grad = (hidden * gate_pre * sig).astype(jnp.bfloat16)
    gate_grad = (hidden * up_pre * sig * (1.0 + gate_pre * (1.0 - sig))).astype(jnp.bfloat16)
    low = dot(gate_grad, gate_ref[:half], NT) + dot(up_grad, up_ref[:half], NT)
    high = dot(gate_grad, gate_ref[half:], NT) + dot(up_grad, up_ref[half:], NT)
    for i, out in enumerate(outs):
        part = slice(i * most, (i + 1) * most)
        pieces = [low[part], high[part]]
        spare = out.shape[0] - 2 * most
        if spare:
            pieces.append(jnp.zeros((spare, half), jnp.float32))
        out[...] = jnp.concatenate(pieces, axis=0).astype(jnp.bfloat16)


def unpack_kernel(distances, started, place_ref, *refs):
    blocks, others, out_ref = refs[: len(distances)], refs[len(distances) : -1], refs[-1]
    if started:
        others, so_far_ref = others[:-1], others[-1]
    half = out_ref.shape[1] // 2
    for side in range(2):
        columns = slice(side * half, (side + 1) * half)
        total = so_far_ref[:, columns].astype(jnp.float32) if started else 0.0
        for k, block_ref in zip(distances, blocks):
            rows = block_ref[...]
            if k == 0:
                rows = rows.astype(jnp.float32)
                for other_ref in others:
                    rows += other_ref[...].astype(jnp.float32)
                rows = rows.astype(jnp.bfloat16)
            total = total + dot(place_ref[side, k], rows, TN)
        out_ref[:, columns] = total.astype(jnp.bfloat16)


def groups_of(wide):
    if wide < 4:
        return [list(range(wide - 1, -1, -1))]
    left = list(range(wide - 2, 1, -1))
    return [[wide - 1, 1, 0]] + [left[i : i + 2] for i in range(0, len(left), 2)]


def local(
    grad_values,
    grad_scales,
    expert_ids,
    route_weights,
    w_gate,
    w_up,
    w_down,
    pre_acts,
    latent_partials,
    latent,
    latent_gain,
):
    wide, narrow = lax.axis_size("ep"), lax.axis_size("tp")
    tokens, width = grad_values.shape
    half = width // 2
    slots, hidden_width = pre_acts.shape[2:]
    most = slots // (wide * narrow)
    rows = -(-2 * most // 8) * 8
    f32, bf16 = jnp.float32, jnp.bfloat16
    block = pltpu.VMEM((rows, half), bf16)
    groups = groups_of(wide)
    order, more = groups[0], [k for group in groups[1:] for k in group]
    packed = call(
        functools.partial(pack_kernel, wide, most, order),
        [block] * len(order)
        + [
            pltpu.VMEM((2, wide, rows, tokens), bf16),
            pltpu.VMEM((1, tokens), f32),
            pltpu.VMEM((grad_scales.shape[1], tokens), f32),
            pltpu.VMEM((tokens, width), bf16),
        ],
        *pinned(
            expert_ids.reshape(1, tokens),
            route_weights.reshape(1, tokens),
            grad_scales.T,
            grad_values,
        ),
        specs=[HBM] * 4,
        scratch=[pltpu.VMEM((1, tokens), jnp.int32), pltpu.SemaphoreType.DMA((4,))],
        name="pack",
    )
    place, *fillers = packed[len(order) :]
    packed = dict(zip(order, packed))
    partials = latent_partials.reshape(narrow, tokens, latent.shape[1])
    fetched = [
        w_down[0],
        pre_acts.reshape(2, wide, narrow * most, hidden_width),
        w_gate[0],
        w_up[0],
        latent,
        latent_gain.reshape(1, -1),
    ]
    blocks = call(
        functools.partial(pack_more_kernel, most, more),
        [block] * len(more) + [like(partials)] + [like(array) for array in fetched],
        place,
        *fillers,
        *pinned(partials, *fetched),
        specs=[VMEM] * 4 + [HBM] * (1 + len(fetched)),
        scratch=[
            pltpu.SemaphoreType.DMA((len(fetched),)),
            pltpu.SemaphoreType.DMA((narrow,)),
        ],
        cost=1 << 25,
        name="pack_more",
    )
    packed.update(zip(more, blocks))
    shares, down, pre, gate, up, latent, latent_gain = blocks[len(more) :]

    def across(k, rows_of_k):
        return [rows_of_k] + [swap(rows_of_k, "tp", j, f"rows{k}") for j in range(1, narrow)]

    taken = {0: across(0, packed[0])}
    first = groups[0][0]
    arrived = {}
    for k in order + more:
        if k:
            arrived[k] = swap(packed[k], "ep", k, f"rows{k}")
            if len(groups) > 1 and k == groups[1][0]:
                arrived[k] = after(arrived[k], packed[first], 1 << 31)
    latent_parts = [shares[0]] + [
        swap(shares[j], "tp", j, "latent") for j in range(1, narrow)
    ]

    def give_back(k, mine, others):
        others = [swap(other, "tp", j + 1, f"back{k}") for j, other in enumerate(others)]
        total = mine.astype(f32)
        for other in others:
            total += other.astype(f32)
        total = total.astype(bf16)
        return total, swap(total, "ep", k, f"back{k}")

    returned = {}
    own, waiting = [], []
    values = latent.astype(f32)
    received, products, moved = None, None, None
    for group in groups:
        for k in group:
            if k == 0:
                continue
            taken[k] = across(k, arrived[k])
            if received is not None:
                taken[k][-1] = after(taken[k][-1], products[0])
            elif k != first and narrow > 1:
                taken[k][-1] = after(taken[k][-1], packed[first], 1 << 31)
        count = len(group) * narrow * most
        extra = group is groups[-1]
        if extra:
            if received is not None:
                latent_parts[-1] = after(latent_parts[-1], summed, 1 << 30)
            own_grad = sum(part.astype(f32) for part in latent_parts)
            gained = own_grad * latent_gain
            row_sums = jnp.stack(
                [jnp.sum(values * values, axis=1), jnp.sum(gained * values, axis=1)]
            )
        summed, sent = call(
            functools.partial(hidden_kernel, most, extra),
            [
                pltpu.VMEM((count, hidden_width), f32),
                pltpu.VMEM((count + (EXTRA if extra else 0), hidden_width), bf16),
            ],
            *[rows_of_k for k in group for rows_of_k in taken[k]],
            *([row_sums] if extra else []),
            down,
            name="hidden",
            earlier=products[:1] if products else (),
        )
        for k, mine, others in waiting:
            others = [after(other, summed) for other in others]
            returned[k] = give_back(k, mine, others)[1]
        waiting = []
        received = swap(sent, "sub", 1, f"hidden{group[0]}")
        if moved is not None:
            received = after(received, moved)
        products = call(
            functools.partial(back_kernel, most, narrow, group),
            [block] * (len(group) * narrow),
            summed,
            received,
            pre,
            gate,
            up,
            name="back",
        )
        for at, k in enumerate(group):
            mine, others = products[at * narrow], products[at * narrow + 1 : (at + 1) * narrow]
            if k == 0:
                returned[0], own = mine, others
            elif k != group[0] and not extra:
                waiting.append((k, mine, others))
            else:
                total, returned[k] = give_back(k, mine, others)
                if k == group[0]:
                    moved = total
    own = [swap(after(value, moved), "tp", j + 1, "back0") for j, value in enumerate(own)]
    tail = received[count : count + 4, :tokens].astype(f32)
    row_sums = row_sums + tail[:2] + tail[2:]
    inverse_rms = lax.rsqrt(row_sums[0] / LAT + 1e-06)[:, None]
    d_latent = (
        inverse_rms * gained - values * inverse_rms**3 * row_sums[1][:, None] / LAT
    ).astype(bf16)
    latest = groups[-1][:1] if len(groups) > 1 else []
    distances = [k for k in sorted(returned, reverse=True) if k not in latest]
    (grad_input,) = call(
        functools.partial(unpack_kernel, distances, False),
        [pltpu.VMEM((tokens, width), bf16) if latest else jax.ShapeDtypeStruct((tokens, width), bf16)],
        place,
        *[returned[k] for k in distances],
        *own,
        name="unpack",
    )
    if latest:
        (grad_input,) = call(
            functools.partial(unpack_kernel, latest, True),
            [jax.ShapeDtypeStruct((tokens, width), bf16)],
            place,
            *[returned[k] for k in latest],
            grad_input,
            name="unpack_latest",
        )
    return (grad_input, d_latent)


def solution(mesh):
    placed = (
        P(("rep", "ep", "tp"), "sub"),
        P(("rep", "ep", "tp"), "sub"),
        P(("rep", "ep", "tp"), None),
        P(("rep", "ep", "tp"), None),
        P("ep", "sub", "tp"),
        P("ep", "sub", "tp"),
        P("ep", "tp", "sub"),
        P(("rep", "ep"), None, None, "tp"),
        P("tp", ("rep", "ep"), "sub"),
        P(("rep", "ep", "tp"), "sub"),
        P("sub"),
    )
    return jax.shard_map(
        local,
        mesh=mesh,
        in_specs=placed,
        out_specs=(P(("rep", "ep", "tp"), "sub"), P(("rep", "ep", "tp"), "sub")),
        check_vma=False,
    )
```

```python
import functools

import jax
import jax.numpy as jnp
from jax import lax
from jax.experimental import pallas as pl
from jax.experimental.pallas import tpu as pltpu
from jax.sharding import PartitionSpec as P

LAT = 512
NT = (((1,), (1,)), ((), ()))
TN = (((0,), (0,)), ((), ()))
VMEM = pl.BlockSpec(memory_space=pltpu.VMEM)
ANY = pl.BlockSpec(memory_space=pl.ANY)
HBM = pl.BlockSpec(memory_space=pltpu.HBM)
EXTRA = 16
VMEM_LIMIT = 20 * 1024 * 1024


def dot(a, b, dims, precision=None):
    return lax.dot_general(a, b, dims, precision=precision, preferred_element_type=jnp.float32)


def swap(value, axis, step, what):
    count = lax.axis_size(axis)
    with jax.named_scope(f"{what}_{axis}"):
        return lax.ppermute(value, axis, [(i, i ^ step) for i in range(count)])


def pinned(*arrays):
    return [pltpu.with_memory_space_constraint(array, pltpu.HBM) for array in arrays]


def like(array):
    return pltpu.VMEM(array.shape, array.dtype)


def call(kernel, outs, *args, cost=0, name=None, specs=None, scratch=(), earlier=()):
    specs = (specs or [VMEM] * len(args)) + [ANY] * len(earlier)
    if earlier:
        taken, body = len(args), kernel

        def kernel(*refs):
            body(*refs[:taken], *refs[taken + len(earlier) :])

    return pl.pallas_call(
        kernel,
        out_shape=outs,
        in_specs=specs,
        out_specs=[VMEM] * len(outs),
        scratch_shapes=scratch,
        compiler_params=pltpu.CompilerParams(vmem_limit_bytes=VMEM_LIMIT),
        cost_estimate=pl.CostEstimate(flops=cost, bytes_accessed=0, transcendentals=0),
        name=name,
    )(*args, *earlier)


def after(value, earlier, cost=0):
    return pl.pallas_call(
        lambda value_ref, earlier_ref, out_ref: None,
        out_shape=jax.ShapeDtypeStruct(value.shape, value.dtype),
        in_specs=[ANY, ANY],
        out_specs=ANY,
        input_output_aliases={0: 0},
        compiler_params=pltpu.CompilerParams(vmem_limit_bytes=1 << 17),
        cost_estimate=pl.CostEstimate(flops=cost, bytes_accessed=0, transcendentals=0),
        name="after",
    )(value, earlier)


def fill(block_ref, most, low, high, weights_ref, scales_ref, grad_ref):
    half, scale_half = grad_ref.shape[1] // 2, scales_ref.shape[0] // 2
    placed = jnp.dot(
        low.astype(jnp.bfloat16), grad_ref[:, :half], preferred_element_type=jnp.float32
    )
    placed += jnp.dot(
        high.astype(jnp.bfloat16), grad_ref[:, half:], preferred_element_type=jnp.float32
    )
    scale = dot(low.astype(jnp.float32), scales_ref[:scale_half], NT, lax.Precision.HIGHEST)
    scale += dot(high.astype(jnp.float32), scales_ref[scale_half:], NT, lax.Precision.HIGHEST)
    weight = jnp.sum(jnp.where(low | high, weights_ref[...], 0.0), axis=1, keepdims=True)
    for b in range(scale_half):
        part = slice(b * 128, (b + 1) * 128)
        block_ref[:, part] = (placed[:, part] * scale[:, b : b + 1] * weight).astype(jnp.bfloat16)


def fetch(sources, targets, sems, first=0):
    copies = [
        pltpu.make_async_copy(source, target, sems.at[first + i])
        for i, (source, target) in enumerate(zip(sources, targets))
    ]
    for copy in copies:
        copy.start()
    return copies


def pack_kernel(most, order, *refs):
    given, partial_ref, refs = refs[:4], refs[4], refs[5:]
    blocks, (place_ref, share_ref), refs = refs[: len(order)], refs[len(order) :][:2], refs[-6:]
    held, sems, share_sems = refs[:4], refs[4], refs[5]
    lane, count = lax.axis_index("tp"), partial_ref.shape[0]
    copies = fetch(given, held, sems)
    shares = fetch(
        [partial_ref.at[lane ^ j] for j in range(count)],
        [share_ref.at[j] for j in range(count)],
        share_sems,
    )
    copies[0].wait()
    ids_ref, weights_ref, scales_ref, grad_ref = held
    tokens, rows = grad_ref.shape[0], blocks[0].shape[0]
    me = lax.axis_index("ep")
    ids = ids_ref[...]
    expert = lax.broadcasted_iota(jnp.int32, (max(8, len(order)), tokens), 0)
    named = expert == ids
    before = lax.broadcasted_iota(jnp.int32, (tokens, tokens), 0) < lax.broadcasted_iota(
        jnp.int32, (tokens, tokens), 1
    )
    earlier = jnp.dot(
        named.astype(jnp.bfloat16), before.astype(jnp.bfloat16), preferred_element_type=jnp.float32
    )
    position = jnp.sum(jnp.where(named, earlier, 0.0), axis=0, keepdims=True).astype(jnp.int32)
    row = lax.broadcasted_iota(jnp.int32, (rows, tokens), 0)
    found = []
    for k in order:
        local = jnp.where(ids == (me ^ k), position, -2 * rows)
        low, high = row == local, row - most == local
        found.append((low, high))
        place_ref[0, k] = low.astype(jnp.bfloat16)
        place_ref[1, k] = high.astype(jnp.bfloat16)
    for copy in copies[1:]:
        copy.wait()
    for block_ref, (low, high) in zip(blocks, found):
        fill(block_ref, most, low, high, weights_ref, scales_ref, grad_ref)
    for copy in shares:
        copy.wait()


def fetch_kernel(*refs):
    count = len(refs) // 2
    for copy in fetch(refs[:count], refs[count : 2 * count], refs[-1]):
        copy.wait()


def hidden_kernel(most, extra, *refs):
    blocks, (down_ref, sum_ref, sent_ref) = refs[:-3], refs[-3:]
    half = down_ref.shape[1] // 2
    count = sum_ref.shape[0]
    if extra:
        blocks, row_sums = blocks[:-1], blocks[-1][...]
        high = row_sums.astype(jnp.bfloat16).astype(jnp.float32)
        spare = jnp.zeros((EXTRA - 4, row_sums.shape[1]), jnp.float32)
        tail = jnp.concatenate([high, row_sums - high, spare], axis=0)
        sent_ref[count:, :] = jnp.zeros((EXTRA, sent_ref.shape[1]), jnp.bfloat16)
        sent_ref[count:, : row_sums.shape[1]] = tail.astype(jnp.bfloat16)
    values = [b[...].astype(jnp.float32) for b in blocks]
    low = jnp.concatenate([v[:most] for v in values], axis=0).astype(jnp.bfloat16)
    high = jnp.concatenate([v[most : 2 * most] for v in values], axis=0).astype(jnp.bfloat16)
    total = dot(low, down_ref[:, :half], NT) + dot(high, down_ref[:, half:], NT)
    sum_ref[...] = total
    sent_ref[:count, :] = total.astype(jnp.bfloat16)


def by_xor(value, most, narrow, lane):
    step = 1
    while step < narrow:
        pieces = [value[i * most : (i + step) * most] for i in range(0, narrow, step)]
        turned = [pieces[i ^ 1] for i in range(len(pieces))]
        value = jnp.where((lane & step) != 0, jnp.concatenate(turned, axis=0), value)
        step *= 2
    return value


def back_kernel(most, narrow, group, sum_ref, other_ref, pre_ref, gate_ref, up_ref, *outs):
    half = gate_ref.shape[0] // 2
    me, lane = lax.axis_index("ep"), lax.axis_index("tp")
    hidden = sum_ref[...] + other_ref[: sum_ref.shape[0], :].astype(jnp.float32)
    gate_pre, up_pre = [
        jnp.concatenate(
            [by_xor(pre_ref[i, me ^ k].astype(jnp.float32), most, narrow, lane) for k in group],
            axis=0,
        )
        for i in range(2)
    ]
    sig = 1.0 / (1.0 + jnp.exp(-gate_pre))
    up_grad = (hidden * gate_pre * sig).astype(jnp.bfloat16)
    gate_grad = (hidden * up_pre * sig * (1.0 + gate_pre * (1.0 - sig))).astype(jnp.bfloat16)
    low = dot(gate_grad, gate_ref[:half], NT) + dot(up_grad, up_ref[:half], NT)
    high = dot(gate_grad, gate_ref[half:], NT) + dot(up_grad, up_ref[half:], NT)
    for i, out in enumerate(outs):
        part = slice(i * most, (i + 1) * most)
        pieces = [low[part], high[part]]
        spare = out.shape[0] - 2 * most
        if spare:
            pieces.append(jnp.zeros((spare, half), jnp.float32))
        out[...] = jnp.concatenate(pieces, axis=0).astype(jnp.bfloat16)


def unpack_kernel(distances, started, place_ref, *refs):
    blocks, others, out_ref = refs[: len(distances)], refs[len(distances) : -1], refs[-1]
    if started:
        others, so_far_ref = others[:-1], others[-1]
    half = out_ref.shape[1] // 2
    for side in range(2):
        columns = slice(side * half, (side + 1) * half)
        total = so_far_ref[:, columns].astype(jnp.float32) if started else 0.0
        for k, block_ref in zip(distances, blocks):
            rows = block_ref[...]
            if k == 0:
                rows = rows.astype(jnp.float32)
                for other_ref in others:
                    rows += other_ref[...].astype(jnp.float32)
                rows = rows.astype(jnp.bfloat16)
            total = total + dot(place_ref[side, k], rows, TN)
        out_ref[:, columns] = total.astype(jnp.bfloat16)


def groups_of(wide):
    if wide < 4:
        return [list(range(wide - 1, -1, -1))]
    left = list(range(wide - 2, 1, -1))
    return [[wide - 1, 1, 0]] + [left[i : i + 2] for i in range(0, len(left), 2)]


def local(
    grad_values,
    grad_scales,
    expert_ids,
    route_weights,
    w_gate,
    w_up,
    w_down,
    pre_acts,
    latent_partials,
    latent,
    latent_gain,
):
    wide, narrow = lax.axis_size("ep"), lax.axis_size("tp")
    tokens, width = grad_values.shape
    half = width // 2
    slots, hidden_width = pre_acts.shape[2:]
    most = slots // (wide * narrow)
    rows = -(-2 * most // 8) * 8
    f32, bf16 = jnp.float32, jnp.bfloat16
    block = pltpu.VMEM((rows, half), bf16)
    groups = groups_of(wide)
    order = [k for group in groups for k in group]
    partials = latent_partials.reshape(narrow, tokens, latent.shape[1])
    packed = call(
        functools.partial(pack_kernel, most, order),
        [block] * wide + [pltpu.VMEM((2, wide, rows, tokens), bf16), like(partials)],
        *pinned(
            expert_ids.reshape(1, tokens),
            route_weights.reshape(1, tokens),
            grad_scales.T,
            grad_values,
            partials,
        ),
        specs=[HBM] * 5,
        scratch=[
            pltpu.VMEM((1, tokens), jnp.int32),
            pltpu.VMEM((1, tokens), f32),
            pltpu.VMEM((grad_scales.shape[1], tokens), f32),
            pltpu.VMEM((tokens, width), bf16),
            pltpu.SemaphoreType.DMA((4,)),
            pltpu.SemaphoreType.DMA((narrow,)),
        ],
        name="pack",
    )
    place, shares = packed[wide:]
    packed = dict(zip(order, packed))

    def across(k, rows_of_k):
        return [rows_of_k] + [swap(rows_of_k, "tp", j, f"rows{k}") for j in range(1, narrow)]

    taken = {0: across(0, packed[0])}
    first = groups[0][0]
    arrived = {}
    for k in order:
        if k:
            arrived[k] = swap(packed[k], "ep", k, f"rows{k}")
            if len(groups) > 1 and k == groups[1][0]:
                arrived[k] = after(arrived[k], packed[first], 1 << 31)
    fetched = [
        w_down[0],
        pre_acts.reshape(2, wide, narrow * most, hidden_width),
        w_gate[0],
        w_up[0],
        latent,
        latent_gain.reshape(1, -1),
    ]
    down, pre, gate, up, latent, latent_gain = call(
        fetch_kernel,
        [like(array) for array in fetched],
        *pinned(*fetched),
        specs=[HBM] * len(fetched),
        scratch=[pltpu.SemaphoreType.DMA((len(fetched),))],
        cost=1 << 31,
        earlier=[arrived[first]],
        name="fetch",
    )
    latent_parts = [shares[0]] + [
        swap(shares[j], "tp", j, "latent") for j in range(1, narrow)
    ]

    def give_back(k, mine, others):
        others = [swap(other, "tp", j + 1, f"back{k}") for j, other in enumerate(others)]
        total = mine.astype(f32)
        for other in others:
            total += other.astype(f32)
        total = total.astype(bf16)
        return total, swap(total, "ep", k, f"back{k}")

    returned = {}
    own, waiting = [], []
    values = latent.astype(f32)
    received, products, moved = None, None, None
    for group in groups:
        for k in group:
            if k == 0:
                continue
            taken[k] = across(k, arrived[k])
            if received is not None:
                taken[k][-1] = after(taken[k][-1], products[0])
            elif k != first and narrow > 1:
                taken[k][-1] = after(taken[k][-1], packed[first], 1 << 31)
        count = len(group) * narrow * most
        extra = group is groups[-1]
        if extra:
            if received is not None:
                latent_parts[-1] = after(latent_parts[-1], summed, 1 << 30)
            own_grad = sum(part.astype(f32) for part in latent_parts)
            gained = own_grad * latent_gain
            row_sums = jnp.stack(
                [jnp.sum(values * values, axis=1), jnp.sum(gained * values, axis=1)]
            )
        summed, sent = call(
            functools.partial(hidden_kernel, most, extra),
            [
                pltpu.VMEM((count, hidden_width), f32),
                pltpu.VMEM((count + (EXTRA if extra else 0), hidden_width), bf16),
            ],
            *[rows_of_k for k in group for rows_of_k in taken[k]],
            *([row_sums] if extra else []),
            down,
            name="hidden",
            earlier=products[:1] if products else (),
        )
        for k, mine, others in waiting:
            others = [after(other, summed) for other in others]
            returned[k] = give_back(k, mine, others)[1]
        waiting = []
        received = swap(sent, "sub", 1, f"hidden{group[0]}")
        if moved is not None:
            received = after(received, moved)
        products = call(
            functools.partial(back_kernel, most, narrow, group),
            [block] * (len(group) * narrow),
            summed,
            received,
            pre,
            gate,
            up,
            name="back",
        )
        for at, k in enumerate(group):
            mine, others = products[at * narrow], products[at * narrow + 1 : (at + 1) * narrow]
            if k == 0:
                returned[0], own = mine, others
            elif k != group[0] and not extra:
                waiting.append((k, mine, others))
            else:
                total, returned[k] = give_back(k, mine, others)
                if k == group[0]:
                    moved = total
    own = [swap(after(value, moved), "tp", j + 1, "back0") for j, value in enumerate(own)]
    tail = received[count : count + 4, :tokens].astype(f32)
    row_sums = row_sums + tail[:2] + tail[2:]
    inverse_rms = lax.rsqrt(row_sums[0] / LAT + 1e-06)[:, None]
    d_latent = (
        inverse_rms * gained - values * inverse_rms**3 * row_sums[1][:, None] / LAT
    ).astype(bf16)
    latest = groups[-1][:1] if len(groups) > 1 else []
    distances = [k for k in sorted(returned, reverse=True) if k not in latest]
    (grad_input,) = call(
        functools.partial(unpack_kernel, distances, False),
        [pltpu.VMEM((tokens, width), bf16) if latest else jax.ShapeDtypeStruct((tokens, width), bf16)],
        place,
        *[returned[k] for k in distances],
        *own,
        name="unpack",
    )
    if latest:
        (grad_input,) = call(
            functools.partial(unpack_kernel, latest, True),
            [jax.ShapeDtypeStruct((tokens, width), bf16)],
            place,
            *[returned[k] for k in latest],
            grad_input,
            name="unpack_latest",
        )
    return (grad_input, d_latent)


def solution(mesh):
    placed = (
        P(("rep", "ep", "tp"), "sub"),
        P(("rep", "ep", "tp"), "sub"),
        P(("rep", "ep", "tp"), None),
        P(("rep", "ep", "tp"), None),
        P("ep", "sub", "tp"),
        P("ep", "sub", "tp"),
        P("ep", "tp", "sub"),
        P(("rep", "ep"), None, None, "tp"),
        P("tp", ("rep", "ep"), "sub"),
        P(("rep", "ep", "tp"), "sub"),
        P("sub"),
    )
    return jax.shard_map(
        local,
        mesh=mesh,
        in_specs=placed,
        out_specs=(P(("rep", "ep", "tp"), "sub"), P(("rep", "ep", "tp"), "sub")),
        check_vma=False,
    )
```

```python
import functools

import jax
import jax.numpy as jnp
from jax import lax
from jax.experimental import pallas as pl
from jax.experimental.pallas import tpu as pltpu
from jax.sharding import PartitionSpec as P

LAT = 512
NT = (((1,), (1,)), ((), ()))
TN = (((0,), (0,)), ((), ()))
VMEM = pl.BlockSpec(memory_space=pltpu.VMEM)
ANY = pl.BlockSpec(memory_space=pl.ANY)
HBM = pl.BlockSpec(memory_space=pltpu.HBM)
EXTRA = 16
VMEM_LIMIT = 20 * 1024 * 1024


def dot(a, b, dims, precision=None):
    return lax.dot_general(a, b, dims, precision=precision, preferred_element_type=jnp.float32)


def swap(value, axis, step, what):
    count = lax.axis_size(axis)
    with jax.named_scope(f"{what}_{axis}"):
        return lax.ppermute(value, axis, [(i, i ^ step) for i in range(count)])


def pinned(*arrays):
    return [pltpu.with_memory_space_constraint(array, pltpu.HBM) for array in arrays]


def like(array):
    return pltpu.VMEM(array.shape, array.dtype)


def call(kernel, outs, *args, cost=0, name=None, specs=None, scratch=(), earlier=()):
    specs = (specs or [VMEM] * len(args)) + [ANY] * len(earlier)
    if earlier:
        taken, body = len(args), kernel

        def kernel(*refs):
            body(*refs[:taken], *refs[taken + len(earlier) :])

    return pl.pallas_call(
        kernel,
        out_shape=outs,
        in_specs=specs,
        out_specs=[VMEM] * len(outs),
        scratch_shapes=scratch,
        compiler_params=pltpu.CompilerParams(vmem_limit_bytes=VMEM_LIMIT),
        cost_estimate=pl.CostEstimate(flops=cost, bytes_accessed=0, transcendentals=0),
        name=name,
    )(*args, *earlier)


def after(value, earlier, cost=0):
    return pl.pallas_call(
        lambda value_ref, earlier_ref, out_ref: None,
        out_shape=jax.ShapeDtypeStruct(value.shape, value.dtype),
        in_specs=[ANY, ANY],
        out_specs=ANY,
        input_output_aliases={0: 0},
        compiler_params=pltpu.CompilerParams(vmem_limit_bytes=1 << 17),
        cost_estimate=pl.CostEstimate(flops=cost, bytes_accessed=0, transcendentals=0),
        name="after",
    )(value, earlier)


def fill(block_ref, most, low, high, weights_ref, scales_ref, grad_ref):
    half, scale_half = grad_ref.shape[1] // 2, scales_ref.shape[0] // 2
    placed = jnp.dot(
        low.astype(jnp.bfloat16), grad_ref[:, :half], preferred_element_type=jnp.float32
    )
    placed += jnp.dot(
        high.astype(jnp.bfloat16), grad_ref[:, half:], preferred_element_type=jnp.float32
    )
    scale = dot(low.astype(jnp.float32), scales_ref[:scale_half], NT, lax.Precision.HIGHEST)
    scale += dot(high.astype(jnp.float32), scales_ref[scale_half:], NT, lax.Precision.HIGHEST)
    weight = jnp.sum(jnp.where(low | high, weights_ref[...], 0.0), axis=1, keepdims=True)
    for b in range(scale_half):
        part = slice(b * 128, (b + 1) * 128)
        block_ref[:, part] = (placed[:, part] * scale[:, b : b + 1] * weight).astype(jnp.bfloat16)


def fetch(sources, targets, sems, first=0):
    copies = [
        pltpu.make_async_copy(source, target, sems.at[first + i])
        for i, (source, target) in enumerate(zip(sources, targets))
    ]
    for copy in copies:
        copy.start()
    return copies


def pack_kernel(most, order, *refs):
    given, partial_ref, refs = refs[:4], refs[4], refs[5:]
    blocks, (place_ref, share_ref), refs = refs[: len(order)], refs[len(order) :][:2], refs[-6:]
    held, sems, share_sems = refs[:4], refs[4], refs[5]
    lane, count = lax.axis_index("tp"), partial_ref.shape[0]
    copies = fetch(given, held, sems)
    shares = fetch(
        [partial_ref.at[lane ^ j] for j in range(count)],
        [share_ref.at[j] for j in range(count)],
        share_sems,
    )
    copies[0].wait()
    ids_ref, weights_ref, scales_ref, grad_ref = held
    tokens, rows = grad_ref.shape[0], blocks[0].shape[0]
    me = lax.axis_index("ep")
    ids = ids_ref[...]
    expert = lax.broadcasted_iota(jnp.int32, (max(8, len(order)), tokens), 0)
    named = expert == ids
    before = lax.broadcasted_iota(jnp.int32, (tokens, tokens), 0) < lax.broadcasted_iota(
        jnp.int32, (tokens, tokens), 1
    )
    earlier = jnp.dot(
        named.astype(jnp.bfloat16), before.astype(jnp.bfloat16), preferred_element_type=jnp.float32
    )
    position = jnp.sum(jnp.where(named, earlier, 0.0), axis=0, keepdims=True).astype(jnp.int32)
    row = lax.broadcasted_iota(jnp.int32, (rows, tokens), 0)
    found = []
    for k in order:
        local = jnp.where(ids == (me ^ k), position, -2 * rows)
        low, high = row == local, row - most == local
        found.append((low, high))
        place_ref[0, k] = low.astype(jnp.bfloat16)
        place_ref[1, k] = high.astype(jnp.bfloat16)
    for copy in copies[1:]:
        copy.wait()
    for block_ref, (low, high) in zip(blocks, found):
        fill(block_ref, most, low, high, weights_ref, scales_ref, grad_ref)
    for copy in shares:
        copy.wait()


def fetch_kernel(*refs):
    count = len(refs) // 2
    for copy in fetch(refs[:count], refs[count : 2 * count], refs[-1]):
        copy.wait()


def hidden_kernel(most, extra, *refs):
    blocks, (down_ref, sum_ref, sent_ref) = refs[:-3], refs[-3:]
    half = down_ref.shape[1] // 2
    count = sum_ref.shape[0]
    if extra:
        blocks, row_sums = blocks[:-1], blocks[-1][...]
        high = row_sums.astype(jnp.bfloat16).astype(jnp.float32)
        spare = jnp.zeros((EXTRA - 4, row_sums.shape[1]), jnp.float32)
        tail = jnp.concatenate([high, row_sums - high, spare], axis=0)
        sent_ref[count:, :] = jnp.zeros((EXTRA, sent_ref.shape[1]), jnp.bfloat16)
        sent_ref[count:, : row_sums.shape[1]] = tail.astype(jnp.bfloat16)
    values = [b[...].astype(jnp.float32) for b in blocks]
    low = jnp.concatenate([v[:most] for v in values], axis=0).astype(jnp.bfloat16)
    high = jnp.concatenate([v[most : 2 * most] for v in values], axis=0).astype(jnp.bfloat16)
    total = dot(low, down_ref[:, :half], NT) + dot(high, down_ref[:, half:], NT)
    sum_ref[...] = total
    sent_ref[:count, :] = total.astype(jnp.bfloat16)


def by_xor(value, most, narrow, lane):
    step = 1
    while step < narrow:
        pieces = [value[i * most : (i + step) * most] for i in range(0, narrow, step)]
        turned = [pieces[i ^ 1] for i in range(len(pieces))]
        value = jnp.where((lane & step) != 0, jnp.concatenate(turned, axis=0), value)
        step *= 2
    return value


def back_kernel(most, narrow, group, sum_ref, other_ref, pre_ref, gate_ref, up_ref, *outs):
    half = gate_ref.shape[0] // 2
    me, lane = lax.axis_index("ep"), lax.axis_index("tp")
    hidden = sum_ref[...] + other_ref[: sum_ref.shape[0], :].astype(jnp.float32)
    gate_pre, up_pre = [
        jnp.concatenate(
            [by_xor(pre_ref[i, me ^ k].astype(jnp.float32), most, narrow, lane) for k in group],
            axis=0,
        )
        for i in range(2)
    ]
    sig = 1.0 / (1.0 + jnp.exp(-gate_pre))
    up_grad = (hidden * gate_pre * sig).astype(jnp.bfloat16)
    gate_grad = (hidden * up_pre * sig * (1.0 + gate_pre * (1.0 - sig))).astype(jnp.bfloat16)
    low = dot(gate_grad, gate_ref[:half], NT) + dot(up_grad, up_ref[:half], NT)
    high = dot(gate_grad, gate_ref[half:], NT) + dot(up_grad, up_ref[half:], NT)
    for i, out in enumerate(outs):
        part = slice(i * most, (i + 1) * most)
        pieces = [low[part], high[part]]
        spare = out.shape[0] - 2 * most
        if spare:
            pieces.append(jnp.zeros((spare, half), jnp.float32))
        out[...] = jnp.concatenate(pieces, axis=0).astype(jnp.bfloat16)


def unpack_kernel(distances, started, place_ref, *refs):
    blocks, others, out_ref = refs[: len(distances)], refs[len(distances) : -1], refs[-1]
    if started:
        others, so_far_ref = others[:-1], others[-1]
    half = out_ref.shape[1] // 2
    for side in range(2):
        columns = slice(side * half, (side + 1) * half)
        total = so_far_ref[:, columns].astype(jnp.float32) if started else 0.0
        for k, block_ref in zip(distances, blocks):
            rows = block_ref[...]
            if k == 0:
                rows = rows.astype(jnp.float32)
                for other_ref in others:
                    rows += other_ref[...].astype(jnp.float32)
                rows = rows.astype(jnp.bfloat16)
            total = total + dot(place_ref[side, k], rows, TN)
        out_ref[:, columns] = total.astype(jnp.bfloat16)


def groups_of(wide):
    if wide < 4:
        return [list(range(wide - 1, -1, -1))]
    left = list(range(wide - 2, 1, -1))
    return [[wide - 1, 1, 0]] + [left[i : i + 2] for i in range(0, len(left), 2)]


def local(
    grad_values,
    grad_scales,
    expert_ids,
    route_weights,
    w_gate,
    w_up,
    w_down,
    pre_acts,
    latent_partials,
    latent,
    latent_gain,
):
    wide, narrow = lax.axis_size("ep"), lax.axis_size("tp")
    tokens, width = grad_values.shape
    half = width // 2
    slots, hidden_width = pre_acts.shape[2:]
    most = slots // (wide * narrow)
    rows = -(-2 * most // 8) * 8
    f32, bf16 = jnp.float32, jnp.bfloat16
    block = pltpu.VMEM((rows, half), bf16)
    groups = groups_of(wide)
    order = [k for group in groups for k in group]
    partials = latent_partials.reshape(narrow, tokens, latent.shape[1])
    packed = call(
        functools.partial(pack_kernel, most, order),
        [block] * wide + [pltpu.VMEM((2, wide, rows, tokens), bf16), like(partials)],
        *pinned(
            expert_ids.reshape(1, tokens),
            route_weights.reshape(1, tokens),
            grad_scales.T,
            grad_values,
            partials,
        ),
        specs=[HBM] * 5,
        scratch=[
            pltpu.VMEM((1, tokens), jnp.int32),
            pltpu.VMEM((1, tokens), f32),
            pltpu.VMEM((grad_scales.shape[1], tokens), f32),
            pltpu.VMEM((tokens, width), bf16),
            pltpu.SemaphoreType.DMA((4,)),
            pltpu.SemaphoreType.DMA((narrow,)),
        ],
        name="pack",
    )
    place, shares = packed[wide:]
    packed = dict(zip(order, packed))

    def across(k, rows_of_k):
        return [rows_of_k] + [swap(rows_of_k, "tp", j, f"rows{k}") for j in range(1, narrow)]

    taken = {0: across(0, packed[0])}
    first = groups[0][0]
    arrived = {}
    for k in order:
        if k:
            given = packed[k] if k in groups[0] else after(packed[k], arrived[1])
            arrived[k] = swap(given, "ep", k, f"rows{k}")
            if len(groups) > 1 and k == groups[1][0]:
                arrived[k] = after(arrived[k], packed[first], 1 << 31)
    fetched = [
        w_down[0],
        pre_acts.reshape(2, wide, narrow * most, hidden_width),
        w_gate[0],
        w_up[0],
        latent,
        latent_gain.reshape(1, -1),
    ]
    down, pre, gate, up, latent, latent_gain = call(
        fetch_kernel,
        [like(array) for array in fetched],
        *pinned(*fetched),
        specs=[HBM] * len(fetched),
        scratch=[pltpu.SemaphoreType.DMA((len(fetched),))],
        cost=1 << 31,
        earlier=[arrived[first]],
        name="fetch",
    )
    latent_parts = [shares[0]] + [
        swap(shares[j], "tp", j, "latent") for j in range(1, narrow)
    ]

    def give_back(k, mine, others):
        others = [swap(other, "tp", j + 1, f"back{k}") for j, other in enumerate(others)]
        total = mine.astype(f32)
        for other in others:
            total += other.astype(f32)
        total = total.astype(bf16)
        return total, swap(total, "ep", k, f"back{k}")

    returned = {}
    own, waiting = [], []
    values = latent.astype(f32)
    received, products, moved = None, None, None
    for group in groups:
        for k in group:
            if k == 0:
                continue
            taken[k] = across(k, arrived[k])
            if received is not None:
                taken[k][-1] = after(taken[k][-1], products[0])
            elif k != first and narrow > 1:
                taken[k][-1] = after(taken[k][-1], packed[first], 1 << 31)
        count = len(group) * narrow * most
        extra = group is groups[-1]
        if extra:
            if received is not None:
                latent_parts[-1] = after(latent_parts[-1], summed, 1 << 30)
            own_grad = sum(part.astype(f32) for part in latent_parts)
            gained = own_grad * latent_gain
            row_sums = jnp.stack(
                [jnp.sum(values * values, axis=1), jnp.sum(gained * values, axis=1)]
            )
        summed, sent = call(
            functools.partial(hidden_kernel, most, extra),
            [
                pltpu.VMEM((count, hidden_width), f32),
                pltpu.VMEM((count + (EXTRA if extra else 0), hidden_width), bf16),
            ],
            *[rows_of_k for k in group for rows_of_k in taken[k]],
            *([row_sums] if extra else []),
            down,
            name="hidden",
            earlier=products[:1] if products else (),
        )
        for k, mine, others in waiting:
            others = [after(other, summed) for other in others]
            returned[k] = give_back(k, mine, others)[1]
        waiting = []
        received = swap(sent, "sub", 1, f"hidden{group[0]}")
        if moved is not None:
            received = after(received, moved)
        products = call(
            functools.partial(back_kernel, most, narrow, group),
            [block] * (len(group) * narrow),
            summed,
            received,
            pre,
            gate,
            up,
            name="back",
        )
        for at, k in enumerate(group):
            mine, others = products[at * narrow], products[at * narrow + 1 : (at + 1) * narrow]
            if k == 0:
                returned[0], own = mine, others
            elif k != group[0] and not extra:
                waiting.append((k, mine, others))
            else:
                total, returned[k] = give_back(k, mine, others)
                if k == group[0]:
                    moved = total
    own = [swap(after(value, moved), "tp", j + 1, "back0") for j, value in enumerate(own)]
    tail = received[count : count + 4, :tokens].astype(f32)
    row_sums = row_sums + tail[:2] + tail[2:]
    inverse_rms = lax.rsqrt(row_sums[0] / LAT + 1e-06)[:, None]
    d_latent = (
        inverse_rms * gained - values * inverse_rms**3 * row_sums[1][:, None] / LAT
    ).astype(bf16)
    latest = groups[-1][:1] if len(groups) > 1 else []
    distances = [k for k in sorted(returned, reverse=True) if k not in latest]
    (grad_input,) = call(
        functools.partial(unpack_kernel, distances, False),
        [pltpu.VMEM((tokens, width), bf16) if latest else jax.ShapeDtypeStruct((tokens, width), bf16)],
        place,
        *[returned[k] for k in distances],
        *own,
        name="unpack",
    )
    if latest:
        (grad_input,) = call(
            functools.partial(unpack_kernel, latest, True),
            [jax.ShapeDtypeStruct((tokens, width), bf16)],
            place,
            *[returned[k] for k in latest],
            grad_input,
            name="unpack_latest",
        )
    return (grad_input, d_latent)


def solution(mesh):
    placed = (
        P(("rep", "ep", "tp"), "sub"),
        P(("rep", "ep", "tp"), "sub"),
        P(("rep", "ep", "tp"), None),
        P(("rep", "ep", "tp"), None),
        P("ep", "sub", "tp"),
        P("ep", "sub", "tp"),
        P("ep", "tp", "sub"),
        P(("rep", "ep"), None, None, "tp"),
        P("tp", ("rep", "ep"), "sub"),
        P(("rep", "ep", "tp"), "sub"),
        P("sub"),
    )
    return jax.shard_map(
        local,
        mesh=mesh,
        in_specs=placed,
        out_specs=(P(("rep", "ep", "tp"), "sub"), P(("rep", "ep", "tp"), "sub")),
        check_vma=False,
    )
```

```python
import functools

import jax
import jax.numpy as jnp
from jax import lax
from jax.experimental import pallas as pl
from jax.experimental.pallas import tpu as pltpu
from jax.sharding import PartitionSpec as P

LAT = 512
NT = (((1,), (1,)), ((), ()))
TN = (((0,), (0,)), ((), ()))
VMEM = pl.BlockSpec(memory_space=pltpu.VMEM)
ANY = pl.BlockSpec(memory_space=pl.ANY)
HBM = pl.BlockSpec(memory_space=pltpu.HBM)
EXTRA = 16
VMEM_LIMIT = 20 * 1024 * 1024


def dot(a, b, dims, precision=None):
    return lax.dot_general(a, b, dims, precision=precision, preferred_element_type=jnp.float32)


def swap(value, axis, step, what):
    count = lax.axis_size(axis)
    with jax.named_scope(f"{what}_{axis}"):
        return lax.ppermute(value, axis, [(i, i ^ step) for i in range(count)])


def pinned(*arrays):
    return [pltpu.with_memory_space_constraint(array, pltpu.HBM) for array in arrays]


def like(array):
    return pltpu.VMEM(array.shape, array.dtype)


def call(kernel, outs, *args, cost=0, name=None, specs=None, scratch=(), earlier=()):
    specs = (specs or [VMEM] * len(args)) + [ANY] * len(earlier)
    if earlier:
        taken, body = len(args), kernel

        def kernel(*refs):
            body(*refs[:taken], *refs[taken + len(earlier) :])

    return pl.pallas_call(
        kernel,
        out_shape=outs,
        in_specs=specs,
        out_specs=[VMEM] * len(outs),
        scratch_shapes=scratch,
        compiler_params=pltpu.CompilerParams(vmem_limit_bytes=VMEM_LIMIT),
        cost_estimate=pl.CostEstimate(flops=cost, bytes_accessed=0, transcendentals=0),
        name=name,
    )(*args, *earlier)


def after(value, earlier, cost=0):
    return pl.pallas_call(
        lambda value_ref, earlier_ref, out_ref: None,
        out_shape=jax.ShapeDtypeStruct(value.shape, value.dtype),
        in_specs=[ANY, ANY],
        out_specs=ANY,
        input_output_aliases={0: 0},
        compiler_params=pltpu.CompilerParams(vmem_limit_bytes=1 << 17),
        cost_estimate=pl.CostEstimate(flops=cost, bytes_accessed=0, transcendentals=0),
        name="after",
    )(value, earlier)


def fill(block_ref, most, low, high, weights_ref, scales_ref, grad_ref):
    half, scale_half = grad_ref.shape[1] // 2, scales_ref.shape[0] // 2
    placed = jnp.dot(
        low.astype(jnp.bfloat16), grad_ref[:, :half], preferred_element_type=jnp.float32
    )
    placed += jnp.dot(
        high.astype(jnp.bfloat16), grad_ref[:, half:], preferred_element_type=jnp.float32
    )
    scale = dot(low.astype(jnp.float32), scales_ref[:scale_half], NT, lax.Precision.HIGHEST)
    scale += dot(high.astype(jnp.float32), scales_ref[scale_half:], NT, lax.Precision.HIGHEST)
    weight = jnp.sum(jnp.where(low | high, weights_ref[...], 0.0), axis=1, keepdims=True)
    for b in range(scale_half):
        part = slice(b * 128, (b + 1) * 128)
        block_ref[:, part] = (placed[:, part] * scale[:, b : b + 1] * weight).astype(jnp.bfloat16)


def fetch(sources, targets, sems, first=0):
    copies = [
        pltpu.make_async_copy(source, target, sems.at[first + i])
        for i, (source, target) in enumerate(zip(sources, targets))
    ]
    for copy in copies:
        copy.start()
    return copies


def pack_kernel(most, order, *refs):
    given, partial_ref, refs = refs[:4], refs[4], refs[5:]
    blocks, (place_ref, share_ref), refs = refs[: len(order)], refs[len(order) :][:2], refs[-6:]
    held, sems, share_sems = refs[:4], refs[4], refs[5]
    lane, count = lax.axis_index("tp"), partial_ref.shape[0]
    copies = fetch(given, held, sems)
    shares = fetch(
        [partial_ref.at[lane ^ j] for j in range(count)],
        [share_ref.at[j] for j in range(count)],
        share_sems,
    )
    copies[0].wait()
    ids_ref, weights_ref, scales_ref, grad_ref = held
    tokens, rows = grad_ref.shape[0], blocks[0].shape[0]
    me = lax.axis_index("ep")
    ids = ids_ref[...]
    expert = lax.broadcasted_iota(jnp.int32, (max(8, len(order)), tokens), 0)
    named = expert == ids
    before = lax.broadcasted_iota(jnp.int32, (tokens, tokens), 0) < lax.broadcasted_iota(
        jnp.int32, (tokens, tokens), 1
    )
    earlier = jnp.dot(
        named.astype(jnp.bfloat16), before.astype(jnp.bfloat16), preferred_element_type=jnp.float32
    )
    position = jnp.sum(jnp.where(named, earlier, 0.0), axis=0, keepdims=True).astype(jnp.int32)
    row = lax.broadcasted_iota(jnp.int32, (rows, tokens), 0)
    found = []
    for k in order:
        local = jnp.where(ids == (me ^ k), position, -2 * rows)
        low, high = row == local, row - most == local
        found.append((low, high))
        place_ref[0, k] = low.astype(jnp.bfloat16)
        place_ref[1, k] = high.astype(jnp.bfloat16)
    for copy in copies[1:]:
        copy.wait()
    for block_ref, (low, high) in zip(blocks, found):
        fill(block_ref, most, low, high, weights_ref, scales_ref, grad_ref)
    for copy in shares:
        copy.wait()


def fetch_kernel(*refs):
    count = len(refs) // 2
    for copy in fetch(refs[:count], refs[count : 2 * count], refs[-1]):
        copy.wait()


def hidden_kernel(most, extra, *refs):
    blocks, (down_ref, sum_ref, sent_ref) = refs[:-3], refs[-3:]
    half = down_ref.shape[1] // 2
    count = sum_ref.shape[0]
    if extra:
        blocks, row_sums = blocks[:-1], blocks[-1][...]
        high = row_sums.astype(jnp.bfloat16).astype(jnp.float32)
        spare = jnp.zeros((EXTRA - 4, row_sums.shape[1]), jnp.float32)
        tail = jnp.concatenate([high, row_sums - high, spare], axis=0)
        sent_ref[count:, :] = jnp.zeros((EXTRA, sent_ref.shape[1]), jnp.bfloat16)
        sent_ref[count:, : row_sums.shape[1]] = tail.astype(jnp.bfloat16)
    values = [b[...].astype(jnp.float32) for b in blocks]
    low = jnp.concatenate([v[:most] for v in values], axis=0).astype(jnp.bfloat16)
    high = jnp.concatenate([v[most : 2 * most] for v in values], axis=0).astype(jnp.bfloat16)
    total = dot(low, down_ref[:, :half], NT) + dot(high, down_ref[:, half:], NT)
    sum_ref[...] = total
    sent_ref[:count, :] = total.astype(jnp.bfloat16)


def by_xor(value, most, narrow, lane):
    step = 1
    while step < narrow:
        pieces = [value[i * most : (i + step) * most] for i in range(0, narrow, step)]
        turned = [pieces[i ^ 1] for i in range(len(pieces))]
        value = jnp.where((lane & step) != 0, jnp.concatenate(turned, axis=0), value)
        step *= 2
    return value


def back_kernel(most, narrow, group, sum_ref, other_ref, pre_ref, gate_ref, up_ref, *outs):
    half = gate_ref.shape[0] // 2
    me, lane = lax.axis_index("ep"), lax.axis_index("tp")
    hidden = sum_ref[...] + other_ref[: sum_ref.shape[0], :].astype(jnp.float32)
    gate_pre, up_pre = [
        jnp.concatenate(
            [by_xor(pre_ref[i, me ^ k].astype(jnp.float32), most, narrow, lane) for k in group],
            axis=0,
        )
        for i in range(2)
    ]
    sig = 1.0 / (1.0 + jnp.exp(-gate_pre))
    up_grad = (hidden * gate_pre * sig).astype(jnp.bfloat16)
    gate_grad = (hidden * up_pre * sig * (1.0 + gate_pre * (1.0 - sig))).astype(jnp.bfloat16)
    low = dot(gate_grad, gate_ref[:half], NT) + dot(up_grad, up_ref[:half], NT)
    high = dot(gate_grad, gate_ref[half:], NT) + dot(up_grad, up_ref[half:], NT)
    for i, out in enumerate(outs):
        part = slice(i * most, (i + 1) * most)
        pieces = [low[part], high[part]]
        spare = out.shape[0] - 2 * most
        if spare:
            pieces.append(jnp.zeros((spare, half), jnp.float32))
        out[...] = jnp.concatenate(pieces, axis=0).astype(jnp.bfloat16)


def unpack_kernel(distances, started, place_ref, *refs):
    blocks, others, out_ref = refs[: len(distances)], refs[len(distances) : -1], refs[-1]
    if started:
        others, so_far_ref = others[:-1], others[-1]
    half = out_ref.shape[1] // 2
    for side in range(2):
        columns = slice(side * half, (side + 1) * half)
        total = so_far_ref[:, columns].astype(jnp.float32) if started else 0.0
        for k, block_ref in zip(distances, blocks):
            rows = block_ref[...]
            if k == 0:
                rows = rows.astype(jnp.float32)
                for other_ref in others:
                    rows += other_ref[...].astype(jnp.float32)
                rows = rows.astype(jnp.bfloat16)
            total = total + dot(place_ref[side, k], rows, TN)
        out_ref[:, columns] = total.astype(jnp.bfloat16)


def groups_of(wide):
    if wide < 4:
        return [list(range(wide - 1, -1, -1))]
    left = list(range(wide - 2, 1, -1))
    return [[wide - 1, 1, 0]] + [left[i : i + 2] for i in range(0, len(left), 2)]


def local(
    grad_values,
    grad_scales,
    expert_ids,
    route_weights,
    w_gate,
    w_up,
    w_down,
    pre_acts,
    latent_partials,
    latent,
    latent_gain,
):
    wide, narrow = lax.axis_size("ep"), lax.axis_size("tp")
    tokens, width = grad_values.shape
    half = width // 2
    slots, hidden_width = pre_acts.shape[2:]
    most = slots // (wide * narrow)
    rows = -(-2 * most // 8) * 8
    f32, bf16 = jnp.float32, jnp.bfloat16
    block = pltpu.VMEM((rows, half), bf16)
    groups = groups_of(wide)
    order = [k for group in groups for k in group]
    partials = latent_partials.reshape(narrow, tokens, latent.shape[1])
    packed = call(
        functools.partial(pack_kernel, most, order),
        [block] * wide + [pltpu.VMEM((2, wide, rows, tokens), bf16), like(partials)],
        *pinned(
            expert_ids.reshape(1, tokens),
            route_weights.reshape(1, tokens),
            grad_scales.T,
            grad_values,
            partials,
        ),
        specs=[HBM] * 5,
        scratch=[
            pltpu.VMEM((1, tokens), jnp.int32),
            pltpu.VMEM((1, tokens), f32),
            pltpu.VMEM((grad_scales.shape[1], tokens), f32),
            pltpu.VMEM((tokens, width), bf16),
            pltpu.SemaphoreType.DMA((4,)),
            pltpu.SemaphoreType.DMA((narrow,)),
        ],
        name="pack",
    )
    place, shares = packed[wide:]
    packed = dict(zip(order, packed))

    def across(k, rows_of_k):
        return [rows_of_k] + [swap(rows_of_k, "tp", j, f"rows{k}") for j in range(1, narrow)]

    taken = {0: across(0, packed[0])}
    first = groups[0][0]
    arrived = {}
    for k in order:
        if k:
            given = packed[k] if k in groups[0] else after(packed[k], arrived[first])
            arrived[k] = swap(given, "ep", k, f"rows{k}")
            if len(groups) > 1 and k == groups[1][0]:
                arrived[k] = after(arrived[k], packed[first], 1 << 31)
    fetched = [
        w_down[0],
        pre_acts.reshape(2, wide, narrow * most, hidden_width),
        w_gate[0],
        w_up[0],
        latent,
        latent_gain.reshape(1, -1),
    ]
    down, pre, gate, up, latent, latent_gain = call(
        fetch_kernel,
        [like(array) for array in fetched],
        *pinned(*fetched),
        specs=[HBM] * len(fetched),
        scratch=[pltpu.SemaphoreType.DMA((len(fetched),))],
        earlier=[arrived[first]],
        name="fetch",
    )
    latent_parts = [shares[0]] + [
        swap(shares[j], "tp", j, "latent") for j in range(1, narrow)
    ]

    def give_back(k, mine, others):
        others = [swap(other, "tp", j + 1, f"back{k}") for j, other in enumerate(others)]
        total = mine.astype(f32)
        for other in others:
            total += other.astype(f32)
        total = total.astype(bf16)
        return total, swap(total, "ep", k, f"back{k}")

    returned = {}
    own, waiting = [], []
    values = latent.astype(f32)
    received, products, moved = None, None, None
    for group in groups:
        for k in group:
            if k == 0:
                continue
            taken[k] = across(k, arrived[k])
            if received is not None:
                taken[k][-1] = after(taken[k][-1], products[0])
            elif k != first and narrow > 1:
                taken[k][-1] = after(taken[k][-1], packed[first], 1 << 31)
        count = len(group) * narrow * most
        extra = group is groups[-1]
        if extra:
            if received is not None:
                latent_parts[-1] = after(latent_parts[-1], summed, 1 << 30)
            own_grad = sum(part.astype(f32) for part in latent_parts)
            gained = own_grad * latent_gain
            row_sums = jnp.stack(
                [jnp.sum(values * values, axis=1), jnp.sum(gained * values, axis=1)]
            )
        summed, sent = call(
            functools.partial(hidden_kernel, most, extra),
            [
                pltpu.VMEM((count, hidden_width), f32),
                pltpu.VMEM((count + (EXTRA if extra else 0), hidden_width), bf16),
            ],
            *[rows_of_k for k in group for rows_of_k in taken[k]],
            *([row_sums] if extra else []),
            down,
            name="hidden",
            earlier=products[:1] if products else (),
        )
        for k, mine, others in waiting:
            others = [after(other, summed) for other in others]
            returned[k] = give_back(k, mine, others)[1]
        waiting = []
        received = swap(sent, "sub", 1, f"hidden{group[0]}")
        if moved is not None:
            received = after(received, moved)
        products = call(
            functools.partial(back_kernel, most, narrow, group),
            [block] * (len(group) * narrow),
            summed,
            received,
            pre,
            gate,
            up,
            name="back",
        )
        for at, k in enumerate(group):
            mine, others = products[at * narrow], products[at * narrow + 1 : (at + 1) * narrow]
            if k == 0:
                returned[0], own = mine, others
            elif k != group[0] and not extra:
                waiting.append((k, mine, others))
            else:
                total, returned[k] = give_back(k, mine, others)
                if k == group[0]:
                    moved = total
    own = [swap(after(value, moved), "tp", j + 1, "back0") for j, value in enumerate(own)]
    tail = received[count : count + 4, :tokens].astype(f32)
    row_sums = row_sums + tail[:2] + tail[2:]
    inverse_rms = lax.rsqrt(row_sums[0] / LAT + 1e-06)[:, None]
    d_latent = (
        inverse_rms * gained - values * inverse_rms**3 * row_sums[1][:, None] / LAT
    ).astype(bf16)
    latest = groups[-1][:1] if len(groups) > 1 else []
    distances = [k for k in sorted(returned, reverse=True) if k not in latest]
    (grad_input,) = call(
        functools.partial(unpack_kernel, distances, False),
        [pltpu.VMEM((tokens, width), bf16) if latest else jax.ShapeDtypeStruct((tokens, width), bf16)],
        place,
        *[returned[k] for k in distances],
        *own,
        name="unpack",
    )
    if latest:
        (grad_input,) = call(
            functools.partial(unpack_kernel, latest, True),
            [jax.ShapeDtypeStruct((tokens, width), bf16)],
            place,
            *[returned[k] for k in latest],
            grad_input,
            name="unpack_latest",
        )
    return (grad_input, d_latent)


def solution(mesh):
    placed = (
        P(("rep", "ep", "tp"), "sub"),
        P(("rep", "ep", "tp"), "sub"),
        P(("rep", "ep", "tp"), None),
        P(("rep", "ep", "tp"), None),
        P("ep", "sub", "tp"),
        P("ep", "sub", "tp"),
        P("ep", "tp", "sub"),
        P(("rep", "ep"), None, None, "tp"),
        P("tp", ("rep", "ep"), "sub"),
        P(("rep", "ep", "tp"), "sub"),
        P("sub"),
    )
    return jax.shard_map(
        local,
        mesh=mesh,
        in_specs=placed,
        out_specs=(P(("rep", "ep", "tp"), "sub"), P(("rep", "ep", "tp"), "sub")),
        check_vma=False,
    )
```

```python
import functools

import jax
import jax.numpy as jnp
import numpy as np
from jax import lax
from jax.experimental import pallas as pl
from jax.experimental.pallas import tpu as pltpu
from jax.sharding import PartitionSpec as P

LAT = 512
NT = (((1,), (1,)), ((), ()))
TN = (((0,), (0,)), ((), ()))
VMEM = pl.BlockSpec(memory_space=pltpu.VMEM)
ANY = pl.BlockSpec(memory_space=pl.ANY)
HBM = pl.BlockSpec(memory_space=pltpu.HBM)
EXTRA = 16
VMEM_LIMIT = 20 * 1024 * 1024


def dot(a, b, dims, precision=None):
    return lax.dot_general(a, b, dims, precision=precision, preferred_element_type=jnp.float32)


def swap(value, what, **steps):
    counts = [lax.axis_size(axis) for axis in steps]
    pairs = []
    for place in np.ndindex(*counts):
        other = [index ^ step for index, step in zip(place, steps.values())]
        pairs.append(tuple(int(np.ravel_multi_index(p, counts)) for p in (place, other)))
    with jax.named_scope("_".join([what, *steps])):
        return lax.ppermute(value, tuple(steps), pairs)


def pinned(*arrays):
    return [pltpu.with_memory_space_constraint(array, pltpu.HBM) for array in arrays]


def like(array):
    return pltpu.VMEM(array.shape, array.dtype)


def call(kernel, outs, *args, cost=0, name=None, specs=None, scratch=(), earlier=()):
    specs = (specs or [VMEM] * len(args)) + [ANY] * len(earlier)
    if earlier:
        taken, body = len(args), kernel

        def kernel(*refs):
            body(*refs[:taken], *refs[taken + len(earlier) :])

    return pl.pallas_call(
        kernel,
        out_shape=outs,
        in_specs=specs,
        out_specs=[VMEM] * len(outs),
        scratch_shapes=scratch,
        compiler_params=pltpu.CompilerParams(vmem_limit_bytes=VMEM_LIMIT),
        cost_estimate=pl.CostEstimate(flops=cost, bytes_accessed=0, transcendentals=0),
        name=name,
    )(*args, *earlier)


def after(value, earlier, cost=0):
    return pl.pallas_call(
        lambda value_ref, earlier_ref, out_ref: None,
        out_shape=jax.ShapeDtypeStruct(value.shape, value.dtype),
        in_specs=[ANY, ANY],
        out_specs=ANY,
        input_output_aliases={0: 0},
        compiler_params=pltpu.CompilerParams(vmem_limit_bytes=1 << 17),
        cost_estimate=pl.CostEstimate(flops=cost, bytes_accessed=0, transcendentals=0),
        name="after",
    )(value, earlier)


def fill(block_ref, most, low, high, weights_ref, scales_ref, grad_ref):
    half, scale_half = grad_ref.shape[1] // 2, scales_ref.shape[0] // 2
    placed = jnp.dot(
        low.astype(jnp.bfloat16), grad_ref[:, :half], preferred_element_type=jnp.float32
    )
    placed += jnp.dot(
        high.astype(jnp.bfloat16), grad_ref[:, half:], preferred_element_type=jnp.float32
    )
    scale = dot(low.astype(jnp.float32), scales_ref[:scale_half], NT, lax.Precision.HIGHEST)
    scale += dot(high.astype(jnp.float32), scales_ref[scale_half:], NT, lax.Precision.HIGHEST)
    weight = jnp.sum(jnp.where(low | high, weights_ref[...], 0.0), axis=1, keepdims=True)
    for b in range(scale_half):
        part = slice(b * 128, (b + 1) * 128)
        block_ref[:, part] = (placed[:, part] * scale[:, b : b + 1] * weight).astype(jnp.bfloat16)


def fetch(sources, targets, sems, first=0):
    copies = [
        pltpu.make_async_copy(source, target, sems.at[first + i])
        for i, (source, target) in enumerate(zip(sources, targets))
    ]
    for copy in copies:
        copy.start()
    return copies


def pack_kernel(most, order, *refs):
    given, partial_ref, refs = refs[:4], refs[4], refs[5:]
    blocks, (place_ref, share_ref), refs = refs[: len(order)], refs[len(order) :][:2], refs[-6:]
    held, sems, share_sems = refs[:4], refs[4], refs[5]
    lane, count = lax.axis_index("tp"), partial_ref.shape[0]
    copies = fetch(given, held, sems)
    shares = fetch(
        [partial_ref.at[lane ^ j] for j in range(count)],
        [share_ref.at[j] for j in range(count)],
        share_sems,
    )
    copies[0].wait()
    ids_ref, weights_ref, scales_ref, grad_ref = held
    tokens, rows = grad_ref.shape[0], blocks[0].shape[0]
    me = lax.axis_index("ep")
    ids = ids_ref[...]
    expert = lax.broadcasted_iota(jnp.int32, (max(8, len(order)), tokens), 0)
    named = expert == ids
    before = lax.broadcasted_iota(jnp.int32, (tokens, tokens), 0) < lax.broadcasted_iota(
        jnp.int32, (tokens, tokens), 1
    )
    earlier = jnp.dot(
        named.astype(jnp.bfloat16), before.astype(jnp.bfloat16), preferred_element_type=jnp.float32
    )
    position = jnp.sum(jnp.where(named, earlier, 0.0), axis=0, keepdims=True).astype(jnp.int32)
    row = lax.broadcasted_iota(jnp.int32, (rows, tokens), 0)
    found = []
    for k in order:
        local = jnp.where(ids == (me ^ k), position, -2 * rows)
        low, high = row == local, row - most == local
        found.append((low, high))
        place_ref[0, k] = low.astype(jnp.bfloat16)
        place_ref[1, k] = high.astype(jnp.bfloat16)
    for copy in copies[1:]:
        copy.wait()
    for block_ref, (low, high) in zip(blocks, found):
        fill(block_ref, most, low, high, weights_ref, scales_ref, grad_ref)
    for copy in shares:
        copy.wait()


def fetch_kernel(*refs):
    count = len(refs) // 2
    for copy in fetch(refs[:count], refs[count : 2 * count], refs[-1]):
        copy.wait()


def hidden_kernel(most, extra, *refs):
    blocks, (down_ref, sum_ref, sent_ref) = refs[:-3], refs[-3:]
    half = down_ref.shape[1] // 2
    count = sum_ref.shape[0]
    if extra:
        blocks, row_sums = blocks[:-1], blocks[-1][...]
        high = row_sums.astype(jnp.bfloat16).astype(jnp.float32)
        spare = jnp.zeros((EXTRA - 4, row_sums.shape[1]), jnp.float32)
        tail = jnp.concatenate([high, row_sums - high, spare], axis=0)
        sent_ref[count:, :] = jnp.zeros((EXTRA, sent_ref.shape[1]), jnp.bfloat16)
        sent_ref[count:, : row_sums.shape[1]] = tail.astype(jnp.bfloat16)
    values = [b[...].astype(jnp.float32) for b in blocks]
    low = jnp.concatenate([v[:most] for v in values], axis=0).astype(jnp.bfloat16)
    high = jnp.concatenate([v[most : 2 * most] for v in values], axis=0).astype(jnp.bfloat16)
    total = dot(low, down_ref[:, :half], NT) + dot(high, down_ref[:, half:], NT)
    sum_ref[...] = total
    sent_ref[:count, :] = total.astype(jnp.bfloat16)


def by_xor(value, most, narrow, lane):
    step = 1
    while step < narrow:
        pieces = [value[i * most : (i + step) * most] for i in range(0, narrow, step)]
        turned = [pieces[i ^ 1] for i in range(len(pieces))]
        value = jnp.where((lane & step) != 0, jnp.concatenate(turned, axis=0), value)
        step *= 2
    return value


def back_kernel(most, narrow, group, sum_ref, other_ref, pre_ref, gate_ref, up_ref, *outs):
    half = gate_ref.shape[0] // 2
    me, lane = lax.axis_index("ep"), lax.axis_index("tp")
    hidden = sum_ref[...] + other_ref[: sum_ref.shape[0], :].astype(jnp.float32)
    gate_pre, up_pre = [
        jnp.concatenate(
            [by_xor(pre_ref[i, me ^ k].astype(jnp.float32), most, narrow, lane) for k in group],
            axis=0,
        )
        for i in range(2)
    ]
    sig = 1.0 / (1.0 + jnp.exp(-gate_pre))
    up_grad = (hidden * gate_pre * sig).astype(jnp.bfloat16)
    gate_grad = (hidden * up_pre * sig * (1.0 + gate_pre * (1.0 - sig))).astype(jnp.bfloat16)
    low = dot(gate_grad, gate_ref[:half], NT) + dot(up_grad, up_ref[:half], NT)
    high = dot(gate_grad, gate_ref[half:], NT) + dot(up_grad, up_ref[half:], NT)
    for i, out in enumerate(outs):
        part = slice(i * most, (i + 1) * most)
        pieces = [low[part], high[part]]
        spare = out.shape[0] - 2 * most
        if spare:
            pieces.append(jnp.zeros((spare, half), jnp.float32))
        out[...] = jnp.concatenate(pieces, axis=0).astype(jnp.bfloat16)


def unpack_kernel(parts, started, place_ref, *refs):
    given, out_ref = list(refs[:-1]), refs[-1]
    half = out_ref.shape[1] // 2
    blocks = {}
    for k, count in parts.items():
        rows = given.pop(0)[...].astype(jnp.float32)
        for _ in range(count - 1):
            rows += given.pop(0)[...].astype(jnp.float32)
        blocks[k] = rows.astype(jnp.bfloat16)
    for side in range(2):
        columns = slice(side * half, (side + 1) * half)
        total = given[0][:, columns].astype(jnp.float32) if started else 0.0
        for k, rows in blocks.items():
            total = total + dot(place_ref[side, k], rows, TN)
        out_ref[:, columns] = total.astype(jnp.bfloat16)


def groups_of(wide):
    if wide < 4:
        return [list(range(wide - 1, -1, -1))]
    left = list(range(wide - 2, 1, -1))
    return [[wide - 1, 1, 0]] + [left[i : i + 2] for i in range(0, len(left), 2)]


def local(
    grad_values,
    grad_scales,
    expert_ids,
    route_weights,
    w_gate,
    w_up,
    w_down,
    pre_acts,
    latent_partials,
    latent,
    latent_gain,
):
    wide, narrow = lax.axis_size("ep"), lax.axis_size("tp")
    tokens, width = grad_values.shape
    half = width // 2
    slots, hidden_width = pre_acts.shape[2:]
    most = slots // (wide * narrow)
    rows = -(-2 * most // 8) * 8
    f32, bf16 = jnp.float32, jnp.bfloat16
    block = pltpu.VMEM((rows, half), bf16)
    groups = groups_of(wide)
    order = [k for group in groups for k in group]
    partials = latent_partials.reshape(narrow, tokens, latent.shape[1])
    packed = call(
        functools.partial(pack_kernel, most, order),
        [block] * wide + [pltpu.VMEM((2, wide, rows, tokens), bf16), like(partials)],
        *pinned(
            expert_ids.reshape(1, tokens),
            route_weights.reshape(1, tokens),
            grad_scales.T,
            grad_values,
            partials,
        ),
        specs=[HBM] * 5,
        scratch=[
            pltpu.VMEM((1, tokens), jnp.int32),
            pltpu.VMEM((1, tokens), f32),
            pltpu.VMEM((grad_scales.shape[1], tokens), f32),
            pltpu.VMEM((tokens, width), bf16),
            pltpu.SemaphoreType.DMA((4,)),
            pltpu.SemaphoreType.DMA((narrow,)),
        ],
        name="pack",
    )
    place, shares = packed[wide:]
    packed = dict(zip(order, packed))

    first, staged = groups[0][0], len(groups) > 1
    taken = {0: [packed[0]] + [swap(packed[0], "rows0", tp=j) for j in range(1, narrow)]}
    arrived = {}
    for k in order:
        if k:
            given = packed[k] if k in groups[0] else after(packed[k], arrived[first])
            arrived[k] = swap(given, f"rows{k}", ep=k)
            if staged and k == groups[1][0]:
                arrived[k] = after(arrived[k], packed[first], 1 << 31)
    fetched = [
        w_down[0],
        pre_acts.reshape(2, wide, narrow * most, hidden_width),
        w_gate[0],
        w_up[0],
        latent,
        latent_gain.reshape(1, -1),
    ]
    down, pre, gate, up, latent, latent_gain = call(
        fetch_kernel,
        [like(array) for array in fetched],
        *pinned(*fetched),
        specs=[HBM] * len(fetched),
        scratch=[pltpu.SemaphoreType.DMA((len(fetched),))],
        earlier=[arrived[first]],
        name="fetch",
    )
    latent_parts = [shares[0]] + [
        swap(shares[j], "latent", tp=j) for j in range(1, narrow)
    ]

    def straight(k, mine, others):
        return [swap(mine, f"back{k}", ep=k)] + [
            swap(other, f"back{k}", ep=k, tp=j + 1) for j, other in enumerate(others)
        ]

    returned, waiting = {}, []
    values = latent.astype(f32)
    received, products, moved = None, None, None
    for group in groups:
        for k in group:
            if staged and k == 1:
                crossing = [swap(packed[k], f"rows{k}", ep=k, tp=j) for j in range(1, narrow)]
            elif k:
                if products:
                    arrived[k] = after(arrived[k], summed)
                crossing = [swap(arrived[k], f"rows{k}", tp=j) for j in range(1, narrow)]
                if products:
                    crossing[-1] = after(crossing[-1], products[0])
            if k:
                taken[k] = [arrived[k]] + crossing
        count = len(group) * narrow * most
        extra = group is groups[-1]
        if extra:
            if received is not None:
                latent_parts[-1] = after(latent_parts[-1], summed, 1 << 30)
            own_grad = sum(part.astype(f32) for part in latent_parts)
            gained = own_grad * latent_gain
            row_sums = jnp.stack(
                [jnp.sum(values * values, axis=1), jnp.sum(gained * values, axis=1)]
            )
        summed, sent = call(
            functools.partial(hidden_kernel, most, extra),
            [
                pltpu.VMEM((count, hidden_width), f32),
                pltpu.VMEM((count + (EXTRA if extra else 0), hidden_width), bf16),
            ],
            *[rows_of_k for k in group for rows_of_k in taken[k]],
            *([row_sums] if extra else []),
            down,
            name="hidden",
            earlier=products[:1] if products else (),
        )
        received = swap(sent, f"hidden{group[0]}", sub=1)
        if moved is not None:
            received = after(received, moved)
        products = call(
            functools.partial(back_kernel, most, narrow, group),
            [block] * (len(group) * narrow),
            summed,
            received,
            pre,
            gate,
            up,
            name="back",
        )
        for at, k in enumerate(group):
            mine, others = products[at * narrow], products[at * narrow + 1 : (at + 1) * narrow]
            if k == 0:
                kept = mine, others
            elif staged and k == 1:
                waiting.append((k, mine, others))
            else:
                total = mine.astype(f32)
                for j, other in enumerate(others):
                    total += swap(other, f"back{k}", tp=j + 1).astype(f32)
                total = total.astype(bf16)
                returned[k] = [swap(total, f"back{k}", ep=k)]
                if k == group[0]:
                    moved = total
    for k, mine, others in waiting:
        returned[k] = straight(k, after(mine, products[0]), [after(other, products[0]) for other in others])
    mine, others = kept
    returned[0] = [mine] + [
        swap(after(other, moved) if staged else other, "back0", tp=j + 1)
        for j, other in enumerate(others)
    ]
    tail = received[count : count + 4, :tokens].astype(f32)
    row_sums = row_sums + tail[:2] + tail[2:]
    inverse_rms = lax.rsqrt(row_sums[0] / LAT + 1e-06)[:, None]
    d_latent = (
        inverse_rms * gained - values * inverse_rms**3 * row_sums[1][:, None] / LAT
    ).astype(bf16)
    latest = groups[-1][:1] if staged else []
    distances = [k for k in order if k not in latest]
    (grad_input,) = call(
        functools.partial(unpack_kernel, {k: len(returned[k]) for k in distances}, False),
        [pltpu.VMEM((tokens, width), bf16) if staged else jax.ShapeDtypeStruct((tokens, width), bf16)],
        place,
        *[part for k in distances for part in returned[k]],
        name="unpack",
    )
    if staged:
        (grad_input,) = call(
            functools.partial(unpack_kernel, {k: len(returned[k]) for k in latest}, True),
            [jax.ShapeDtypeStruct((tokens, width), bf16)],
            place,
            *[part for k in latest for part in returned[k]],
            grad_input,
            name="unpack_latest",
        )
    return (grad_input, d_latent)


def solution(mesh):
    placed = (
        P(("rep", "ep", "tp"), "sub"),
        P(("rep", "ep", "tp"), "sub"),
        P(("rep", "ep", "tp"), None),
        P(("rep", "ep", "tp"), None),
        P("ep", "sub", "tp"),
        P("ep", "sub", "tp"),
        P("ep", "tp", "sub"),
        P(("rep", "ep"), None, None, "tp"),
        P("tp", ("rep", "ep"), "sub"),
        P(("rep", "ep", "tp"), "sub"),
        P("sub"),
    )
    return jax.shard_map(
        local,
        mesh=mesh,
        in_specs=placed,
        out_specs=(P(("rep", "ep", "tp"), "sub"), P(("rep", "ep", "tp"), "sub")),
        check_vma=False,
    )
```

```python
import functools

import jax
import jax.numpy as jnp
import numpy as np
from jax import lax
from jax.experimental import pallas as pl
from jax.experimental.pallas import tpu as pltpu
from jax.sharding import PartitionSpec as P

LAT = 512
NT = (((1,), (1,)), ((), ()))
TN = (((0,), (0,)), ((), ()))
VMEM = pl.BlockSpec(memory_space=pltpu.VMEM)
ANY = pl.BlockSpec(memory_space=pl.ANY)
HBM = pl.BlockSpec(memory_space=pltpu.HBM)
EXTRA = 16
VMEM_LIMIT = 20 * 1024 * 1024


def dot(a, b, dims, precision=None):
    return lax.dot_general(a, b, dims, precision=precision, preferred_element_type=jnp.float32)


def swap(value, what, **steps):
    counts = [lax.axis_size(axis) for axis in steps]
    pairs = []
    for place in np.ndindex(*counts):
        other = [index ^ step for index, step in zip(place, steps.values())]
        pairs.append(tuple(int(np.ravel_multi_index(p, counts)) for p in (place, other)))
    with jax.named_scope("_".join([what, *steps])):
        return lax.ppermute(value, tuple(steps), pairs)


def pinned(*arrays):
    return [pltpu.with_memory_space_constraint(array, pltpu.HBM) for array in arrays]


def like(array):
    return pltpu.VMEM(array.shape, array.dtype)


def call(kernel, outs, *args, cost=0, name=None, specs=None, scratch=(), earlier=()):
    specs = (specs or [VMEM] * len(args)) + [ANY] * len(earlier)
    if earlier:
        taken, body = len(args), kernel

        def kernel(*refs):
            body(*refs[:taken], *refs[taken + len(earlier) :])

    return pl.pallas_call(
        kernel,
        out_shape=outs,
        in_specs=specs,
        out_specs=[VMEM] * len(outs),
        scratch_shapes=scratch,
        compiler_params=pltpu.CompilerParams(vmem_limit_bytes=VMEM_LIMIT),
        cost_estimate=pl.CostEstimate(flops=cost, bytes_accessed=0, transcendentals=0),
        name=name,
    )(*args, *earlier)


def after(value, earlier, cost=0):
    return pl.pallas_call(
        lambda value_ref, earlier_ref, out_ref: None,
        out_shape=jax.ShapeDtypeStruct(value.shape, value.dtype),
        in_specs=[ANY, ANY],
        out_specs=ANY,
        input_output_aliases={0: 0},
        compiler_params=pltpu.CompilerParams(vmem_limit_bytes=1 << 17),
        cost_estimate=pl.CostEstimate(flops=cost, bytes_accessed=0, transcendentals=0),
        name="after",
    )(value, earlier)


def fill(block_ref, most, low, high, weights_ref, scales_ref, grad_ref):
    half, scale_half = grad_ref.shape[1] // 2, scales_ref.shape[0] // 2
    placed = jnp.dot(
        low.astype(jnp.bfloat16), grad_ref[:, :half], preferred_element_type=jnp.float32
    )
    placed += jnp.dot(
        high.astype(jnp.bfloat16), grad_ref[:, half:], preferred_element_type=jnp.float32
    )
    scale = dot(low.astype(jnp.float32), scales_ref[:scale_half], NT, lax.Precision.HIGHEST)
    scale += dot(high.astype(jnp.float32), scales_ref[scale_half:], NT, lax.Precision.HIGHEST)
    weight = jnp.sum(jnp.where(low | high, weights_ref[...], 0.0), axis=1, keepdims=True)
    for b in range(scale_half):
        part = slice(b * 128, (b + 1) * 128)
        block_ref[:, part] = (placed[:, part] * scale[:, b : b + 1] * weight).astype(jnp.bfloat16)


def fetch(sources, targets, sems, first=0):
    copies = [
        pltpu.make_async_copy(source, target, sems.at[first + i])
        for i, (source, target) in enumerate(zip(sources, targets))
    ]
    for copy in copies:
        copy.start()
    return copies


def pack_kernel(most, order, leading, *refs):
    given, refs = refs[:4], refs[4:]
    blocks, (place_ref, *held), (ids_ref, sems) = refs[:leading], refs[leading:-2], refs[-2:]
    held = [ids_ref] + held
    copies = fetch(given, held, sems)
    copies[0].wait()
    weights_ref, scales_ref, grad_ref = held[1:]
    tokens, rows = grad_ref.shape[0], blocks[0].shape[0]
    me = lax.axis_index("ep")
    ids = ids_ref[...]
    expert = lax.broadcasted_iota(jnp.int32, (max(8, len(order)), tokens), 0)
    named = expert == ids
    before = lax.broadcasted_iota(jnp.int32, (tokens, tokens), 0) < lax.broadcasted_iota(
        jnp.int32, (tokens, tokens), 1
    )
    earlier = jnp.dot(
        named.astype(jnp.bfloat16), before.astype(jnp.bfloat16), preferred_element_type=jnp.float32
    )
    position = jnp.sum(jnp.where(named, earlier, 0.0), axis=0, keepdims=True).astype(jnp.int32)
    row = lax.broadcasted_iota(jnp.int32, (rows, tokens), 0)
    found = []
    for k in order:
        local = jnp.where(ids == (me ^ k), position, -2 * rows)
        low, high = row == local, row - most == local
        found.append((low, high))
        place_ref[0, k] = low.astype(jnp.bfloat16)
        place_ref[1, k] = high.astype(jnp.bfloat16)
    for copy in copies[1:]:
        copy.wait()
    for block_ref, (low, high) in zip(blocks, found):
        fill(block_ref, most, low, high, weights_ref, scales_ref, grad_ref)


def pack_more_kernel(most, order, place_ref, weights_ref, scales_ref, grad_ref, partial_ref, *refs):
    blocks, (share_ref, sems) = refs[:-2], refs[-2:]
    lane, count = lax.axis_index("tp"), partial_ref.shape[0]
    shares = fetch(
        [partial_ref.at[lane ^ j] for j in range(count)],
        [share_ref.at[j] for j in range(count)],
        sems,
    )
    for block_ref, k in zip(blocks, order):
        low, high = place_ref[0, k] != 0, place_ref[1, k] != 0
        fill(block_ref, most, low, high, weights_ref, scales_ref, grad_ref)
    for copy in shares:
        copy.wait()


def by_xor(value, most, narrow, lane):
    step = 1
    while step < narrow:
        pieces = [value[i * most : (i + step) * most] for i in range(0, narrow, step)]
        turned = [pieces[i ^ 1] for i in range(len(pieces))]
        value = jnp.where((lane & step) != 0, jnp.concatenate(turned, axis=0), value)
        step *= 2
    return value


def fetch_kernel(most, *refs):
    pre_ref, sems = refs[-2:]
    wide = pre_ref.shape[1]
    narrow = pre_ref.shape[2] // most
    count = (len(refs) - 3) // 2
    given, (up_ref, gate_ref, *held) = refs[:count], refs[count:-2]
    copies = fetch(given, [pre_ref] + held, sems)
    me, lane = lax.axis_index("ep"), lax.axis_index("tp")
    copies[0].wait()
    for k in range(wide):
        gate_pre, up_pre = [
            by_xor(pre_ref[i, me ^ k].astype(jnp.float32), most, narrow, lane) for i in range(2)
        ]
        sig = 1.0 / (1.0 + jnp.exp(-gate_pre))
        up_ref[k] = gate_pre * sig
        gate_ref[k] = up_pre * sig * (1.0 + gate_pre * (1.0 - sig))
    for copy in copies[1:]:
        copy.wait()


def hidden_kernel(most, extra, *refs):
    blocks, (down_ref, sum_ref, sent_ref) = refs[:-3], refs[-3:]
    half = down_ref.shape[1] // 2
    count = sum_ref.shape[0]
    if extra:
        blocks, row_sums = blocks[:-1], blocks[-1][...]
        high = row_sums.astype(jnp.bfloat16).astype(jnp.float32)
        spare = jnp.zeros((EXTRA - 4, row_sums.shape[1]), jnp.float32)
        tail = jnp.concatenate([high, row_sums - high, spare], axis=0)
        sent_ref[count:, :] = jnp.zeros((EXTRA, sent_ref.shape[1]), jnp.bfloat16)
        sent_ref[count:, : row_sums.shape[1]] = tail.astype(jnp.bfloat16)
    values = [b[...].astype(jnp.float32) for b in blocks]
    low = jnp.concatenate([v[:most] for v in values], axis=0).astype(jnp.bfloat16)
    high = jnp.concatenate([v[most : 2 * most] for v in values], axis=0).astype(jnp.bfloat16)
    total = dot(low, down_ref[:, :half], NT) + dot(high, down_ref[:, half:], NT)
    sum_ref[...] = total
    sent_ref[:count, :] = total.astype(jnp.bfloat16)


def back_kernel(most, group, sum_ref, other_ref, up_by_ref, gate_by_ref, gate_ref, up_ref, *outs):
    half = gate_ref.shape[0] // 2
    hidden = sum_ref[...] + other_ref[: sum_ref.shape[0], :].astype(jnp.float32)
    up_by, gate_by = [
        jnp.concatenate([by_ref[k] for k in group], axis=0) for by_ref in (up_by_ref, gate_by_ref)
    ]
    up_grad = (hidden * up_by).astype(jnp.bfloat16)
    gate_grad = (hidden * gate_by).astype(jnp.bfloat16)
    low = dot(gate_grad, gate_ref[:half], NT) + dot(up_grad, up_ref[:half], NT)
    high = dot(gate_grad, gate_ref[half:], NT) + dot(up_grad, up_ref[half:], NT)
    for i, out in enumerate(outs):
        part = slice(i * most, (i + 1) * most)
        pieces = [low[part], high[part]]
        spare = out.shape[0] - 2 * most
        if spare:
            pieces.append(jnp.zeros((spare, half), jnp.float32))
        out[...] = jnp.concatenate(pieces, axis=0).astype(jnp.bfloat16)


def unpack_kernel(parts, started, place_ref, *refs):
    given, out_ref = list(refs[:-1]), refs[-1]
    half = out_ref.shape[1] // 2
    blocks = {}
    for k, count in parts.items():
        rows = given.pop(0)[...].astype(jnp.float32)
        for _ in range(count - 1):
            rows += given.pop(0)[...].astype(jnp.float32)
        blocks[k] = rows.astype(jnp.bfloat16)
    for side in range(2):
        columns = slice(side * half, (side + 1) * half)
        total = given[0][:, columns].astype(jnp.float32) if started else 0.0
        for k, rows in blocks.items():
            total = total + dot(place_ref[side, k], rows, TN)
        out_ref[:, columns] = total.astype(jnp.bfloat16)


def groups_of(wide):
    if wide < 4:
        return [list(range(wide - 1, -1, -1))]
    left = list(range(wide - 2, 1, -1))
    return [[wide - 1, 1, 0]] + [left[i : i + 2] for i in range(0, len(left), 2)]


def local(
    grad_values,
    grad_scales,
    expert_ids,
    route_weights,
    w_gate,
    w_up,
    w_down,
    pre_acts,
    latent_partials,
    latent,
    latent_gain,
):
    wide, narrow = lax.axis_size("ep"), lax.axis_size("tp")
    tokens, width = grad_values.shape
    half = width // 2
    slots, hidden_width = pre_acts.shape[2:]
    most = slots // (wide * narrow)
    rows = -(-2 * most // 8) * 8
    f32, bf16 = jnp.float32, jnp.bfloat16
    block = pltpu.VMEM((rows, half), bf16)
    groups = groups_of(wide)
    order = [k for group in groups for k in group]
    partials = latent_partials.reshape(narrow, tokens, latent.shape[1])
    leading, place, *fillers = call(
        functools.partial(pack_kernel, most, order, 1),
        [
            block,
            pltpu.VMEM((2, wide, rows, tokens), bf16),
            pltpu.VMEM((1, tokens), f32),
            pltpu.VMEM((grad_scales.shape[1], tokens), f32),
            pltpu.VMEM((tokens, width), bf16),
        ],
        *pinned(
            expert_ids.reshape(1, tokens),
            route_weights.reshape(1, tokens),
            grad_scales.T,
            grad_values,
        ),
        specs=[HBM] * 4,
        scratch=[pltpu.VMEM((1, tokens), jnp.int32), pltpu.SemaphoreType.DMA((4,))],
        name="pack",
    )
    *packed, shares = call(
        functools.partial(pack_more_kernel, most, order[1:]),
        [block] * (wide - 1) + [like(partials)],
        place,
        *fillers,
        *pinned(partials),
        specs=[VMEM] * 4 + [HBM],
        scratch=[pltpu.SemaphoreType.DMA((narrow,))],
        name="pack_more",
    )
    packed = dict(zip(order, [leading] + packed))

    first, staged = groups[0][0], len(groups) > 1
    taken = {0: [packed[0]] + [swap(packed[0], "rows0", tp=j) for j in range(1, narrow)]}
    arrived = {}
    for k in order:
        if k:
            given = packed[k] if k in groups[0] else after(packed[k], arrived[first])
            arrived[k] = swap(given, f"rows{k}", ep=k)
            if staged and k == groups[1][0]:
                arrived[k] = after(arrived[k], packed[first], 1 << 31)
    fetched = [
        pre_acts.reshape(2, wide, narrow * most, hidden_width),
        w_down[0],
        w_gate[0],
        w_up[0],
        latent,
        latent_gain.reshape(1, -1),
    ]
    factors = pltpu.VMEM((wide, narrow * most, hidden_width), f32)
    up_by, gate_by, down, gate, up, latent, latent_gain = call(
        functools.partial(fetch_kernel, most),
        [factors, factors] + [like(array) for array in fetched[1:]],
        *pinned(*fetched),
        specs=[HBM] * len(fetched),
        scratch=[like(fetched[0]), pltpu.SemaphoreType.DMA((len(fetched),))],
        earlier=[arrived[first]],
        name="fetch",
    )
    latent_parts = [shares[0]] + [
        swap(shares[j], "latent", tp=j) for j in range(1, narrow)
    ]

    def straight(k, mine, others):
        return [swap(mine, f"back{k}", ep=k)] + [
            swap(other, f"back{k}", ep=k, tp=j + 1) for j, other in enumerate(others)
        ]

    returned, waiting = {}, []
    values = latent.astype(f32)
    received, products, moved = None, None, None
    for group in groups:
        for k in group:
            if staged and k == 1:
                crossing = [swap(packed[k], f"rows{k}", ep=k, tp=j) for j in range(1, narrow)]
            elif k:
                if products:
                    arrived[k] = after(arrived[k], summed)
                crossing = [swap(arrived[k], f"rows{k}", tp=j) for j in range(1, narrow)]
                if products:
                    crossing[-1] = after(crossing[-1], products[0])
            if k:
                taken[k] = [arrived[k]] + crossing
        count = len(group) * narrow * most
        extra = group is groups[-1]
        if extra:
            if received is not None:
                latent_parts[-1] = after(latent_parts[-1], summed, 1 << 30)
            own_grad = sum(part.astype(f32) for part in latent_parts)
            gained = own_grad * latent_gain
            row_sums = jnp.stack(
                [jnp.sum(values * values, axis=1), jnp.sum(gained * values, axis=1)]
            )
        summed, sent = call(
            functools.partial(hidden_kernel, most, extra),
            [
                pltpu.VMEM((count, hidden_width), f32),
                pltpu.VMEM((count + (EXTRA if extra else 0), hidden_width), bf16),
            ],
            *[rows_of_k for k in group for rows_of_k in taken[k]],
            *([row_sums] if extra else []),
            down,
            name="hidden",
            earlier=products[:1] if products else (),
        )
        received = swap(sent, f"hidden{group[0]}", sub=1)
        if moved is not None:
            received = after(received, moved)
        products = call(
            functools.partial(back_kernel, most, group),
            [block] * (len(group) * narrow),
            summed,
            received,
            up_by,
            gate_by,
            gate,
            up,
            name="back",
        )
        for at, k in enumerate(group):
            mine, others = products[at * narrow], products[at * narrow + 1 : (at + 1) * narrow]
            if k == 0:
                kept = mine, others
            elif staged and k == 1:
                waiting.append((k, mine, others))
            else:
                total = mine.astype(f32)
                for j, other in enumerate(others):
                    total += swap(other, f"back{k}", tp=j + 1).astype(f32)
                total = total.astype(bf16)
                returned[k] = [swap(total, f"back{k}", ep=k)]
                if k == group[0]:
                    moved = total
    for k, mine, others in waiting:
        returned[k] = straight(k, after(mine, products[0]), [after(other, products[0]) for other in others])
    mine, others = kept
    returned[0] = [mine] + [
        swap(after(other, moved) if staged else other, "back0", tp=j + 1)
        for j, other in enumerate(others)
    ]
    tail = received[count : count + 4, :tokens].astype(f32)
    row_sums = row_sums + tail[:2] + tail[2:]
    inverse_rms = lax.rsqrt(row_sums[0] / LAT + 1e-06)[:, None]
    d_latent = (
        inverse_rms * gained - values * inverse_rms**3 * row_sums[1][:, None] / LAT
    ).astype(bf16)
    latest = groups[-1][:1] if staged else []
    distances = [k for k in order if k not in latest]
    (grad_input,) = call(
        functools.partial(unpack_kernel, {k: len(returned[k]) for k in distances}, False),
        [pltpu.VMEM((tokens, width), bf16) if staged else jax.ShapeDtypeStruct((tokens, width), bf16)],
        place,
        *[part for k in distances for part in returned[k]],
        name="unpack",
    )
    if staged:
        (grad_input,) = call(
            functools.partial(unpack_kernel, {k: len(returned[k]) for k in latest}, True),
            [jax.ShapeDtypeStruct((tokens, width), bf16)],
            place,
            *[part for k in latest for part in returned[k]],
            grad_input,
            name="unpack_latest",
        )
    return (grad_input, d_latent)


def solution(mesh):
    placed = (
        P(("rep", "ep", "tp"), "sub"),
        P(("rep", "ep", "tp"), "sub"),
        P(("rep", "ep", "tp"), None),
        P(("rep", "ep", "tp"), None),
        P("ep", "sub", "tp"),
        P("ep", "sub", "tp"),
        P("ep", "tp", "sub"),
        P(("rep", "ep"), None, None, "tp"),
        P("tp", ("rep", "ep"), "sub"),
        P(("rep", "ep", "tp"), "sub"),
        P("sub"),
    )
    return jax.shard_map(
        local,
        mesh=mesh,
        in_specs=placed,
        out_specs=(P(("rep", "ep", "tp"), "sub"), P(("rep", "ep", "tp"), "sub")),
        check_vma=False,
    )
```

```python
import functools

import jax
import jax.numpy as jnp
import numpy as np
from jax import lax
from jax.experimental import pallas as pl
from jax.experimental.pallas import tpu as pltpu
from jax.sharding import PartitionSpec as P

LAT = 512
NT = (((1,), (1,)), ((), ()))
TN = (((0,), (0,)), ((), ()))
VMEM = pl.BlockSpec(memory_space=pltpu.VMEM)
ANY = pl.BlockSpec(memory_space=pl.ANY)
HBM = pl.BlockSpec(memory_space=pltpu.HBM)
EXTRA = 16
VMEM_LIMIT = 20 * 1024 * 1024


def dot(a, b, dims, precision=None):
    return lax.dot_general(a, b, dims, precision=precision, preferred_element_type=jnp.float32)


def swap(value, what, **steps):
    counts = [lax.axis_size(axis) for axis in steps]
    pairs = []
    for place in np.ndindex(*counts):
        other = [index ^ step for index, step in zip(place, steps.values())]
        pairs.append(tuple(int(np.ravel_multi_index(p, counts)) for p in (place, other)))
    with jax.named_scope("_".join([what, *steps])):
        return lax.ppermute(value, tuple(steps), pairs)


def pinned(*arrays):
    return [pltpu.with_memory_space_constraint(array, pltpu.HBM) for array in arrays]


def like(array):
    return pltpu.VMEM(array.shape, array.dtype)


def call(kernel, outs, *args, cost=0, name=None, specs=None, scratch=(), earlier=()):
    specs = (specs or [VMEM] * len(args)) + [ANY] * len(earlier)
    if earlier:
        taken, body = len(args), kernel

        def kernel(*refs):
            body(*refs[:taken], *refs[taken + len(earlier) :])

    return pl.pallas_call(
        kernel,
        out_shape=outs,
        in_specs=specs,
        out_specs=[VMEM] * len(outs),
        scratch_shapes=scratch,
        compiler_params=pltpu.CompilerParams(vmem_limit_bytes=VMEM_LIMIT),
        cost_estimate=pl.CostEstimate(flops=cost, bytes_accessed=0, transcendentals=0),
        name=name,
    )(*args, *earlier)


def after(value, earlier, cost=0):
    return pl.pallas_call(
        lambda value_ref, earlier_ref, out_ref: None,
        out_shape=jax.ShapeDtypeStruct(value.shape, value.dtype),
        in_specs=[ANY, ANY],
        out_specs=ANY,
        input_output_aliases={0: 0},
        compiler_params=pltpu.CompilerParams(vmem_limit_bytes=1 << 17),
        cost_estimate=pl.CostEstimate(flops=cost, bytes_accessed=0, transcendentals=0),
        name="after",
    )(value, earlier)


def fill(block_ref, most, low, high, weights_ref, scales_ref, grad_ref):
    half, scale_half = grad_ref.shape[1] // 2, scales_ref.shape[0] // 2
    placed = jnp.dot(
        low.astype(jnp.bfloat16), grad_ref[:, :half], preferred_element_type=jnp.float32
    )
    placed += jnp.dot(
        high.astype(jnp.bfloat16), grad_ref[:, half:], preferred_element_type=jnp.float32
    )
    scale = dot(low.astype(jnp.float32), scales_ref[:scale_half], NT, lax.Precision.HIGHEST)
    scale += dot(high.astype(jnp.float32), scales_ref[scale_half:], NT, lax.Precision.HIGHEST)
    weight = jnp.sum(jnp.where(low | high, weights_ref[...], 0.0), axis=1, keepdims=True)
    for b in range(scale_half):
        part = slice(b * 128, (b + 1) * 128)
        block_ref[:, part] = (placed[:, part] * scale[:, b : b + 1] * weight).astype(jnp.bfloat16)


def fetch(sources, targets, sems, first=0):
    copies = [
        pltpu.make_async_copy(source, target, sems.at[first + i])
        for i, (source, target) in enumerate(zip(sources, targets))
    ]
    for copy in copies:
        copy.start()
    return copies


def pack_kernel(most, order, leading, *refs):
    given, refs = refs[:4], refs[4:]
    blocks, (place_ref, *held), (ids_ref, sems) = refs[:leading], refs[leading:-2], refs[-2:]
    held = [ids_ref] + held
    copies = fetch(given, held, sems)
    copies[0].wait()
    weights_ref, scales_ref, grad_ref = held[1:]
    tokens, rows = grad_ref.shape[0], blocks[0].shape[0]
    me = lax.axis_index("ep")
    ids = ids_ref[...]
    expert = lax.broadcasted_iota(jnp.int32, (max(8, len(order)), tokens), 0)
    named = expert == ids
    before = lax.broadcasted_iota(jnp.int32, (tokens, tokens), 0) < lax.broadcasted_iota(
        jnp.int32, (tokens, tokens), 1
    )
    earlier = jnp.dot(
        named.astype(jnp.bfloat16), before.astype(jnp.bfloat16), preferred_element_type=jnp.float32
    )
    position = jnp.sum(jnp.where(named, earlier, 0.0), axis=0, keepdims=True).astype(jnp.int32)
    row = lax.broadcasted_iota(jnp.int32, (rows, tokens), 0)
    found = []
    for k in order:
        local = jnp.where(ids == (me ^ k), position, -2 * rows)
        low, high = row == local, row - most == local
        found.append((low, high))
        place_ref[0, k] = low.astype(jnp.bfloat16)
        place_ref[1, k] = high.astype(jnp.bfloat16)
    for copy in copies[1:]:
        copy.wait()
    for block_ref, (low, high) in zip(blocks, found):
        fill(block_ref, most, low, high, weights_ref, scales_ref, grad_ref)


def shares_of(tokens, columns, width):
    across = width // columns
    deep = -(-tokens // across // 16) * 16
    return deep, [(at, i * columns) for i, at in enumerate(range(0, tokens, deep))]


def pack_more_kernel(most, order, place_ref, weights_ref, scales_ref, grad_ref, partial_ref, *refs):
    count, tokens, columns = partial_ref.shape
    blocks, crossing = refs[: len(order)], refs[len(order) : len(order) + count - 1]
    own_ref, sems = refs[-2:]
    lane, rows = lax.axis_index("tp"), blocks[0].shape[0]
    deep, parts = shares_of(tokens, columns, blocks[0].shape[1])
    sources, targets = [partial_ref.at[lane]], [own_ref]
    for j in range(1, count):
        for at, column in parts:
            size = min(deep, tokens - at)
            sources.append(partial_ref.at[lane ^ j, pl.ds(at, size)])
            targets.append(crossing[j - 1].at[pl.ds(0, size), pl.ds(column, columns)])
    copies = fetch(sources, targets, sems)
    for block_ref, k in zip(blocks, order):
        low, high = place_ref[0, k] != 0, place_ref[1, k] != 0
        fill(block_ref, most, low, high, weights_ref, scales_ref, grad_ref)
        if k == 0:
            for both_ref in crossing:
                both_ref[deep:, :] = block_ref[...]
    for copy in copies:
        copy.wait()


def by_xor(value, most, narrow, lane):
    step = 1
    while step < narrow:
        pieces = [value[i * most : (i + step) * most] for i in range(0, narrow, step)]
        turned = [pieces[i ^ 1] for i in range(len(pieces))]
        value = jnp.where((lane & step) != 0, jnp.concatenate(turned, axis=0), value)
        step *= 2
    return value


def fetch_kernel(most, *refs):
    pre_ref, sems = refs[-2:]
    wide = pre_ref.shape[1]
    narrow = pre_ref.shape[2] // most
    count = (len(refs) - 3) // 2
    given, (up_ref, gate_ref, *held) = refs[:count], refs[count:-2]
    copies = fetch(given, [pre_ref] + held, sems)
    me, lane = lax.axis_index("ep"), lax.axis_index("tp")
    copies[0].wait()
    for k in range(wide):
        gate_pre, up_pre = [
            by_xor(pre_ref[i, me ^ k].astype(jnp.float32), most, narrow, lane) for i in range(2)
        ]
        sig = 1.0 / (1.0 + jnp.exp(-gate_pre))
        up_ref[k] = gate_pre * sig
        gate_ref[k] = up_pre * sig * (1.0 + gate_pre * (1.0 - sig))
    for copy in copies[1:]:
        copy.wait()


def hidden_kernel(most, extra, skips, *refs):
    blocks, (down_ref, sum_ref, sent_ref) = refs[:-3], refs[-3:]
    half = down_ref.shape[1] // 2
    count = sum_ref.shape[0]
    if extra:
        blocks, row_sums = blocks[:-1], blocks[-1][...]
        high = row_sums.astype(jnp.bfloat16).astype(jnp.float32)
        spare = jnp.zeros((EXTRA - 4, row_sums.shape[1]), jnp.float32)
        tail = jnp.concatenate([high, row_sums - high, spare], axis=0)
        sent_ref[count:, :] = jnp.zeros((EXTRA, sent_ref.shape[1]), jnp.bfloat16)
        sent_ref[count:, : row_sums.shape[1]] = tail.astype(jnp.bfloat16)
    values = [b[skip:, :].astype(jnp.float32) for b, skip in zip(blocks, skips)]
    low = jnp.concatenate([v[:most] for v in values], axis=0).astype(jnp.bfloat16)
    high = jnp.concatenate([v[most : 2 * most] for v in values], axis=0).astype(jnp.bfloat16)
    total = dot(low, down_ref[:, :half], NT) + dot(high, down_ref[:, half:], NT)
    sum_ref[...] = total
    sent_ref[:count, :] = total.astype(jnp.bfloat16)


def back_kernel(most, group, sum_ref, other_ref, up_by_ref, gate_by_ref, gate_ref, up_ref, *outs):
    half = gate_ref.shape[0] // 2
    hidden = sum_ref[...] + other_ref[: sum_ref.shape[0], :].astype(jnp.float32)
    up_by, gate_by = [
        jnp.concatenate([by_ref[k] for k in group], axis=0) for by_ref in (up_by_ref, gate_by_ref)
    ]
    up_grad = (hidden * up_by).astype(jnp.bfloat16)
    gate_grad = (hidden * gate_by).astype(jnp.bfloat16)
    low = dot(gate_grad, gate_ref[:half], NT) + dot(up_grad, up_ref[:half], NT)
    high = dot(gate_grad, gate_ref[half:], NT) + dot(up_grad, up_ref[half:], NT)
    for i, out in enumerate(outs):
        part = slice(i * most, (i + 1) * most)
        pieces = [low[part], high[part]]
        spare = out.shape[0] - 2 * most
        if spare:
            pieces.append(jnp.zeros((spare, half), jnp.float32))
        out[...] = jnp.concatenate(pieces, axis=0).astype(jnp.bfloat16)


def unpack_kernel(parts, started, place_ref, *refs):
    given, out_ref = list(refs[:-1]), refs[-1]
    half = out_ref.shape[1] // 2
    blocks = {}
    for k, count in parts.items():
        rows = given.pop(0)[...].astype(jnp.float32)
        for _ in range(count - 1):
            rows += given.pop(0)[...].astype(jnp.float32)
        blocks[k] = rows.astype(jnp.bfloat16)
    for side in range(2):
        columns = slice(side * half, (side + 1) * half)
        total = given[0][:, columns].astype(jnp.float32) if started else 0.0
        for k, rows in blocks.items():
            total = total + dot(place_ref[side, k], rows, TN)
        out_ref[:, columns] = total.astype(jnp.bfloat16)


def groups_of(wide):
    left = list(range(wide - 1, -1, -1))
    if wide < 4:
        return [left]
    return [[left[0], 0]] + [left[i : min(i + 2, wide - 1)] for i in range(1, wide - 1, 2)]


def local(
    grad_values,
    grad_scales,
    expert_ids,
    route_weights,
    w_gate,
    w_up,
    w_down,
    pre_acts,
    latent_partials,
    latent,
    latent_gain,
):
    wide, narrow = lax.axis_size("ep"), lax.axis_size("tp")
    tokens, width = grad_values.shape
    half = width // 2
    slots, hidden_width = pre_acts.shape[2:]
    most = slots // (wide * narrow)
    rows = -(-2 * most // 8) * 8
    f32, bf16 = jnp.float32, jnp.bfloat16
    block = pltpu.VMEM((rows, half), bf16)
    groups = groups_of(wide)
    order = [k for group in groups for k in group]
    partials = latent_partials.reshape(narrow, tokens, latent.shape[1])
    leading, place, *fillers = call(
        functools.partial(pack_kernel, most, order, 1),
        [
            block,
            pltpu.VMEM((2, wide, rows, tokens), bf16),
            pltpu.VMEM((1, tokens), f32),
            pltpu.VMEM((grad_scales.shape[1], tokens), f32),
            pltpu.VMEM((tokens, width), bf16),
        ],
        *pinned(
            expert_ids.reshape(1, tokens),
            route_weights.reshape(1, tokens),
            grad_scales.T,
            grad_values,
        ),
        specs=[HBM] * 4,
        scratch=[pltpu.VMEM((1, tokens), jnp.int32), pltpu.SemaphoreType.DMA((4,))],
        name="pack",
    )
    deep, parts = shares_of(tokens, latent.shape[1], half)
    more = call(
        functools.partial(pack_more_kernel, most, order[1:]),
        [block] * (wide - 1)
        + [pltpu.VMEM((deep + rows, half), bf16)] * (narrow - 1)
        + [pltpu.VMEM(latent.shape, bf16)],
        place,
        *fillers,
        *pinned(partials),
        specs=[VMEM] * 4 + [HBM],
        scratch=[pltpu.SemaphoreType.DMA((1 + (narrow - 1) * len(parts),))],
        name="pack_more",
    )
    packed = dict(zip(order, [leading, *more]))

    first, staged = groups[0][0], len(groups) > 1
    both = [swap(more[wide - 2 + j], "rows0", tp=j) for j in range(1, narrow)]
    if staged and narrow > 1:
        both[-1] = after(both[-1], place, 1 << 27)
    taken = {0: [packed[0]] + both}
    arrived = {}
    for k in order:
        if k:
            given = packed[k] if k in (first, 1) else after(packed[k], arrived[first])
            arrived[k] = swap(given, f"rows{k}", ep=k)
            if staged and k == groups[1][0]:
                arrived[k] = after(arrived[k], packed[first], 1 << 28)
    fetched = [
        pre_acts.reshape(2, wide, narrow * most, hidden_width),
        w_down[0],
        w_gate[0],
        w_up[0],
        latent,
        latent_gain.reshape(1, -1),
    ]
    factors = pltpu.VMEM((wide, narrow * most, hidden_width), f32)
    up_by, gate_by, down, gate, up, latent, latent_gain = call(
        functools.partial(fetch_kernel, most),
        [factors, factors] + [like(array) for array in fetched[1:]],
        *pinned(*fetched),
        specs=[HBM] * len(fetched),
        scratch=[like(fetched[0]), pltpu.SemaphoreType.DMA((len(fetched),))],
        earlier=[arrived[first]],
        name="fetch",
    )
    returned = {}
    values = latent.astype(f32)
    received, products, moved = None, None, None
    for group in groups:
        for k in group:
            if k:
                if products and k == group[0]:
                    arrived[k] = after(arrived[k], summed)
                if products and k == 1:
                    arrived[k] = after(arrived[k], down)
                crossing = [swap(arrived[k], f"rows{k}", tp=j) for j in range(1, narrow)]
                if products:
                    crossing[-1] = after(crossing[-1], products[0])
            if k:
                taken[k] = [arrived[k]] + crossing
        count = len(group) * narrow * most
        extra = group is groups[-1]
        if extra:
            if staged:
                both[-1] = after(both[-1], summed)
            own_grad = more[-1].astype(f32)
            for value in both:
                pieces = [
                    value[: min(deep, tokens - at), column : column + latent.shape[1]]
                    for at, column in parts
                ]
                own_grad += jnp.concatenate(pieces, axis=0).astype(f32)
            gained = own_grad * latent_gain
            row_sums = jnp.stack(
                [jnp.sum(values * values, axis=1), jnp.sum(gained * values, axis=1)]
            )
        summed, sent = call(
            functools.partial(hidden_kernel, most, extra, [0 if j == 0 or k else deep for k in group for j in range(narrow)]),
            [
                pltpu.VMEM((count, hidden_width), f32),
                pltpu.VMEM((count + (EXTRA if extra else 0), hidden_width), bf16),
            ],
            *[rows_of_k for k in group for rows_of_k in taken[k]],
            *([row_sums] if extra else []),
            down,
            name="hidden",
            earlier=products[:1] if products else (),
        )
        received = swap(sent, f"hidden{group[0]}", sub=1)
        if moved is not None:
            received = after(received, moved)
        products = call(
            functools.partial(back_kernel, most, group),
            [block] * (len(group) * narrow),
            summed,
            received,
            up_by,
            gate_by,
            gate,
            up,
            name="back",
        )
        for at, k in enumerate(group):
            mine, others = products[at * narrow], products[at * narrow + 1 : (at + 1) * narrow]
            if k == 0:
                kept = mine, others
            else:
                total = mine.astype(f32)
                for j, other in enumerate(others):
                    total += swap(other, f"back{k}", tp=j + 1).astype(f32)
                total = total.astype(bf16)
                returned[k] = [swap(total, f"back{k}", ep=k)]
                if k == group[0]:
                    moved = total
    mine, others = kept
    returned[0] = [mine] + [
        swap(after(other, moved) if staged else other, "back0", tp=j + 1)
        for j, other in enumerate(others)
    ]
    tail = received[count : count + 4, :tokens].astype(f32)
    row_sums = row_sums + tail[:2] + tail[2:]
    inverse_rms = lax.rsqrt(row_sums[0] / LAT + 1e-06)[:, None]
    d_latent = (
        inverse_rms * gained - values * inverse_rms**3 * row_sums[1][:, None] / LAT
    ).astype(bf16)
    latest = groups[-1][:1] if staged else []
    distances = [k for k in order if k not in latest]
    (grad_input,) = call(
        functools.partial(unpack_kernel, {k: len(returned[k]) for k in distances}, False),
        [pltpu.VMEM((tokens, width), bf16) if staged else jax.ShapeDtypeStruct((tokens, width), bf16)],
        place,
        *[part for k in distances for part in returned[k]],
        name="unpack",
    )
    if staged:
        (grad_input,) = call(
            functools.partial(unpack_kernel, {k: len(returned[k]) for k in latest}, True),
            [jax.ShapeDtypeStruct((tokens, width), bf16)],
            place,
            *[part for k in latest for part in returned[k]],
            grad_input,
            name="unpack_latest",
        )
    return (grad_input, d_latent)


def solution(mesh):
    placed = (
        P(("rep", "ep", "tp"), "sub"),
        P(("rep", "ep", "tp"), "sub"),
        P(("rep", "ep", "tp"), None),
        P(("rep", "ep", "tp"), None),
        P("ep", "sub", "tp"),
        P("ep", "sub", "tp"),
        P("ep", "tp", "sub"),
        P(("rep", "ep"), None, None, "tp"),
        P("tp", ("rep", "ep"), "sub"),
        P(("rep", "ep", "tp"), "sub"),
        P("sub"),
    )
    return jax.shard_map(
        local,
        mesh=mesh,
        in_specs=placed,
        out_specs=(P(("rep", "ep", "tp"), "sub"), P(("rep", "ep", "tp"), "sub")),
        check_vma=False,
    )
```

```python
import functools

import jax
import jax.numpy as jnp
import numpy as np
from jax import lax
from jax.experimental import pallas as pl
from jax.experimental.pallas import tpu as pltpu
from jax.sharding import PartitionSpec as P

LAT = 512
NT = (((1,), (1,)), ((), ()))
TN = (((0,), (0,)), ((), ()))
VMEM = pl.BlockSpec(memory_space=pltpu.VMEM)
ANY = pl.BlockSpec(memory_space=pl.ANY)
HBM = pl.BlockSpec(memory_space=pltpu.HBM)
EXTRA = 16
VMEM_LIMIT = 20 * 1024 * 1024


def dot(a, b, dims, precision=None):
    return lax.dot_general(a, b, dims, precision=precision, preferred_element_type=jnp.float32)


def swap(value, what, **steps):
    counts = [lax.axis_size(axis) for axis in steps]
    pairs = []
    for place in np.ndindex(*counts):
        other = [index ^ step for index, step in zip(place, steps.values())]
        pairs.append(tuple(int(np.ravel_multi_index(p, counts)) for p in (place, other)))
    with jax.named_scope("_".join([what, *steps])):
        return lax.ppermute(value, tuple(steps), pairs)


def pinned(*arrays):
    return [pltpu.with_memory_space_constraint(array, pltpu.HBM) for array in arrays]


def like(array):
    return pltpu.VMEM(array.shape, array.dtype)


def call(kernel, outs, *args, cost=0, name=None, specs=None, scratch=(), earlier=()):
    specs = (specs or [VMEM] * len(args)) + [ANY] * len(earlier)
    if earlier:
        taken, body = len(args), kernel

        def kernel(*refs):
            body(*refs[:taken], *refs[taken + len(earlier) :])

    return pl.pallas_call(
        kernel,
        out_shape=outs,
        in_specs=specs,
        out_specs=[VMEM] * len(outs),
        scratch_shapes=scratch,
        compiler_params=pltpu.CompilerParams(vmem_limit_bytes=VMEM_LIMIT),
        cost_estimate=pl.CostEstimate(flops=cost, bytes_accessed=0, transcendentals=0),
        name=name,
    )(*args, *earlier)


def after(value, earlier, cost=0):
    return pl.pallas_call(
        lambda value_ref, earlier_ref, out_ref: None,
        out_shape=jax.ShapeDtypeStruct(value.shape, value.dtype),
        in_specs=[ANY, ANY],
        out_specs=ANY,
        input_output_aliases={0: 0},
        compiler_params=pltpu.CompilerParams(vmem_limit_bytes=1 << 17),
        cost_estimate=pl.CostEstimate(flops=cost, bytes_accessed=0, transcendentals=0),
        name="after",
    )(value, earlier)


def fill(block_ref, most, low, high, weights_ref, scales_ref, grad_ref):
    half, scale_half = grad_ref.shape[1] // 2, scales_ref.shape[0] // 2
    placed = jnp.dot(
        low.astype(jnp.bfloat16), grad_ref[:, :half], preferred_element_type=jnp.float32
    )
    placed += jnp.dot(
        high.astype(jnp.bfloat16), grad_ref[:, half:], preferred_element_type=jnp.float32
    )
    scale = dot(low.astype(jnp.float32), scales_ref[:scale_half], NT, lax.Precision.HIGHEST)
    scale += dot(high.astype(jnp.float32), scales_ref[scale_half:], NT, lax.Precision.HIGHEST)
    weight = jnp.sum(jnp.where(low | high, weights_ref[...], 0.0), axis=1, keepdims=True)
    for b in range(scale_half):
        part = slice(b * 128, (b + 1) * 128)
        block_ref[:, part] = (placed[:, part] * scale[:, b : b + 1] * weight).astype(jnp.bfloat16)


def fetch(sources, targets, sems, first=0):
    copies = [
        pltpu.make_async_copy(source, target, sems.at[first + i])
        for i, (source, target) in enumerate(zip(sources, targets))
    ]
    for copy in copies:
        copy.start()
    return copies


def pack_kernel(most, order, leading, *refs):
    given, refs = refs[:4], refs[4:]
    blocks, (place_ref, *held), (ids_ref, sems) = refs[:leading], refs[leading:-2], refs[-2:]
    held = [ids_ref] + held
    copies = fetch(given, held, sems)
    copies[0].wait()
    weights_ref, scales_ref, grad_ref = held[1:]
    tokens, rows = grad_ref.shape[0], blocks[0].shape[0]
    me = lax.axis_index("ep")
    ids = ids_ref[...]
    expert = lax.broadcasted_iota(jnp.int32, (max(8, len(order)), tokens), 0)
    named = expert == ids
    before = lax.broadcasted_iota(jnp.int32, (tokens, tokens), 0) < lax.broadcasted_iota(
        jnp.int32, (tokens, tokens), 1
    )
    earlier = jnp.dot(
        named.astype(jnp.bfloat16), before.astype(jnp.bfloat16), preferred_element_type=jnp.float32
    )
    position = jnp.sum(jnp.where(named, earlier, 0.0), axis=0, keepdims=True).astype(jnp.int32)
    row = lax.broadcasted_iota(jnp.int32, (rows, tokens), 0)
    found = []
    for k in order:
        local = jnp.where(ids == (me ^ k), position, -2 * rows)
        low, high = row == local, row - most == local
        found.append((low, high))
        place_ref[0, k] = low.astype(jnp.bfloat16)
        place_ref[1, k] = high.astype(jnp.bfloat16)
    for copy in copies[1:]:
        copy.wait()
    for block_ref, (low, high) in zip(blocks, found):
        fill(block_ref, most, low, high, weights_ref, scales_ref, grad_ref)


def shares_of(tokens, columns, width):
    across = width // columns
    deep = -(-tokens // across // 16) * 16
    return deep, [(at, i * columns) for i, at in enumerate(range(0, tokens, deep))]


def pack_more_kernel(most, order, place_ref, weights_ref, scales_ref, grad_ref, partial_ref, *refs):
    count, tokens, columns = partial_ref.shape
    blocks, crossing = refs[: len(order)], refs[len(order) : len(order) + count - 1]
    own_ref, sems = refs[-2:]
    lane, rows = lax.axis_index("tp"), blocks[0].shape[0]
    deep, parts = shares_of(tokens, columns, blocks[0].shape[1])
    sources, targets = [partial_ref.at[lane]], [own_ref]
    for j in range(1, count):
        for at, column in parts:
            size = min(deep, tokens - at)
            sources.append(partial_ref.at[lane ^ j, pl.ds(at, size)])
            targets.append(crossing[j - 1].at[pl.ds(0, size), pl.ds(column, columns)])
    copies = fetch(sources, targets, sems)
    for block_ref, k in zip(blocks, order):
        low, high = place_ref[0, k] != 0, place_ref[1, k] != 0
        fill(block_ref, most, low, high, weights_ref, scales_ref, grad_ref)
        if k == 0:
            for both_ref in crossing:
                both_ref[deep:, :] = block_ref[...]
    for copy in copies:
        copy.wait()


def by_xor(value, most, narrow, lane):
    step = 1
    while step < narrow:
        pieces = [value[i * most : (i + step) * most] for i in range(0, narrow, step)]
        turned = [pieces[i ^ 1] for i in range(len(pieces))]
        value = jnp.where((lane & step) != 0, jnp.concatenate(turned, axis=0), value)
        step *= 2
    return value


def fetch_kernel(most, *refs):
    pre_ref, sems = refs[-2:]
    wide = pre_ref.shape[1]
    narrow = pre_ref.shape[2] // most
    count = (len(refs) - 3) // 2
    given, (up_ref, gate_ref, *held) = refs[:count], refs[count:-2]
    copies = fetch(given, [pre_ref] + held, sems)
    me, lane = lax.axis_index("ep"), lax.axis_index("tp")
    copies[0].wait()
    for k in range(wide):
        gate_pre, up_pre = [
            by_xor(pre_ref[i, me ^ k].astype(jnp.float32), most, narrow, lane) for i in range(2)
        ]
        sig = 1.0 / (1.0 + jnp.exp(-gate_pre))
        up_ref[k] = gate_pre * sig
        gate_ref[k] = up_pre * sig * (1.0 + gate_pre * (1.0 - sig))
    for copy in copies[1:]:
        copy.wait()


def hidden_kernel(most, extra, skips, *refs):
    blocks, (down_ref, sum_ref, sent_ref) = refs[:-3], refs[-3:]
    half = down_ref.shape[1] // 2
    count = sum_ref.shape[0]
    if extra:
        blocks, row_sums = blocks[:-1], blocks[-1][...]
        high = row_sums.astype(jnp.bfloat16).astype(jnp.float32)
        spare = jnp.zeros((EXTRA - 4, row_sums.shape[1]), jnp.float32)
        tail = jnp.concatenate([high, row_sums - high, spare], axis=0)
        sent_ref[count:, :] = jnp.zeros((EXTRA, sent_ref.shape[1]), sent_ref.dtype)
        sent_ref[count:, : row_sums.shape[1]] = tail.astype(sent_ref.dtype)
    values = [b[skip:, :].astype(jnp.float32) for b, skip in zip(blocks, skips)]
    low = jnp.concatenate([v[:most] for v in values], axis=0).astype(jnp.bfloat16)
    high = jnp.concatenate([v[most : 2 * most] for v in values], axis=0).astype(jnp.bfloat16)
    total = dot(low, down_ref[:, :half], NT) + dot(high, down_ref[:, half:], NT)
    sum_ref[...] = total
    sent_ref[:count, :] = total.astype(sent_ref.dtype)


def back_kernel(most, group, sum_ref, other_ref, up_by_ref, gate_by_ref, gate_ref, up_ref, *outs):
    half = gate_ref.shape[0] // 2
    hidden = sum_ref[...] + other_ref[: sum_ref.shape[0], :].astype(jnp.float32)
    up_by, gate_by = [
        jnp.concatenate([by_ref[k] for k in group], axis=0) for by_ref in (up_by_ref, gate_by_ref)
    ]
    up_grad = (hidden * up_by).astype(jnp.bfloat16)
    gate_grad = (hidden * gate_by).astype(jnp.bfloat16)
    low = dot(gate_grad, gate_ref[:half], NT) + dot(up_grad, up_ref[:half], NT)
    high = dot(gate_grad, gate_ref[half:], NT) + dot(up_grad, up_ref[half:], NT)
    for i, out in enumerate(outs):
        part = slice(i * most, (i + 1) * most)
        pieces = [low[part], high[part]]
        spare = out.shape[0] - 2 * most
        if spare:
            pieces.append(jnp.zeros((spare, half), jnp.float32))
        out[...] = jnp.concatenate(pieces, axis=0).astype(jnp.bfloat16)


def unpack_kernel(parts, started, place_ref, *refs):
    given, out_ref = list(refs[:-1]), refs[-1]
    half = out_ref.shape[1] // 2
    blocks = {}
    for k, count in parts.items():
        rows = given.pop(0)[...].astype(jnp.float32)
        for _ in range(count - 1):
            rows += given.pop(0)[...].astype(jnp.float32)
        blocks[k] = rows.astype(jnp.bfloat16)
    for side in range(2):
        columns = slice(side * half, (side + 1) * half)
        total = given[0][:, columns].astype(jnp.float32) if started else 0.0
        for k, rows in blocks.items():
            total = total + dot(place_ref[side, k], rows, TN)
        out_ref[:, columns] = total.astype(jnp.bfloat16)


def groups_of(wide):
    left = list(range(wide - 1, -1, -1))
    if wide < 4:
        return [left]
    return [[left[0], 0]] + [left[i : min(i + 2, wide - 1)] for i in range(1, wide - 1, 2)]


def local(
    grad_values,
    grad_scales,
    expert_ids,
    route_weights,
    w_gate,
    w_up,
    w_down,
    pre_acts,
    latent_partials,
    latent,
    latent_gain,
):
    wide, narrow = lax.axis_size("ep"), lax.axis_size("tp")
    tokens, width = grad_values.shape
    half = width // 2
    slots, hidden_width = pre_acts.shape[2:]
    most = slots // (wide * narrow)
    rows = -(-2 * most // 8) * 8
    f32, bf16 = jnp.float32, jnp.bfloat16
    block = pltpu.VMEM((rows, half), bf16)
    groups = groups_of(wide)
    order = [k for group in groups for k in group]
    partials = latent_partials.reshape(narrow, tokens, latent.shape[1])
    leading, place, *fillers = call(
        functools.partial(pack_kernel, most, order, 1),
        [
            block,
            pltpu.VMEM((2, wide, rows, tokens), bf16),
            pltpu.VMEM((1, tokens), f32),
            pltpu.VMEM((grad_scales.shape[1], tokens), f32),
            pltpu.VMEM((tokens, width), bf16),
        ],
        *pinned(
            expert_ids.reshape(1, tokens),
            route_weights.reshape(1, tokens),
            grad_scales.T,
            grad_values,
        ),
        specs=[HBM] * 4,
        scratch=[pltpu.VMEM((1, tokens), jnp.int32), pltpu.SemaphoreType.DMA((4,))],
        name="pack",
    )
    deep, parts = shares_of(tokens, latent.shape[1], half)
    more = call(
        functools.partial(pack_more_kernel, most, order[1:]),
        [block] * (wide - 1)
        + [pltpu.VMEM((deep + rows, half), bf16)] * (narrow - 1)
        + [pltpu.VMEM(latent.shape, bf16)],
        place,
        *fillers,
        *pinned(partials),
        specs=[VMEM] * 4 + [HBM],
        scratch=[pltpu.SemaphoreType.DMA((1 + (narrow - 1) * len(parts),))],
        name="pack_more",
    )
    packed = dict(zip(order, [leading, *more]))

    first, staged = groups[0][0], len(groups) > 1
    both = [swap(more[wide - 2 + j], "rows0", tp=j) for j in range(1, narrow)]
    if staged and narrow > 1:
        both[-1] = after(both[-1], place, 1 << 27)
    taken = {0: [packed[0]] + both}
    arrived = {}
    for k in order:
        if k:
            given = packed[k] if k in (first, 1) else after(packed[k], arrived[first])
            arrived[k] = swap(given, f"rows{k}", ep=k)
            if staged and k == groups[1][0]:
                arrived[k] = after(arrived[k], packed[first], 1 << 28)
    fetched = [
        pre_acts.reshape(2, wide, narrow * most, hidden_width),
        w_down[0],
        w_gate[0],
        w_up[0],
        latent,
        latent_gain.reshape(1, -1),
    ]
    factors = pltpu.VMEM((wide, narrow * most, hidden_width), f32)
    up_by, gate_by, down, gate, up, latent, latent_gain = call(
        functools.partial(fetch_kernel, most),
        [factors, factors] + [like(array) for array in fetched[1:]],
        *pinned(*fetched),
        specs=[HBM] * len(fetched),
        scratch=[like(fetched[0]), pltpu.SemaphoreType.DMA((len(fetched),))],
        earlier=[arrived[first]],
        name="fetch",
    )
    returned = {}
    values = latent.astype(f32)
    received, products, moved = None, None, None
    for group in groups:
        for k in group:
            if k:
                if products and k == group[0]:
                    arrived[k] = after(arrived[k], summed)
                if products and k == 1:
                    arrived[k] = after(arrived[k], down)
                crossing = [swap(arrived[k], f"rows{k}", tp=j) for j in range(1, narrow)]
                if products:
                    crossing[-1] = after(crossing[-1], products[0], (1 << 31) * (k == 1))
            if k:
                taken[k] = [arrived[k]] + crossing
        count = len(group) * narrow * most
        extra = group is groups[-1]
        if extra:
            if staged:
                both[-1] = after(both[-1], summed)
            own_grad = more[-1].astype(f32)
            for value in both:
                pieces = [
                    value[: min(deep, tokens - at), column : column + latent.shape[1]]
                    for at, column in parts
                ]
                own_grad += jnp.concatenate(pieces, axis=0).astype(f32)
            gained = own_grad * latent_gain
            row_sums = jnp.stack(
                [jnp.sum(values * values, axis=1), jnp.sum(gained * values, axis=1)]
            )
        summed, sent = call(
            functools.partial(hidden_kernel, most, extra, [0 if j == 0 or k else deep for k in group for j in range(narrow)]),
            [
                pltpu.VMEM((count, hidden_width), f32),
                pltpu.VMEM((count + (EXTRA if extra else 0), hidden_width), bf16 if products else f32),
            ],
            *[rows_of_k for k in group for rows_of_k in taken[k]],
            *([row_sums] if extra else []),
            down,
            name="hidden",
            earlier=products[:1] if products else (),
        )
        received = swap(sent, f"hidden{group[0]}", sub=1)
        if moved is not None:
            received = after(received, moved)
        products = call(
            functools.partial(back_kernel, most, group),
            [block] * (len(group) * narrow),
            summed,
            received,
            up_by,
            gate_by,
            gate,
            up,
            name="back",
        )
        for at, k in enumerate(group):
            mine, others = products[at * narrow], products[at * narrow + 1 : (at + 1) * narrow]
            if k == 0:
                kept = mine, others
            else:
                total = mine.astype(f32)
                for j, other in enumerate(others):
                    total += swap(other, f"back{k}", tp=j + 1).astype(f32)
                total = total.astype(bf16)
                returned[k] = [swap(total, f"back{k}", ep=k)]
                if k == group[0]:
                    moved = total
    mine, others = kept
    returned[0] = [mine] + [
        swap(after(other, moved) if staged else other, "back0", tp=j + 1)
        for j, other in enumerate(others)
    ]
    tail = received[count : count + 4, :tokens].astype(f32)
    row_sums = row_sums + tail[:2] + tail[2:]
    inverse_rms = lax.rsqrt(row_sums[0] / LAT + 1e-06)[:, None]
    d_latent = (
        inverse_rms * gained - values * inverse_rms**3 * row_sums[1][:, None] / LAT
    ).astype(bf16)
    latest = groups[-1][:1] if staged else []
    distances = [k for k in order if k not in latest]
    (grad_input,) = call(
        functools.partial(unpack_kernel, {k: len(returned[k]) for k in distances}, False),
        [pltpu.VMEM((tokens, width), bf16) if staged else jax.ShapeDtypeStruct((tokens, width), bf16)],
        place,
        *[part for k in distances for part in returned[k]],
        name="unpack",
    )
    if staged:
        (grad_input,) = call(
            functools.partial(unpack_kernel, {k: len(returned[k]) for k in latest}, True),
            [jax.ShapeDtypeStruct((tokens, width), bf16)],
            place,
            *[part for k in latest for part in returned[k]],
            grad_input,
            name="unpack_latest",
        )
    return (grad_input, d_latent)


def solution(mesh):
    placed = (
        P(("rep", "ep", "tp"), "sub"),
        P(("rep", "ep", "tp"), "sub"),
        P(("rep", "ep", "tp"), None),
        P(("rep", "ep", "tp"), None),
        P("ep", "sub", "tp"),
        P("ep", "sub", "tp"),
        P("ep", "tp", "sub"),
        P(("rep", "ep"), None, None, "tp"),
        P("tp", ("rep", "ep"), "sub"),
        P(("rep", "ep", "tp"), "sub"),
        P("sub"),
    )
    return jax.shard_map(
        local,
        mesh=mesh,
        in_specs=placed,
        out_specs=(P(("rep", "ep", "tp"), "sub"), P(("rep", "ep", "tp"), "sub")),
        check_vma=False,
    )
```

```python
import functools

import jax
import jax.numpy as jnp
import numpy as np
from jax import lax
from jax.experimental import pallas as pl
from jax.experimental.pallas import tpu as pltpu
from jax.sharding import PartitionSpec as P

LAT = 512
NT = (((1,), (1,)), ((), ()))
TN = (((0,), (0,)), ((), ()))
VMEM = pl.BlockSpec(memory_space=pltpu.VMEM)
ANY = pl.BlockSpec(memory_space=pl.ANY)
HBM = pl.BlockSpec(memory_space=pltpu.HBM)
EXTRA = 16
VMEM_LIMIT = 20 * 1024 * 1024


def dot(a, b, dims, precision=None):
    return lax.dot_general(a, b, dims, precision=precision, preferred_element_type=jnp.float32)


def swap(value, what, **steps):
    counts = [lax.axis_size(axis) for axis in steps]
    pairs = []
    for place in np.ndindex(*counts):
        other = [index ^ step for index, step in zip(place, steps.values())]
        pairs.append(tuple(int(np.ravel_multi_index(p, counts)) for p in (place, other)))
    with jax.named_scope("_".join([what, *steps])):
        return lax.ppermute(value, tuple(steps), pairs)


def pinned(*arrays):
    return [pltpu.with_memory_space_constraint(array, pltpu.HBM) for array in arrays]


def like(array):
    return pltpu.VMEM(array.shape, array.dtype)


def call(kernel, outs, *args, cost=0, name=None, specs=None, scratch=(), earlier=()):
    specs = (specs or [VMEM] * len(args)) + [ANY] * len(earlier)
    if earlier:
        taken, body = len(args), kernel

        def kernel(*refs):
            body(*refs[:taken], *refs[taken + len(earlier) :])

    return pl.pallas_call(
        kernel,
        out_shape=outs,
        in_specs=specs,
        out_specs=[VMEM] * len(outs),
        scratch_shapes=scratch,
        compiler_params=pltpu.CompilerParams(vmem_limit_bytes=VMEM_LIMIT),
        cost_estimate=pl.CostEstimate(flops=cost, bytes_accessed=0, transcendentals=0),
        name=name,
    )(*args, *earlier)


def after(value, earlier, cost=0):
    return pl.pallas_call(
        lambda value_ref, earlier_ref, out_ref: None,
        out_shape=jax.ShapeDtypeStruct(value.shape, value.dtype),
        in_specs=[ANY, ANY],
        out_specs=ANY,
        input_output_aliases={0: 0},
        compiler_params=pltpu.CompilerParams(vmem_limit_bytes=1 << 17),
        cost_estimate=pl.CostEstimate(flops=cost, bytes_accessed=0, transcendentals=0),
        name="after",
    )(value, earlier)


def fill(block_ref, most, low, high, weights_ref, scales_ref, grad_ref):
    half, scale_half = grad_ref.shape[1] // 2, scales_ref.shape[0] // 2
    placed = jnp.dot(
        low.astype(jnp.bfloat16), grad_ref[:, :half], preferred_element_type=jnp.float32
    )
    placed += jnp.dot(
        high.astype(jnp.bfloat16), grad_ref[:, half:], preferred_element_type=jnp.float32
    )
    scale = dot(low.astype(jnp.float32), scales_ref[:scale_half], NT, lax.Precision.HIGHEST)
    scale += dot(high.astype(jnp.float32), scales_ref[scale_half:], NT, lax.Precision.HIGHEST)
    weight = jnp.sum(jnp.where(low | high, weights_ref[...], 0.0), axis=1, keepdims=True)
    for b in range(scale_half):
        part = slice(b * 128, (b + 1) * 128)
        block_ref[:, part] = (placed[:, part] * scale[:, b : b + 1] * weight).astype(jnp.bfloat16)


def fetch(sources, targets, sems, first=0):
    copies = [
        pltpu.make_async_copy(source, target, sems.at[first + i])
        for i, (source, target) in enumerate(zip(sources, targets))
    ]
    for copy in copies:
        copy.start()
    return copies


def pack_kernel(most, order, leading, *refs):
    given, refs = refs[:4], refs[4:]
    blocks, (place_ref, *held), (ids_ref, sems) = refs[:leading], refs[leading:-2], refs[-2:]
    held = [ids_ref] + held
    copies = fetch(given, held, sems)
    copies[0].wait()
    weights_ref, scales_ref, grad_ref = held[1:]
    tokens, rows = grad_ref.shape[0], blocks[0].shape[0]
    me = lax.axis_index("ep")
    ids = ids_ref[...]
    expert = lax.broadcasted_iota(jnp.int32, (max(8, len(order)), tokens), 0)
    named = expert == ids
    before = lax.broadcasted_iota(jnp.int32, (tokens, tokens), 0) < lax.broadcasted_iota(
        jnp.int32, (tokens, tokens), 1
    )
    earlier = jnp.dot(
        named.astype(jnp.bfloat16), before.astype(jnp.bfloat16), preferred_element_type=jnp.float32
    )
    position = jnp.sum(jnp.where(named, earlier, 0.0), axis=0, keepdims=True).astype(jnp.int32)
    row = lax.broadcasted_iota(jnp.int32, (rows, tokens), 0)
    found = []
    for k in order:
        local = jnp.where(ids == (me ^ k), position, -2 * rows)
        low, high = row == local, row - most == local
        found.append((low, high))
        place_ref[0, k] = low.astype(jnp.bfloat16)
        place_ref[1, k] = high.astype(jnp.bfloat16)
    for copy in copies[1:]:
        copy.wait()
    for block_ref, (low, high) in zip(blocks, found):
        fill(block_ref, most, low, high, weights_ref, scales_ref, grad_ref)


def shares_of(tokens, columns, width):
    across = width // columns
    deep = -(-tokens // across // 16) * 16
    return deep, [(at, i * columns) for i, at in enumerate(range(0, tokens, deep))]


def pack_more_kernel(most, order, place_ref, weights_ref, scales_ref, grad_ref, partial_ref, *refs):
    count, tokens, columns = partial_ref.shape
    blocks, crossing = refs[: len(order)], refs[len(order) : len(order) + count - 1]
    own_ref, sems = refs[-2:]
    lane, rows = lax.axis_index("tp"), blocks[0].shape[0]
    deep, parts = shares_of(tokens, columns, blocks[0].shape[1])
    sources, targets = [partial_ref.at[lane]], [own_ref]
    for j in range(1, count):
        for at, column in parts:
            size = min(deep, tokens - at)
            sources.append(partial_ref.at[lane ^ j, pl.ds(at, size)])
            targets.append(crossing[j - 1].at[pl.ds(0, size), pl.ds(column, columns)])
    copies = fetch(sources, targets, sems)
    for block_ref, k in zip(blocks, order):
        low, high = place_ref[0, k] != 0, place_ref[1, k] != 0
        fill(block_ref, most, low, high, weights_ref, scales_ref, grad_ref)
        if k == 0:
            for both_ref in crossing:
                both_ref[deep:, :] = block_ref[...]
    for copy in copies:
        copy.wait()


def by_xor(value, most, narrow, lane):
    step = 1
    while step < narrow:
        pieces = [value[i * most : (i + step) * most] for i in range(0, narrow, step)]
        turned = [pieces[i ^ 1] for i in range(len(pieces))]
        value = jnp.where((lane & step) != 0, jnp.concatenate(turned, axis=0), value)
        step *= 2
    return value


def fetch_kernel(most, *refs):
    pre_ref, sems = refs[-2:]
    wide = pre_ref.shape[1]
    narrow = pre_ref.shape[2] // most
    count = (len(refs) - 3) // 2
    given, (up_ref, gate_ref, *held) = refs[:count], refs[count:-2]
    copies = fetch(given, [pre_ref] + held, sems)
    me, lane = lax.axis_index("ep"), lax.axis_index("tp")
    copies[0].wait()
    for k in range(wide):
        gate_pre, up_pre = [
            by_xor(pre_ref[i, me ^ k].astype(jnp.float32), most, narrow, lane) for i in range(2)
        ]
        sig = 1.0 / (1.0 + jnp.exp(-gate_pre))
        up_ref[k] = gate_pre * sig
        gate_ref[k] = up_pre * sig * (1.0 + gate_pre * (1.0 - sig))
    for copy in copies[1:]:
        copy.wait()


def hidden_kernel(most, extra, skips, *refs):
    blocks, (down_ref, sum_ref, sent_ref) = refs[:-3], refs[-3:]
    half = down_ref.shape[1] // 2
    count = sum_ref.shape[0]
    if extra:
        blocks, row_sums = blocks[:-1], blocks[-1][...]
        high = row_sums.astype(jnp.bfloat16).astype(jnp.float32)
        spare = jnp.zeros((EXTRA - 4, row_sums.shape[1]), jnp.float32)
        tail = jnp.concatenate([high, row_sums - high, spare], axis=0)
        sent_ref[count:, :] = jnp.zeros((EXTRA, sent_ref.shape[1]), sent_ref.dtype)
        sent_ref[count:, : row_sums.shape[1]] = tail.astype(sent_ref.dtype)
    values = [b[skip:, :].astype(jnp.float32) for b, skip in zip(blocks, skips)]
    low = jnp.concatenate([v[:most] for v in values], axis=0).astype(jnp.bfloat16)
    high = jnp.concatenate([v[most : 2 * most] for v in values], axis=0).astype(jnp.bfloat16)
    total = dot(low, down_ref[:, :half], NT) + dot(high, down_ref[:, half:], NT)
    sum_ref[...] = total
    sent_ref[:count, :] = total.astype(sent_ref.dtype)


def back_kernel(most, group, sum_ref, other_ref, up_by_ref, gate_by_ref, gate_ref, up_ref, *outs):
    half = gate_ref.shape[0] // 2
    hidden = sum_ref[...] + other_ref[: sum_ref.shape[0], :].astype(jnp.float32)
    up_by, gate_by = [
        jnp.concatenate([by_ref[k] for k in group], axis=0) for by_ref in (up_by_ref, gate_by_ref)
    ]
    up_grad = (hidden * up_by).astype(jnp.bfloat16)
    gate_grad = (hidden * gate_by).astype(jnp.bfloat16)
    low = dot(gate_grad, gate_ref[:half], NT) + dot(up_grad, up_ref[:half], NT)
    high = dot(gate_grad, gate_ref[half:], NT) + dot(up_grad, up_ref[half:], NT)
    for i, out in enumerate(outs):
        part = slice(i * most, (i + 1) * most)
        pieces = [low[part], high[part]]
        spare = out.shape[0] - 2 * most
        if spare:
            pieces.append(jnp.zeros((spare, half), jnp.float32))
        out[...] = jnp.concatenate(pieces, axis=0).astype(jnp.bfloat16)


def unpack_kernel(parts, started, place_ref, *refs):
    given, out_ref = list(refs[:-1]), refs[-1]
    half = out_ref.shape[1] // 2
    blocks = {}
    for k, count in parts.items():
        rows = given.pop(0)[...].astype(jnp.float32)
        for _ in range(count - 1):
            rows += given.pop(0)[...].astype(jnp.float32)
        blocks[k] = rows.astype(jnp.bfloat16)
    for side in range(2):
        columns = slice(side * half, (side + 1) * half)
        total = given[0][:, columns].astype(jnp.float32) if started else 0.0
        for k, rows in blocks.items():
            total = total + dot(place_ref[side, k], rows, TN)
        out_ref[:, columns] = total.astype(jnp.bfloat16)


def groups_of(wide):
    if wide < 4:
        return [list(range(wide - 1, -1, -1))]
    left = list(range(wide - 2, 1, -1))
    return [[wide - 1, 0], [1]] + [left[i : i + 2] for i in range(0, len(left), 2)]


def local(
    grad_values,
    grad_scales,
    expert_ids,
    route_weights,
    w_gate,
    w_up,
    w_down,
    pre_acts,
    latent_partials,
    latent,
    latent_gain,
):
    wide, narrow = lax.axis_size("ep"), lax.axis_size("tp")
    tokens, width = grad_values.shape
    half = width // 2
    slots, hidden_width = pre_acts.shape[2:]
    most = slots // (wide * narrow)
    rows = -(-2 * most // 8) * 8
    f32, bf16 = jnp.float32, jnp.bfloat16
    block = pltpu.VMEM((rows, half), bf16)
    groups = groups_of(wide)
    order = [k for group in groups for k in group]
    partials = latent_partials.reshape(narrow, tokens, latent.shape[1])
    leading, place, *fillers = call(
        functools.partial(pack_kernel, most, order, 1),
        [
            block,
            pltpu.VMEM((2, wide, rows, tokens), bf16),
            pltpu.VMEM((1, tokens), f32),
            pltpu.VMEM((grad_scales.shape[1], tokens), f32),
            pltpu.VMEM((tokens, width), bf16),
        ],
        *pinned(
            expert_ids.reshape(1, tokens),
            route_weights.reshape(1, tokens),
            grad_scales.T,
            grad_values,
        ),
        specs=[HBM] * 4,
        scratch=[pltpu.VMEM((1, tokens), jnp.int32), pltpu.SemaphoreType.DMA((4,))],
        name="pack",
    )
    deep, parts = shares_of(tokens, latent.shape[1], half)
    more = call(
        functools.partial(pack_more_kernel, most, order[1:]),
        [block] * (wide - 1)
        + [pltpu.VMEM((deep + rows, half), bf16)] * (narrow - 1)
        + [pltpu.VMEM(latent.shape, bf16)],
        place,
        *fillers,
        *pinned(partials),
        specs=[VMEM] * 4 + [HBM],
        scratch=[pltpu.SemaphoreType.DMA((1 + (narrow - 1) * len(parts),))],
        name="pack_more",
    )
    packed = dict(zip(order, [leading, *more]))

    first, staged = groups[0][0], len(groups) > 1
    both = [swap(more[wide - 2 + j], "rows0", tp=j) for j in range(1, narrow)]
    if staged and narrow > 1:
        both[-1] = after(both[-1], place, 1 << 27)
    taken = {0: [packed[0]] + both}
    arrived = {}
    for k in order:
        if k:
            given = packed[k] if k in (first, 1) else after(packed[k], arrived[first])
            arrived[k] = swap(given, f"rows{k}", ep=k)
            if staged and k == groups[2][0]:
                arrived[k] = after(arrived[k], packed[first], 1 << 28)
    fetched = [
        pre_acts.reshape(2, wide, narrow * most, hidden_width),
        w_down[0],
        w_gate[0],
        w_up[0],
        latent,
        latent_gain.reshape(1, -1),
    ]
    factors = pltpu.VMEM((wide, narrow * most, hidden_width), f32)
    up_by, gate_by, down, gate, up, latent, latent_gain = call(
        functools.partial(fetch_kernel, most),
        [factors, factors] + [like(array) for array in fetched[1:]],
        *pinned(*fetched),
        specs=[HBM] * len(fetched),
        scratch=[like(fetched[0]), pltpu.SemaphoreType.DMA((len(fetched),))],
        earlier=[arrived[first]],
        name="fetch",
    )
    values = latent.astype(f32)
    returned = {}

    def forward(group, kind, earlier=(), row_sums=()):
        count = len(group) * narrow * most
        skips = [0 if j == 0 or k else deep for k in group for j in range(narrow)]
        summed, sent = call(
            functools.partial(hidden_kernel, most, len(row_sums), skips),
            [
                pltpu.VMEM((count, hidden_width), f32),
                pltpu.VMEM((count + EXTRA * len(row_sums), hidden_width), kind),
            ],
            *[rows_of_k for k in group for rows_of_k in taken[k]],
            *row_sums,
            down,
            name="hidden",
            earlier=earlier,
        )
        return summed, swap(sent, f"hidden{group[0]}", sub=1)

    def backward(group, summed, received):
        products = call(
            functools.partial(back_kernel, most, group),
            [block] * (len(group) * narrow),
            summed,
            received,
            up_by,
            gate_by,
            gate,
            up,
            name="back",
        )
        return {k: products[i * narrow : (i + 1) * narrow] for i, k in enumerate(group)}

    def give_back(k, products):
        total = products[0].astype(f32)
        for j in range(1, narrow):
            total += swap(products[j], f"back{k}", tp=j).astype(f32)
        total = total.astype(bf16)
        returned[k] = [swap(total, f"back{k}", ep=k)]
        return total

    def row_sums_of(both):
        own_grad = more[-1].astype(f32)
        for value in both:
            pieces = [
                value[: min(deep, tokens - at), column : column + latent.shape[1]]
                for at, column in parts
            ]
            own_grad += jnp.concatenate(pieces, axis=0).astype(f32)
        gained = own_grad * latent_gain
        return gained, jnp.stack(
            [jnp.sum(values * values, axis=1), jnp.sum(gained * values, axis=1)]
        )

    def crossed(k, rows_of_k):
        return [swap(rows_of_k, f"rows{k}", tp=j) for j in range(1, narrow)]

    for k in groups[0]:
        if k:
            taken[k] = [arrived[k]] + crossed(k, arrived[k])
    gained, row_sums = row_sums_of(both) if not staged else (None, None)
    summed, received = forward(groups[0], f32, row_sums=() if staged else [row_sums])
    products = backward(groups[0], summed, received)
    kept = products[0]
    moved = give_back(first, products[first]) if first else None
    if staged:
        first_summed, gate_open = summed, products[first][:1]
        rows_of_k = after(arrived[1], down)
        crossing = crossed(1, rows_of_k)
        crossing[-1] = after(crossing[-1], gate_open[0], 1 << 31)
        taken[1] = [rows_of_k] + crossing
        near_summed, near_received = forward([1], bf16, earlier=gate_open)
        gate_open, near = [near_summed], True
        for group in groups[2:]:
            for k in group:
                rows_of_k = after(arrived[k], first_summed) if k == group[0] else arrived[k]
                crossing = crossed(k, rows_of_k)
                crossing[-1] = after(crossing[-1], gate_open[0])
                taken[k] = [rows_of_k] + crossing
            last = group is groups[-1]
            if last:
                both[-1] = after(both[-1], first_summed)
                gained, row_sums = row_sums_of(both)
            summed, received = forward(
                group, f32, earlier=gate_open, row_sums=[row_sums] if last else ()
            )
            if near:
                products = backward([1], near_summed, after(near_received, summed))
                give_back(1, products[1])
                near = False
            products = backward(group, summed, after(received, moved))
            gate_open = products[group[0]][:1]
            moved = [give_back(k, products[k]) for k in group][0]
    else:
        for k in groups[0][1:-1]:
            give_back(k, products[k])
    returned[0] = [kept[0]] + [
        swap(after(kept[j], moved) if staged else kept[j], "back0", tp=j) for j in range(1, narrow)
    ]
    count = summed.shape[0]
    tail = received[count : count + 4, :tokens].astype(f32)
    row_sums = row_sums + tail[:2] + tail[2:]
    inverse_rms = lax.rsqrt(row_sums[0] / LAT + 1e-06)[:, None]
    d_latent = (
        inverse_rms * gained - values * inverse_rms**3 * row_sums[1][:, None] / LAT
    ).astype(bf16)
    latest = groups[-1][:1] if staged else []
    distances = [k for k in order if k not in latest]
    (grad_input,) = call(
        functools.partial(unpack_kernel, {k: len(returned[k]) for k in distances}, False),
        [pltpu.VMEM((tokens, width), bf16) if staged else jax.ShapeDtypeStruct((tokens, width), bf16)],
        place,
        *[part for k in distances for part in returned[k]],
        name="unpack",
    )
    if staged:
        (grad_input,) = call(
            functools.partial(unpack_kernel, {k: len(returned[k]) for k in latest}, True),
            [jax.ShapeDtypeStruct((tokens, width), bf16)],
            place,
            *[part for k in latest for part in returned[k]],
            grad_input,
            name="unpack_latest",
        )
    return (grad_input, d_latent)


def solution(mesh):
    placed = (
        P(("rep", "ep", "tp"), "sub"),
        P(("rep", "ep", "tp"), "sub"),
        P(("rep", "ep", "tp"), None),
        P(("rep", "ep", "tp"), None),
        P("ep", "sub", "tp"),
        P("ep", "sub", "tp"),
        P("ep", "tp", "sub"),
        P(("rep", "ep"), None, None, "tp"),
        P("tp", ("rep", "ep"), "sub"),
        P(("rep", "ep", "tp"), "sub"),
        P("sub"),
    )
    return jax.shard_map(
        local,
        mesh=mesh,
        in_specs=placed,
        out_specs=(P(("rep", "ep", "tp"), "sub"), P(("rep", "ep", "tp"), "sub")),
        check_vma=False,
    )
```

```python
import functools

import jax
import jax.numpy as jnp
import numpy as np
from jax import lax
from jax.experimental import pallas as pl
from jax.experimental.pallas import tpu as pltpu
from jax.sharding import PartitionSpec as P

LAT = 512
NT = (((1,), (1,)), ((), ()))
TN = (((0,), (0,)), ((), ()))
VMEM = pl.BlockSpec(memory_space=pltpu.VMEM)
ANY = pl.BlockSpec(memory_space=pl.ANY)
HBM = pl.BlockSpec(memory_space=pltpu.HBM)
EXTRA = 16
VMEM_LIMIT = 20 * 1024 * 1024


def dot(a, b, dims, precision=None):
    return lax.dot_general(a, b, dims, precision=precision, preferred_element_type=jnp.float32)


def swap(value, what, **steps):
    counts = [lax.axis_size(axis) for axis in steps]
    pairs = []
    for place in np.ndindex(*counts):
        other = [index ^ step for index, step in zip(place, steps.values())]
        pairs.append(tuple(int(np.ravel_multi_index(p, counts)) for p in (place, other)))
    with jax.named_scope("_".join([what, *steps])):
        return lax.ppermute(value, tuple(steps), pairs)


def pinned(*arrays):
    return [pltpu.with_memory_space_constraint(array, pltpu.HBM) for array in arrays]


def like(array):
    return pltpu.VMEM(array.shape, array.dtype)


def call(kernel, outs, *args, cost=0, name=None, specs=None, scratch=(), earlier=()):
    specs = (specs or [VMEM] * len(args)) + [ANY] * len(earlier)
    if earlier:
        taken, body = len(args), kernel

        def kernel(*refs):
            body(*refs[:taken], *refs[taken + len(earlier) :])

    return pl.pallas_call(
        kernel,
        out_shape=outs,
        in_specs=specs,
        out_specs=[VMEM] * len(outs),
        scratch_shapes=scratch,
        compiler_params=pltpu.CompilerParams(vmem_limit_bytes=VMEM_LIMIT),
        cost_estimate=pl.CostEstimate(flops=cost, bytes_accessed=0, transcendentals=0),
        name=name,
    )(*args, *earlier)


def after(value, earlier, cost=0):
    return pl.pallas_call(
        lambda value_ref, earlier_ref, out_ref: None,
        out_shape=jax.ShapeDtypeStruct(value.shape, value.dtype),
        in_specs=[ANY, ANY],
        out_specs=ANY,
        input_output_aliases={0: 0},
        compiler_params=pltpu.CompilerParams(vmem_limit_bytes=1 << 17),
        cost_estimate=pl.CostEstimate(flops=cost, bytes_accessed=0, transcendentals=0),
        name="after",
    )(value, earlier)


def fill(block_ref, most, low, high, weights_ref, scales_ref, grad_ref):
    half, scale_half = grad_ref.shape[1] // 2, scales_ref.shape[0] // 2
    placed = jnp.dot(
        low.astype(jnp.bfloat16), grad_ref[:, :half], preferred_element_type=jnp.float32
    )
    placed += jnp.dot(
        high.astype(jnp.bfloat16), grad_ref[:, half:], preferred_element_type=jnp.float32
    )
    scale = dot(low.astype(jnp.float32), scales_ref[:scale_half], NT, lax.Precision.HIGHEST)
    scale += dot(high.astype(jnp.float32), scales_ref[scale_half:], NT, lax.Precision.HIGHEST)
    weight = jnp.sum(jnp.where(low | high, weights_ref[...], 0.0), axis=1, keepdims=True)
    for b in range(scale_half):
        part = slice(b * 128, (b + 1) * 128)
        block_ref[:, part] = (placed[:, part] * scale[:, b : b + 1] * weight).astype(jnp.bfloat16)


def fetch(sources, targets, sems, first=0):
    copies = [
        pltpu.make_async_copy(source, target, sems.at[first + i])
        for i, (source, target) in enumerate(zip(sources, targets))
    ]
    for copy in copies:
        copy.start()
    return copies


def pack_kernel(most, order, leading, *refs):
    given, refs = refs[:4], refs[4:]
    blocks, (place_ref, *held), (ids_ref, sems) = refs[:leading], refs[leading:-2], refs[-2:]
    held = [ids_ref] + held
    copies = fetch(given, held, sems)
    copies[0].wait()
    weights_ref, scales_ref, grad_ref = held[1:]
    tokens, rows = grad_ref.shape[0], blocks[0].shape[0]
    me = lax.axis_index("ep")
    ids = ids_ref[...]
    expert = lax.broadcasted_iota(jnp.int32, (max(8, len(order)), tokens), 0)
    named = expert == ids
    before = lax.broadcasted_iota(jnp.int32, (tokens, tokens), 0) < lax.broadcasted_iota(
        jnp.int32, (tokens, tokens), 1
    )
    earlier = jnp.dot(
        named.astype(jnp.bfloat16), before.astype(jnp.bfloat16), preferred_element_type=jnp.float32
    )
    position = jnp.sum(jnp.where(named, earlier, 0.0), axis=0, keepdims=True).astype(jnp.int32)
    row = lax.broadcasted_iota(jnp.int32, (rows, tokens), 0)
    found = []
    for k in order:
        local = jnp.where(ids == (me ^ k), position, -2 * rows)
        low, high = row == local, row - most == local
        found.append((low, high))
        place_ref[0, k] = low.astype(jnp.bfloat16)
        place_ref[1, k] = high.astype(jnp.bfloat16)
    for copy in copies[1:]:
        copy.wait()
    for block_ref, (low, high) in zip(blocks, found):
        fill(block_ref, most, low, high, weights_ref, scales_ref, grad_ref)


def shares_of(tokens, columns, width):
    across = width // columns
    deep = -(-tokens // across // 16) * 16
    return deep, [(at, i * columns) for i, at in enumerate(range(0, tokens, deep))]


def pack_more_kernel(most, order, place_ref, weights_ref, scales_ref, grad_ref, partial_ref, *refs):
    count, tokens, columns = partial_ref.shape
    blocks, crossing = refs[: len(order)], refs[len(order) : len(order) + count - 1]
    own_ref, sems = refs[-2:]
    lane, rows = lax.axis_index("tp"), blocks[0].shape[0]
    deep, parts = shares_of(tokens, columns, blocks[0].shape[1])
    sources, targets = [partial_ref.at[lane]], [own_ref]
    for j in range(1, count):
        for at, column in parts:
            size = min(deep, tokens - at)
            sources.append(partial_ref.at[lane ^ j, pl.ds(at, size)])
            targets.append(crossing[j - 1].at[pl.ds(0, size), pl.ds(column, columns)])
    copies = fetch(sources, targets, sems)
    for block_ref, k in zip(blocks, order):
        low, high = place_ref[0, k] != 0, place_ref[1, k] != 0
        fill(block_ref, most, low, high, weights_ref, scales_ref, grad_ref)
        if k == 0:
            for both_ref in crossing:
                both_ref[deep:, :] = block_ref[...]
    for copy in copies:
        copy.wait()


def by_xor(value, most, narrow, lane):
    step = 1
    while step < narrow:
        pieces = [value[i * most : (i + step) * most] for i in range(0, narrow, step)]
        turned = [pieces[i ^ 1] for i in range(len(pieces))]
        value = jnp.where((lane & step) != 0, jnp.concatenate(turned, axis=0), value)
        step *= 2
    return value


def fetch_kernel(most, *refs):
    pre_ref, sems = refs[-2:]
    wide = pre_ref.shape[1]
    narrow = pre_ref.shape[2] // most
    count = (len(refs) - 3) // 2
    given, (up_ref, gate_ref, *held) = refs[:count], refs[count:-2]
    copies = fetch(given, [pre_ref] + held, sems)
    me, lane = lax.axis_index("ep"), lax.axis_index("tp")
    copies[0].wait()
    for k in range(wide):
        gate_pre, up_pre = [
            by_xor(pre_ref[i, me ^ k].astype(jnp.float32), most, narrow, lane) for i in range(2)
        ]
        sig = 1.0 / (1.0 + jnp.exp(-gate_pre))
        up_ref[k] = gate_pre * sig
        gate_ref[k] = up_pre * sig * (1.0 + gate_pre * (1.0 - sig))
    for copy in copies[1:]:
        copy.wait()


def hidden_kernel(most, extra, skips, *refs):
    blocks, (down_ref, sum_ref, sent_ref) = refs[:-3], refs[-3:]
    half = down_ref.shape[1] // 2
    count = sum_ref.shape[0]
    if extra:
        blocks, row_sums = blocks[:-1], blocks[-1][...]
        high = row_sums.astype(jnp.bfloat16).astype(jnp.float32)
        spare = jnp.zeros((EXTRA - 4, row_sums.shape[1]), jnp.float32)
        tail = jnp.concatenate([high, row_sums - high, spare], axis=0)
        sent_ref[count:, :] = jnp.zeros((EXTRA, sent_ref.shape[1]), sent_ref.dtype)
        sent_ref[count:, : row_sums.shape[1]] = tail.astype(sent_ref.dtype)
    values = [b[skip:, :].astype(jnp.float32) for b, skip in zip(blocks, skips)]
    low = jnp.concatenate([v[:most] for v in values], axis=0).astype(jnp.bfloat16)
    high = jnp.concatenate([v[most : 2 * most] for v in values], axis=0).astype(jnp.bfloat16)
    total = dot(low, down_ref[:, :half], NT) + dot(high, down_ref[:, half:], NT)
    sum_ref[...] = total
    sent_ref[:count, :] = total.astype(sent_ref.dtype)


def back_kernel(most, group, sum_ref, other_ref, up_by_ref, gate_by_ref, gate_ref, up_ref, *outs):
    half = gate_ref.shape[0] // 2
    hidden = sum_ref[...] + other_ref[: sum_ref.shape[0], :].astype(jnp.float32)
    up_by, gate_by = [
        jnp.concatenate([by_ref[k] for k in group], axis=0) for by_ref in (up_by_ref, gate_by_ref)
    ]
    up_grad = (hidden * up_by).astype(jnp.bfloat16)
    gate_grad = (hidden * gate_by).astype(jnp.bfloat16)
    low = dot(gate_grad, gate_ref[:half], NT) + dot(up_grad, up_ref[:half], NT)
    high = dot(gate_grad, gate_ref[half:], NT) + dot(up_grad, up_ref[half:], NT)
    for i, out in enumerate(outs):
        part = slice(i * most, (i + 1) * most)
        pieces = [low[part], high[part]]
        spare = out.shape[0] - 2 * most
        if spare:
            pieces.append(jnp.zeros((spare, half), jnp.float32))
        out[...] = jnp.concatenate(pieces, axis=0).astype(jnp.bfloat16)


def unpack_kernel(parts, started, place_ref, *refs):
    given, out_ref = list(refs[:-1]), refs[-1]
    half = out_ref.shape[1] // 2
    blocks = {}
    for k, count in parts.items():
        rows = given.pop(0)[...].astype(jnp.float32)
        for _ in range(count - 1):
            rows += given.pop(0)[...].astype(jnp.float32)
        blocks[k] = rows.astype(jnp.bfloat16)
    for side in range(2):
        columns = slice(side * half, (side + 1) * half)
        total = given[0][:, columns].astype(jnp.float32) if started else 0.0
        for k, rows in blocks.items():
            total = total + dot(place_ref[side, k], rows, TN)
        out_ref[:, columns] = total.astype(jnp.bfloat16)


def groups_of(wide):
    if wide < 4:
        return [list(range(wide - 1, -1, -1))]
    left = list(range(wide - 2, 1, -1))
    return [[wide - 1, 0], [1]] + [left[i : i + 2] for i in range(0, len(left), 2)]


def local(
    grad_values,
    grad_scales,
    expert_ids,
    route_weights,
    w_gate,
    w_up,
    w_down,
    pre_acts,
    latent_partials,
    latent,
    latent_gain,
):
    wide, narrow = lax.axis_size("ep"), lax.axis_size("tp")
    tokens, width = grad_values.shape
    half = width // 2
    slots, hidden_width = pre_acts.shape[2:]
    most = slots // (wide * narrow)
    rows = -(-2 * most // 8) * 8
    f32, bf16 = jnp.float32, jnp.bfloat16
    block = pltpu.VMEM((rows, half), bf16)
    groups = groups_of(wide)
    order = [k for group in groups for k in group]
    partials = latent_partials.reshape(narrow, tokens, latent.shape[1])
    leading, place, *fillers = call(
        functools.partial(pack_kernel, most, order, 1),
        [
            block,
            pltpu.VMEM((2, wide, rows, tokens), bf16),
            pltpu.VMEM((1, tokens), f32),
            pltpu.VMEM((grad_scales.shape[1], tokens), f32),
            pltpu.VMEM((tokens, width), bf16),
        ],
        *pinned(
            expert_ids.reshape(1, tokens),
            route_weights.reshape(1, tokens),
            grad_scales.T,
            grad_values,
        ),
        specs=[HBM] * 4,
        scratch=[pltpu.VMEM((1, tokens), jnp.int32), pltpu.SemaphoreType.DMA((4,))],
        name="pack",
    )
    deep, parts = shares_of(tokens, latent.shape[1], half)
    more = call(
        functools.partial(pack_more_kernel, most, order[1:]),
        [block] * (wide - 1)
        + [pltpu.VMEM((deep + rows, half), bf16)] * (narrow - 1)
        + [pltpu.VMEM(latent.shape, bf16)],
        place,
        *fillers,
        *pinned(partials),
        specs=[VMEM] * 4 + [HBM],
        scratch=[pltpu.SemaphoreType.DMA((1 + (narrow - 1) * len(parts),))],
        name="pack_more",
    )
    packed = dict(zip(order, [leading, *more]))

    first, staged = groups[0][0], len(groups) > 1
    both = [swap(more[wide - 2 + j], "rows0", tp=j) for j in range(1, narrow)]
    if staged and narrow > 1:
        both[-1] = after(both[-1], place, 1 << 27)
    taken = {0: [packed[0]] + both}
    arrived = {}
    for k in order:
        if k:
            given = packed[k] if k in (first, 1) else after(packed[k], arrived[first])
            arrived[k] = swap(given, f"rows{k}", ep=k)
            if staged and k == groups[2][0]:
                arrived[k] = after(arrived[k], packed[first], 1 << 28)
    fetched = [
        pre_acts.reshape(2, wide, narrow * most, hidden_width),
        w_down[0],
        w_gate[0],
        w_up[0],
        latent,
        latent_gain.reshape(1, -1),
    ]
    factors = pltpu.VMEM((wide, narrow * most, hidden_width), f32)
    up_by, gate_by, down, gate, up, latent, latent_gain = call(
        functools.partial(fetch_kernel, most),
        [factors, factors] + [like(array) for array in fetched[1:]],
        *pinned(*fetched),
        specs=[HBM] * len(fetched),
        scratch=[like(fetched[0]), pltpu.SemaphoreType.DMA((len(fetched),))],
        earlier=[arrived[first]],
        name="fetch",
    )
    values = latent.astype(f32)
    returned = {}

    def forward(group, kind, earlier=(), row_sums=()):
        count = len(group) * narrow * most
        skips = [0 if j == 0 or k else deep for k in group for j in range(narrow)]
        summed, sent = call(
            functools.partial(hidden_kernel, most, len(row_sums), skips),
            [
                pltpu.VMEM((count, hidden_width), f32),
                pltpu.VMEM((count + EXTRA * len(row_sums), hidden_width), kind),
            ],
            *[rows_of_k for k in group for rows_of_k in taken[k]],
            *row_sums,
            down,
            name="hidden",
            earlier=earlier,
        )
        return summed, swap(sent, f"hidden{group[0]}", sub=1)

    def backward(group, summed, received):
        products = call(
            functools.partial(back_kernel, most, group),
            [block] * (len(group) * narrow),
            summed,
            received,
            up_by,
            gate_by,
            gate,
            up,
            name="back",
        )
        return {k: products[i * narrow : (i + 1) * narrow] for i, k in enumerate(group)}

    def give_back(k, products):
        total = products[0].astype(f32)
        for j in range(1, narrow):
            total += swap(products[j], f"back{k}", tp=j).astype(f32)
        total = total.astype(bf16)
        returned[k] = [swap(total, f"back{k}", ep=k)]
        return total

    def row_sums_of(both):
        own_grad = more[-1].astype(f32)
        for value in both:
            pieces = [
                value[: min(deep, tokens - at), column : column + latent.shape[1]]
                for at, column in parts
            ]
            own_grad += jnp.concatenate(pieces, axis=0).astype(f32)
        gained = own_grad * latent_gain
        return gained, jnp.stack(
            [jnp.sum(values * values, axis=1), jnp.sum(gained * values, axis=1)]
        )

    def crossed(k, rows_of_k):
        return [swap(rows_of_k, f"rows{k}", tp=j) for j in range(1, narrow)]

    for k in groups[0]:
        if k:
            taken[k] = [arrived[k]] + crossed(k, arrived[k])
    gained, row_sums = row_sums_of(both) if not staged else (None, None)
    summed, received = forward(groups[0], f32, row_sums=() if staged else [row_sums])
    products = backward(groups[0], summed, received)
    kept = products[0]
    moved = give_back(first, products[first]) if first else None
    if staged:
        first_summed, gate_open = summed, products[first][:1]
        rows_of_k = after(arrived[1], down)
        crossing = crossed(1, rows_of_k)
        crossing[-1] = after(crossing[-1], gate_open[0], 1 << 31)
        taken[1] = [rows_of_k] + crossing
        near_summed, near_received = forward([1], bf16, earlier=gate_open)
        gate_open, near = [near_summed], True
        for group in groups[2:]:
            for k in group:
                rows_of_k = after(arrived[k], first_summed) if k == group[0] else arrived[k]
                crossing = crossed(k, rows_of_k)
                crossing[-1] = after(crossing[-1], gate_open[0])
                taken[k] = [rows_of_k] + crossing
            last = group is groups[-1]
            if last:
                both[-1] = after(both[-1], first_summed)
                gained, row_sums = row_sums_of(both)
            summed, received = forward(
                group, f32, earlier=gate_open, row_sums=[row_sums] if last else ()
            )
            products = backward(group, summed, received)
            gate_open = products[group[0]][:1]
            moved = [give_back(k, products[k]) for k in group][0]
            if near:
                products = backward([1], near_summed, after(near_received, gate_open[0], 0))
                give_back(1, products[1])
                near = False
    else:
        for k in groups[0][1:-1]:
            give_back(k, products[k])
    returned[0] = [kept[0]] + [
        swap(after(kept[j], moved) if staged else kept[j], "back0", tp=j) for j in range(1, narrow)
    ]
    count = summed.shape[0]
    tail = received[count : count + 4, :tokens].astype(f32)
    row_sums = row_sums + tail[:2] + tail[2:]
    inverse_rms = lax.rsqrt(row_sums[0] / LAT + 1e-06)[:, None]
    d_latent = (
        inverse_rms * gained - values * inverse_rms**3 * row_sums[1][:, None] / LAT
    ).astype(bf16)
    latest = [1, groups[-1][0]] if staged else []
    distances = [k for k in order if k not in latest]
    (grad_input,) = call(
        functools.partial(unpack_kernel, {k: len(returned[k]) for k in distances}, False),
        [pltpu.VMEM((tokens, width), bf16) if staged else jax.ShapeDtypeStruct((tokens, width), bf16)],
        place,
        *[part for k in distances for part in returned[k]],
        name="unpack",
    )
    if staged:
        (grad_input,) = call(
            functools.partial(unpack_kernel, {k: len(returned[k]) for k in latest}, True),
            [jax.ShapeDtypeStruct((tokens, width), bf16)],
            place,
            *[part for k in latest for part in returned[k]],
            grad_input,
            name="unpack_latest",
        )
    return (grad_input, d_latent)


def solution(mesh):
    placed = (
        P(("rep", "ep", "tp"), "sub"),
        P(("rep", "ep", "tp"), "sub"),
        P(("rep", "ep", "tp"), None),
        P(("rep", "ep", "tp"), None),
        P("ep", "sub", "tp"),
        P("ep", "sub", "tp"),
        P("ep", "tp", "sub"),
        P(("rep", "ep"), None, None, "tp"),
        P("tp", ("rep", "ep"), "sub"),
        P(("rep", "ep", "tp"), "sub"),
        P("sub"),
    )
    return jax.shard_map(
        local,
        mesh=mesh,
        in_specs=placed,
        out_specs=(P(("rep", "ep", "tp"), "sub"), P(("rep", "ep", "tp"), "sub")),
        check_vma=False,
    )
```

```python
import functools

import jax
import jax.numpy as jnp
import numpy as np
from jax import lax
from jax.experimental import pallas as pl
from jax.experimental.pallas import tpu as pltpu
from jax.sharding import PartitionSpec as P

LAT = 512
NT = (((1,), (1,)), ((), ()))
TN = (((0,), (0,)), ((), ()))
VMEM = pl.BlockSpec(memory_space=pltpu.VMEM)
ANY = pl.BlockSpec(memory_space=pl.ANY)
HBM = pl.BlockSpec(memory_space=pltpu.HBM)
EXTRA = 16
VMEM_LIMIT = 20 * 1024 * 1024


def dot(a, b, dims, precision=None):
    return lax.dot_general(a, b, dims, precision=precision, preferred_element_type=jnp.float32)


def swap(value, what, **steps):
    counts = [lax.axis_size(axis) for axis in steps]
    pairs = []
    for place in np.ndindex(*counts):
        other = [index ^ step for index, step in zip(place, steps.values())]
        pairs.append(tuple(int(np.ravel_multi_index(p, counts)) for p in (place, other)))
    with jax.named_scope("_".join([what, *steps])):
        return lax.ppermute(value, tuple(steps), pairs)


def pinned(*arrays):
    return [pltpu.with_memory_space_constraint(array, pltpu.HBM) for array in arrays]


def like(array):
    return pltpu.VMEM(array.shape, array.dtype)


def call(kernel, outs, *args, cost=0, name=None, specs=None, scratch=(), earlier=()):
    specs = (specs or [VMEM] * len(args)) + [ANY] * len(earlier)
    if earlier:
        taken, body = len(args), kernel

        def kernel(*refs):
            body(*refs[:taken], *refs[taken + len(earlier) :])

    return pl.pallas_call(
        kernel,
        out_shape=outs,
        in_specs=specs,
        out_specs=[VMEM] * len(outs),
        scratch_shapes=scratch,
        compiler_params=pltpu.CompilerParams(vmem_limit_bytes=VMEM_LIMIT),
        cost_estimate=pl.CostEstimate(flops=cost, bytes_accessed=0, transcendentals=0),
        name=name,
    )(*args, *earlier)


def after(value, earlier, cost=0):
    return pl.pallas_call(
        lambda value_ref, earlier_ref, out_ref: None,
        out_shape=jax.ShapeDtypeStruct(value.shape, value.dtype),
        in_specs=[ANY, ANY],
        out_specs=ANY,
        input_output_aliases={0: 0},
        compiler_params=pltpu.CompilerParams(vmem_limit_bytes=1 << 17),
        cost_estimate=pl.CostEstimate(flops=cost, bytes_accessed=0, transcendentals=0),
        name="after",
    )(value, earlier)


def fill(block_ref, most, low, high, weights_ref, scales_ref, grad_ref):
    half, scale_half = grad_ref.shape[1] // 2, scales_ref.shape[0] // 2
    placed = jnp.dot(
        low.astype(jnp.bfloat16), grad_ref[:, :half], preferred_element_type=jnp.float32
    )
    placed += jnp.dot(
        high.astype(jnp.bfloat16), grad_ref[:, half:], preferred_element_type=jnp.float32
    )
    scale = dot(low.astype(jnp.float32), scales_ref[:scale_half], NT, lax.Precision.HIGHEST)
    scale += dot(high.astype(jnp.float32), scales_ref[scale_half:], NT, lax.Precision.HIGHEST)
    weight = jnp.sum(jnp.where(low | high, weights_ref[...], 0.0), axis=1, keepdims=True)
    for b in range(scale_half):
        part = slice(b * 128, (b + 1) * 128)
        block_ref[:, part] = (placed[:, part] * scale[:, b : b + 1] * weight).astype(jnp.bfloat16)


def fetch(sources, targets, sems, first=0):
    copies = [
        pltpu.make_async_copy(source, target, sems.at[first + i])
        for i, (source, target) in enumerate(zip(sources, targets))
    ]
    for copy in copies:
        copy.start()
    return copies


def pack_kernel(most, order, leading, *refs):
    given, refs = refs[:4], refs[4:]
    blocks, (place_ref, *held), (ids_ref, sems) = refs[:leading], refs[leading:-2], refs[-2:]
    held = [ids_ref] + held
    copies = fetch(given, held, sems)
    copies[0].wait()
    weights_ref, scales_ref, grad_ref = held[1:]
    tokens, rows = grad_ref.shape[0], blocks[0].shape[0]
    me = lax.axis_index("ep")
    ids = ids_ref[...]
    expert = lax.broadcasted_iota(jnp.int32, (max(8, len(order)), tokens), 0)
    named = expert == ids
    before = lax.broadcasted_iota(jnp.int32, (tokens, tokens), 0) < lax.broadcasted_iota(
        jnp.int32, (tokens, tokens), 1
    )
    earlier = jnp.dot(
        named.astype(jnp.bfloat16), before.astype(jnp.bfloat16), preferred_element_type=jnp.float32
    )
    position = jnp.sum(jnp.where(named, earlier, 0.0), axis=0, keepdims=True).astype(jnp.int32)
    row = lax.broadcasted_iota(jnp.int32, (rows, tokens), 0)
    found = []
    for k in order:
        local = jnp.where(ids == (me ^ k), position, -2 * rows)
        low, high = row == local, row - most == local
        found.append((low, high))
        place_ref[0, k] = low.astype(jnp.bfloat16)
        place_ref[1, k] = high.astype(jnp.bfloat16)
    for copy in copies[1:]:
        copy.wait()
    for block_ref, (low, high) in zip(blocks, found):
        fill(block_ref, most, low, high, weights_ref, scales_ref, grad_ref)


def shares_of(tokens, columns, width):
    across = width // columns
    deep = -(-tokens // across // 16) * 16
    return deep, [(at, i * columns) for i, at in enumerate(range(0, tokens, deep))]


def pack_more_kernel(most, order, place_ref, weights_ref, scales_ref, grad_ref, partial_ref, *refs):
    count, tokens, columns = partial_ref.shape
    blocks, crossing = refs[: len(order)], refs[len(order) : len(order) + count - 1]
    own_ref, sems = refs[-2:]
    lane, rows = lax.axis_index("tp"), blocks[0].shape[0]
    deep, parts = shares_of(tokens, columns, blocks[0].shape[1])
    sources, targets = [partial_ref.at[lane]], [own_ref]
    for j in range(1, count):
        for at, column in parts:
            size = min(deep, tokens - at)
            sources.append(partial_ref.at[lane ^ j, pl.ds(at, size)])
            targets.append(crossing[j - 1].at[pl.ds(0, size), pl.ds(column, columns)])
    copies = fetch(sources, targets, sems)
    for block_ref, k in zip(blocks, order):
        low, high = place_ref[0, k] != 0, place_ref[1, k] != 0
        fill(block_ref, most, low, high, weights_ref, scales_ref, grad_ref)
        if k == 0:
            for both_ref in crossing:
                both_ref[deep:, :] = block_ref[...]
    for copy in copies:
        copy.wait()


def by_xor(value, most, narrow, lane):
    step = 1
    while step < narrow:
        pieces = [value[i * most : (i + step) * most] for i in range(0, narrow, step)]
        turned = [pieces[i ^ 1] for i in range(len(pieces))]
        value = jnp.where((lane & step) != 0, jnp.concatenate(turned, axis=0), value)
        step *= 2
    return value


def fetch_kernel(most, *refs):
    pre_ref, sems = refs[-2:]
    wide = pre_ref.shape[1]
    narrow = pre_ref.shape[2] // most
    count = (len(refs) - 3) // 2
    given, (up_ref, gate_ref, *held) = refs[:count], refs[count:-2]
    copies = fetch(given, [pre_ref] + held, sems)
    me, lane = lax.axis_index("ep"), lax.axis_index("tp")
    copies[0].wait()
    for k in range(wide):
        gate_pre, up_pre = [
            by_xor(pre_ref[i, me ^ k].astype(jnp.float32), most, narrow, lane) for i in range(2)
        ]
        sig = 1.0 / (1.0 + jnp.exp(-gate_pre))
        up_ref[k] = gate_pre * sig
        gate_ref[k] = up_pre * sig * (1.0 + gate_pre * (1.0 - sig))
    for copy in copies[1:]:
        copy.wait()


def hidden_kernel(most, extra, skips, *refs):
    blocks, (down_ref, sum_ref, sent_ref) = refs[:-3], refs[-3:]
    half = down_ref.shape[1] // 2
    count = sum_ref.shape[0]
    if extra:
        blocks, row_sums = blocks[:-1], blocks[-1][...]
        high = row_sums.astype(jnp.bfloat16).astype(jnp.float32)
        spare = jnp.zeros((EXTRA - 4, row_sums.shape[1]), jnp.float32)
        tail = jnp.concatenate([high, row_sums - high, spare], axis=0)
        sent_ref[count:, :] = jnp.zeros((EXTRA, sent_ref.shape[1]), sent_ref.dtype)
        sent_ref[count:, : row_sums.shape[1]] = tail.astype(sent_ref.dtype)
    values = [b[skip:, :].astype(jnp.float32) for b, skip in zip(blocks, skips)]
    low = jnp.concatenate([v[:most] for v in values], axis=0).astype(jnp.bfloat16)
    high = jnp.concatenate([v[most : 2 * most] for v in values], axis=0).astype(jnp.bfloat16)
    total = dot(low, down_ref[:, :half], NT) + dot(high, down_ref[:, half:], NT)
    sum_ref[...] = total
    sent_ref[:count, :] = total.astype(sent_ref.dtype)


def back_kernel(most, group, sum_ref, other_ref, up_by_ref, gate_by_ref, gate_ref, up_ref, *outs):
    half = gate_ref.shape[0] // 2
    hidden = sum_ref[...] + other_ref[: sum_ref.shape[0], :].astype(jnp.float32)
    up_by, gate_by = [
        jnp.concatenate([by_ref[k] for k in group], axis=0) for by_ref in (up_by_ref, gate_by_ref)
    ]
    up_grad = (hidden * up_by).astype(jnp.bfloat16)
    gate_grad = (hidden * gate_by).astype(jnp.bfloat16)
    low = dot(gate_grad, gate_ref[:half], NT) + dot(up_grad, up_ref[:half], NT)
    high = dot(gate_grad, gate_ref[half:], NT) + dot(up_grad, up_ref[half:], NT)
    for i, out in enumerate(outs):
        part = slice(i * most, (i + 1) * most)
        pieces = [low[part], high[part]]
        spare = out.shape[0] - 2 * most
        if spare:
            pieces.append(jnp.zeros((spare, half), jnp.float32))
        out[...] = jnp.concatenate(pieces, axis=0).astype(jnp.bfloat16)


def unpack_kernel(parts, started, place_ref, *refs):
    given, out_ref = list(refs[:-1]), refs[-1]
    half = out_ref.shape[1] // 2
    blocks = {}
    for k, count in parts.items():
        rows = given.pop(0)[...].astype(jnp.float32)
        for _ in range(count - 1):
            rows += given.pop(0)[...].astype(jnp.float32)
        blocks[k] = rows.astype(jnp.bfloat16)
    for side in range(2):
        columns = slice(side * half, (side + 1) * half)
        total = given[0][:, columns].astype(jnp.float32) if started else 0.0
        for k, rows in blocks.items():
            total = total + dot(place_ref[side, k], rows, TN)
        out_ref[:, columns] = total.astype(jnp.bfloat16)


def groups_of(wide):
    if wide < 4:
        return [list(range(wide - 1, -1, -1))]
    left = list(range(wide - 2, 1, -1))
    return [[wide - 1, 0], [1]] + [left[i : i + 2] for i in range(0, len(left), 2)]


def local(
    grad_values,
    grad_scales,
    expert_ids,
    route_weights,
    w_gate,
    w_up,
    w_down,
    pre_acts,
    latent_partials,
    latent,
    latent_gain,
):
    wide, narrow = lax.axis_size("ep"), lax.axis_size("tp")
    tokens, width = grad_values.shape
    half = width // 2
    slots, hidden_width = pre_acts.shape[2:]
    most = slots // (wide * narrow)
    rows = -(-2 * most // 8) * 8
    f32, bf16 = jnp.float32, jnp.bfloat16
    block = pltpu.VMEM((rows, half), bf16)
    groups = groups_of(wide)
    order = [k for group in groups for k in group]
    partials = latent_partials.reshape(narrow, tokens, latent.shape[1])
    leading, place, *fillers = call(
        functools.partial(pack_kernel, most, order, 1),
        [
            block,
            pltpu.VMEM((2, wide, rows, tokens), bf16),
            pltpu.VMEM((1, tokens), f32),
            pltpu.VMEM((grad_scales.shape[1], tokens), f32),
            pltpu.VMEM((tokens, width), bf16),
        ],
        *pinned(
            expert_ids.reshape(1, tokens),
            route_weights.reshape(1, tokens),
            grad_scales.T,
            grad_values,
        ),
        specs=[HBM] * 4,
        scratch=[pltpu.VMEM((1, tokens), jnp.int32), pltpu.SemaphoreType.DMA((4,))],
        name="pack",
    )
    deep, parts = shares_of(tokens, latent.shape[1], half)
    more = call(
        functools.partial(pack_more_kernel, most, order[1:]),
        [block] * (wide - 1)
        + [pltpu.VMEM((deep + rows, half), bf16)] * (narrow - 1)
        + [pltpu.VMEM(latent.shape, bf16)],
        place,
        *fillers,
        *pinned(partials),
        specs=[VMEM] * 4 + [HBM],
        scratch=[pltpu.SemaphoreType.DMA((1 + (narrow - 1) * len(parts),))],
        name="pack_more",
    )
    packed = dict(zip(order, [leading, *more]))

    first, staged = groups[0][0], len(groups) > 1
    both = [swap(more[wide - 2 + j], "rows0", tp=j) for j in range(1, narrow)]
    if staged and narrow > 1:
        both[-1] = after(both[-1], place, 1 << 27)
    taken = {0: [packed[0]] + both}
    arrived = {}
    for k in order:
        if k:
            given = packed[k] if k in (first, 1) else after(packed[k], arrived[first])
            arrived[k] = swap(given, f"rows{k}", ep=k)
            if staged and k == groups[2][0]:
                arrived[k] = after(arrived[k], packed[first], 1 << 28)
    fetched = [
        pre_acts.reshape(2, wide, narrow * most, hidden_width),
        w_down[0],
        w_gate[0],
        w_up[0],
        latent,
        latent_gain.reshape(1, -1),
    ]
    factors = pltpu.VMEM((wide, narrow * most, hidden_width), f32)
    up_by, gate_by, down, gate, up, latent, latent_gain = call(
        functools.partial(fetch_kernel, most),
        [factors, factors] + [like(array) for array in fetched[1:]],
        *pinned(*fetched),
        specs=[HBM] * len(fetched),
        scratch=[like(fetched[0]), pltpu.SemaphoreType.DMA((len(fetched),))],
        earlier=[arrived[first]],
        name="fetch",
    )
    values = latent.astype(f32)
    returned = {}

    def forward(group, kind, earlier=(), row_sums=()):
        count = len(group) * narrow * most
        skips = [0 if j == 0 or k else deep for k in group for j in range(narrow)]
        summed, sent = call(
            functools.partial(hidden_kernel, most, len(row_sums), skips),
            [
                pltpu.VMEM((count, hidden_width), f32),
                pltpu.VMEM((count + EXTRA * len(row_sums), hidden_width), kind),
            ],
            *[rows_of_k for k in group for rows_of_k in taken[k]],
            *row_sums,
            down,
            name="hidden",
            earlier=earlier,
        )
        return summed, swap(sent, f"hidden{group[0]}", sub=1)

    def backward(group, summed, received):
        products = call(
            functools.partial(back_kernel, most, group),
            [block] * (len(group) * narrow),
            summed,
            received,
            up_by,
            gate_by,
            gate,
            up,
            name="back",
        )
        return {k: products[i * narrow : (i + 1) * narrow] for i, k in enumerate(group)}

    def give_back(k, products):
        total = products[0].astype(f32)
        for j in range(1, narrow):
            total += swap(products[j], f"back{k}", tp=j).astype(f32)
        total = total.astype(bf16)
        returned[k] = [swap(total, f"back{k}", ep=k)]
        return total

    def row_sums_of(both):
        own_grad = more[-1].astype(f32)
        for value in both:
            pieces = [
                value[: min(deep, tokens - at), column : column + latent.shape[1]]
                for at, column in parts
            ]
            own_grad += jnp.concatenate(pieces, axis=0).astype(f32)
        gained = own_grad * latent_gain
        return gained, jnp.stack(
            [jnp.sum(values * values, axis=1), jnp.sum(gained * values, axis=1)]
        )

    def crossed(k, rows_of_k):
        return [swap(rows_of_k, f"rows{k}", tp=j) for j in range(1, narrow)]

    for k in groups[0]:
        if k:
            taken[k] = [arrived[k]] + crossed(k, arrived[k])
    gained, row_sums = row_sums_of(both) if not staged else (None, None)
    summed, received = forward(groups[0], f32, row_sums=() if staged else [row_sums])
    products = backward(groups[0], summed, received)
    kept = products[0]
    moved = give_back(first, products[first]) if first else None
    if staged:
        first_summed, gate_open = summed, products[first][:1]
        rows_of_k = after(arrived[1], down)
        crossing = crossed(1, rows_of_k)
        crossing[-1] = after(crossing[-1], gate_open[0], 1 << 31)
        taken[1] = [rows_of_k] + crossing
        near_summed, near_received = forward([1], bf16, earlier=gate_open)
        gate_open, near = [near_summed], True
        for group in groups[2:]:
            for k in group:
                rows_of_k = after(arrived[k], first_summed) if k == group[0] else arrived[k]
                crossing = crossed(k, rows_of_k)
                crossing[-1] = after(crossing[-1], gate_open[0])
                taken[k] = [rows_of_k] + crossing
            last = group is groups[-1]
            if last:
                both[-1] = after(both[-1], first_summed)
                gained, row_sums = row_sums_of(both)
            summed, received = forward(
                group, f32, earlier=gate_open, row_sums=[row_sums] if last else ()
            )
            products = backward(group, summed, received)
            gate_open = products[group[0]][:1]
            moved = [give_back(k, products[k]) for k in group][0]
            if near:
                products = backward([1], near_summed, after(near_received, gate_open[0], 0))
                give_back(1, products[1])
                near = False
    else:
        for k in groups[0][1:-1]:
            give_back(k, products[k])
    returned[0] = [kept[0]] + [
        swap(after(kept[j], summed) if staged else kept[j], "back0", tp=j) for j in range(1, narrow)
    ]
    count = summed.shape[0]
    tail = received[count : count + 4, :tokens].astype(f32)
    row_sums = row_sums + tail[:2] + tail[2:]
    inverse_rms = lax.rsqrt(row_sums[0] / LAT + 1e-06)[:, None]
    d_latent = (
        inverse_rms * gained - values * inverse_rms**3 * row_sums[1][:, None] / LAT
    ).astype(bf16)
    latest = [1, groups[-1][0]] if staged else []
    distances = [k for k in order if k not in latest]
    (grad_input,) = call(
        functools.partial(unpack_kernel, {k: len(returned[k]) for k in distances}, False),
        [pltpu.VMEM((tokens, width), bf16) if staged else jax.ShapeDtypeStruct((tokens, width), bf16)],
        place,
        *[part for k in distances for part in returned[k]],
        name="unpack",
    )
    if staged:
        (grad_input,) = call(
            functools.partial(unpack_kernel, {k: len(returned[k]) for k in latest}, True),
            [jax.ShapeDtypeStruct((tokens, width), bf16)],
            place,
            *[part for k in latest for part in returned[k]],
            grad_input,
            name="unpack_latest",
        )
    return (grad_input, d_latent)


def solution(mesh):
    placed = (
        P(("rep", "ep", "tp"), "sub"),
        P(("rep", "ep", "tp"), "sub"),
        P(("rep", "ep", "tp"), None),
        P(("rep", "ep", "tp"), None),
        P("ep", "sub", "tp"),
        P("ep", "sub", "tp"),
        P("ep", "tp", "sub"),
        P(("rep", "ep"), None, None, "tp"),
        P("tp", ("rep", "ep"), "sub"),
        P(("rep", "ep", "tp"), "sub"),
        P("sub"),
    )
    return jax.shard_map(
        local,
        mesh=mesh,
        in_specs=placed,
        out_specs=(P(("rep", "ep", "tp"), "sub"), P(("rep", "ep", "tp"), "sub")),
        check_vma=False,
    )
```

```python
import functools

import jax
import jax.numpy as jnp
from jax import lax
from jax.experimental import pallas as pl
from jax.experimental.pallas import tpu as pltpu
from jax.sharding import PartitionSpec as P

LAT = 512
NT = (((1,), (1,)), ((), ()))
TN = (((0,), (0,)), ((), ()))
VMEM = pl.BlockSpec(memory_space=pltpu.VMEM)
ANY = pl.BlockSpec(memory_space=pl.ANY)
HBM = pl.BlockSpec(memory_space=pltpu.HBM)
EXTRA = 16
VMEM_LIMIT = 20 * 1024 * 1024


def dot(a, b, dims, precision=None):
    return lax.dot_general(a, b, dims, precision=precision, preferred_element_type=jnp.float32)


def swap(value, axis, step, what):
    count = lax.axis_size(axis)
    with jax.named_scope(f"{what}_{axis}"):
        return lax.ppermute(value, axis, [(i, i ^ step) for i in range(count)])


def pinned(*arrays):
    return [pltpu.with_memory_space_constraint(array, pltpu.HBM) for array in arrays]


def like(array):
    return pltpu.VMEM(array.shape, array.dtype)


def call(kernel, outs, *args, cost=0, name=None, specs=None, outs_in=VMEM, scratch=(), earlier=()):
    specs = (specs or [VMEM] * len(args)) + [ANY] * len(earlier)
    if earlier:
        taken, body = len(args), kernel

        def kernel(*refs):
            body(*refs[:taken], *refs[taken + len(earlier) :])

    return pl.pallas_call(
        kernel,
        out_shape=outs,
        in_specs=specs,
        out_specs=[outs_in] * len(outs),
        scratch_shapes=scratch,
        compiler_params=pltpu.CompilerParams(vmem_limit_bytes=VMEM_LIMIT),
        cost_estimate=pl.CostEstimate(flops=cost, bytes_accessed=0, transcendentals=0),
        name=name,
    )(*args, *earlier)


def after(value, earlier, cost=0):
    return pl.pallas_call(
        lambda value_ref, earlier_ref, out_ref: None,
        out_shape=jax.ShapeDtypeStruct(value.shape, value.dtype),
        in_specs=[ANY, ANY],
        out_specs=ANY,
        input_output_aliases={0: 0},
        compiler_params=pltpu.CompilerParams(vmem_limit_bytes=1 << 17),
        cost_estimate=pl.CostEstimate(flops=cost, bytes_accessed=0, transcendentals=0),
        name="after",
    )(value, earlier)


def fill(block_ref, most, low, high, weights_ref, scales_ref, grad_ref):
    half, scale_half = grad_ref.shape[1] // 2, scales_ref.shape[0] // 2
    placed = jnp.dot(
        low.astype(jnp.bfloat16), grad_ref[:, :half], preferred_element_type=jnp.float32
    )
    placed += jnp.dot(
        high.astype(jnp.bfloat16), grad_ref[:, half:], preferred_element_type=jnp.float32
    )
    scale = dot(low.astype(jnp.float32), scales_ref[:scale_half], NT, lax.Precision.HIGHEST)
    scale += dot(high.astype(jnp.float32), scales_ref[scale_half:], NT, lax.Precision.HIGHEST)
    weight = jnp.sum(jnp.where(low | high, weights_ref[...], 0.0), axis=1, keepdims=True)
    for b in range(scale_half):
        part = slice(b * 128, (b + 1) * 128)
        block_ref[:, part] = (placed[:, part] * scale[:, b : b + 1] * weight).astype(jnp.bfloat16)


def fetch(sources, targets, sems, first=0):
    copies = [
        pltpu.make_async_copy(source, target, sems.at[first + i])
        for i, (source, target) in enumerate(zip(sources, targets))
    ]
    for copy in copies:
        copy.start()
    return copies


def pack_kernel(most, order, *refs):
    given, partial_ref, refs = refs[:4], refs[4], refs[5:]
    blocks, (place_ref, share_ref), refs = refs[: len(order)], refs[len(order) :][:2], refs[-6:]
    held, sems, share_sems = refs[:4], refs[4], refs[5]
    lane, count = lax.axis_index("tp"), partial_ref.shape[0]
    copies = fetch(given, held, sems)
    shares = fetch(
        [partial_ref.at[lane ^ j] for j in range(count)],
        [share_ref.at[j] for j in range(count)],
        share_sems,
    )
    copies[0].wait()
    ids_ref, weights_ref, scales_ref, grad_ref = held
    tokens, rows = grad_ref.shape[0], blocks[0].shape[0]
    me = lax.axis_index("ep")
    ids = ids_ref[...]
    expert = lax.broadcasted_iota(jnp.int32, (max(8, len(order)), tokens), 0)
    named = expert == ids
    before = lax.broadcasted_iota(jnp.int32, (tokens, tokens), 0) < lax.broadcasted_iota(
        jnp.int32, (tokens, tokens), 1
    )
    earlier = jnp.dot(
        named.astype(jnp.bfloat16), before.astype(jnp.bfloat16), preferred_element_type=jnp.float32
    )
    position = jnp.sum(jnp.where(named, earlier, 0.0), axis=0, keepdims=True).astype(jnp.int32)
    row = lax.broadcasted_iota(jnp.int32, (rows, tokens), 0)
    found = []
    for k in order:
        local = jnp.where(ids == (me ^ k), position, -2 * rows)
        low, high = row == local, row - most == local
        found.append((low, high))
        place_ref[0, k] = low.astype(jnp.bfloat16)
        place_ref[1, k] = high.astype(jnp.bfloat16)
    for copy in copies[1:]:
        copy.wait()
    for block_ref, (low, high) in zip(blocks, found):
        fill(block_ref, most, low, high, weights_ref, scales_ref, grad_ref)
    for copy in shares:
        copy.wait()


def by_xor(value, most, narrow, lane):
    step = 1
    while step < narrow:
        pieces = [value[i * most : (i + step) * most] for i in range(0, narrow, step)]
        turned = [pieces[i ^ 1] for i in range(len(pieces))]
        value = jnp.where((lane & step) != 0, jnp.concatenate(turned, axis=0), value)
        step *= 2
    return value


def fetch_kernel(most, *refs):
    pre_ref, sems = refs[-2:]
    wide = pre_ref.shape[1]
    narrow = pre_ref.shape[2] // most
    count = (len(refs) - 3) // 2
    given, (up_ref, gate_ref, *held) = refs[:count], refs[count:-2]
    copies = fetch(given, [pre_ref] + held, sems)
    me, lane = lax.axis_index("ep"), lax.axis_index("tp")
    copies[0].wait()
    for k in range(wide):
        gate_pre, up_pre = [
            by_xor(pre_ref[i, me ^ k].astype(jnp.float32), most, narrow, lane) for i in range(2)
        ]
        sig = 1.0 / (1.0 + jnp.exp(-gate_pre))
        up_ref[k] = gate_pre * sig
        gate_ref[k] = up_pre * sig * (1.0 + gate_pre * (1.0 - sig))
    for copy in copies[1:]:
        copy.wait()


def hidden_kernel(most, extra, *refs):
    blocks, (down_ref, sum_ref, sent_ref) = refs[:-3], refs[-3:]
    half = down_ref.shape[1] // 2
    count = sum_ref.shape[0]
    if extra:
        blocks, row_sums = blocks[:-1], blocks[-1][...]
        high = row_sums.astype(jnp.bfloat16).astype(jnp.float32)
        spare = jnp.zeros((EXTRA - 4, row_sums.shape[1]), jnp.float32)
        tail = jnp.concatenate([high, row_sums - high, spare], axis=0)
        sent_ref[count:, :] = jnp.zeros((EXTRA, sent_ref.shape[1]), jnp.bfloat16)
        sent_ref[count:, : row_sums.shape[1]] = tail.astype(jnp.bfloat16)
    values = [b[...].astype(jnp.float32) for b in blocks]
    low = jnp.concatenate([v[:most] for v in values], axis=0).astype(jnp.bfloat16)
    high = jnp.concatenate([v[most : 2 * most] for v in values], axis=0).astype(jnp.bfloat16)
    total = dot(low, down_ref[:, :half], NT) + dot(high, down_ref[:, half:], NT)
    sum_ref[...] = total
    sent_ref[:count, :] = total.astype(jnp.bfloat16)


def back_kernel(most, group, sum_ref, other_ref, up_by_ref, gate_by_ref, gate_ref, up_ref, *outs):
    half = gate_ref.shape[0] // 2
    hidden = sum_ref[...] + other_ref[: sum_ref.shape[0], :].astype(jnp.float32)
    up_by, gate_by = [
        jnp.concatenate([by_ref[k] for k in group], axis=0) for by_ref in (up_by_ref, gate_by_ref)
    ]
    up_grad = (hidden * up_by).astype(jnp.bfloat16)
    gate_grad = (hidden * gate_by).astype(jnp.bfloat16)
    low = dot(gate_grad, gate_ref[:half], NT) + dot(up_grad, up_ref[:half], NT)
    high = dot(gate_grad, gate_ref[half:], NT) + dot(up_grad, up_ref[half:], NT)
    for i, out in enumerate(outs):
        part = slice(i * most, (i + 1) * most)
        pieces = [low[part], high[part]]
        spare = out.shape[0] - 2 * most
        if spare:
            pieces.append(jnp.zeros((spare, half), jnp.float32))
        out[...] = jnp.concatenate(pieces, axis=0).astype(jnp.bfloat16)


def unpack_kernel(distances, started, place_ref, *refs):
    if started:
        refs, held_ref, sems = refs[:-2], refs[-2], refs[-1]
    blocks, others, out_ref = refs[: len(distances)], refs[len(distances) : -1], refs[-1]
    if started:
        others, so_far_ref = others[:-1], others[-1]
    half = out_ref.shape[1] // 2
    copies = []
    for side in range(2):
        columns = slice(side * half, (side + 1) * half)
        total = so_far_ref[:, columns].astype(jnp.float32) if started else 0.0
        for k, block_ref in zip(distances, blocks):
            rows = block_ref[...]
            if k == 0:
                rows = rows.astype(jnp.float32)
                for other_ref in others:
                    rows += other_ref[...].astype(jnp.float32)
                rows = rows.astype(jnp.bfloat16)
            total = total + dot(place_ref[side, k], rows, TN)
        if started:
            held_ref[side] = total.astype(jnp.bfloat16)
            copies.append(
                pltpu.make_async_copy(
                    held_ref.at[side], out_ref.at[:, pl.ds(side * half, half)], sems.at[side]
                )
            )
            copies[-1].start()
        else:
            out_ref[:, columns] = total.astype(jnp.bfloat16)
    for copy in copies:
        copy.wait()


def groups_of(wide):
    if wide < 4:
        return [list(range(wide - 1, -1, -1))]
    left = list(range(wide - 2, 1, -1))
    return [[wide - 1, 1, 0]] + [left[i : i + 2] for i in range(0, len(left), 2)]


def local(
    grad_values,
    grad_scales,
    expert_ids,
    route_weights,
    w_gate,
    w_up,
    w_down,
    pre_acts,
    latent_partials,
    latent,
    latent_gain,
):
    wide, narrow = lax.axis_size("ep"), lax.axis_size("tp")
    tokens, width = grad_values.shape
    half = width // 2
    slots, hidden_width = pre_acts.shape[2:]
    most = slots // (wide * narrow)
    rows = -(-2 * most // 8) * 8
    f32, bf16 = jnp.float32, jnp.bfloat16
    block = pltpu.VMEM((rows, half), bf16)
    groups = groups_of(wide)
    order = [k for group in groups for k in group]
    partials = latent_partials.reshape(narrow, tokens, latent.shape[1])
    packed = call(
        functools.partial(pack_kernel, most, order),
        [block] * wide + [pltpu.VMEM((2, wide, rows, tokens), bf16), like(partials)],
        *pinned(
            expert_ids.reshape(1, tokens),
            route_weights.reshape(1, tokens),
            grad_scales.T,
            grad_values,
            partials,
        ),
        specs=[HBM] * 5,
        scratch=[
            pltpu.VMEM((1, tokens), jnp.int32),
            pltpu.VMEM((1, tokens), f32),
            pltpu.VMEM((grad_scales.shape[1], tokens), f32),
            pltpu.VMEM((tokens, width), bf16),
            pltpu.SemaphoreType.DMA((4,)),
            pltpu.SemaphoreType.DMA((narrow,)),
        ],
        name="pack",
    )
    place, shares = packed[wide:]
    packed = dict(zip(order, packed))

    def across(k, rows_of_k):
        return [rows_of_k] + [swap(rows_of_k, "tp", j, f"rows{k}") for j in range(1, narrow)]

    taken = {0: across(0, packed[0])}
    first = groups[0][0]
    arrived = {}
    for k in order:
        if k:
            given = packed[k] if k in groups[0] else after(packed[k], arrived[first])
            arrived[k] = swap(given, "ep", k, f"rows{k}")
            if len(groups) > 1 and k == groups[1][0]:
                arrived[k] = after(arrived[k], packed[first], 1 << 31)
    fetched = [
        pre_acts.reshape(2, wide, narrow * most, hidden_width),
        w_down[0],
        w_gate[0],
        w_up[0],
        latent,
        latent_gain.reshape(1, -1),
    ]
    factors = pltpu.VMEM((wide, narrow * most, hidden_width), f32)
    up_by, gate_by, down, gate, up, latent, latent_gain = call(
        functools.partial(fetch_kernel, most),
        [factors, factors] + [like(array) for array in fetched[1:]],
        *pinned(*fetched),
        specs=[HBM] * len(fetched),
        scratch=[like(fetched[0]), pltpu.SemaphoreType.DMA((len(fetched),))],
        earlier=[arrived[first]],
        name="fetch",
    )
    latent_parts = [shares[0]] + [
        swap(shares[j], "tp", j, "latent") for j in range(1, narrow)
    ]

    def give_back(k, mine, others):
        others = [swap(other, "tp", j + 1, f"back{k}") for j, other in enumerate(others)]
        total = mine.astype(f32)
        for other in others:
            total += other.astype(f32)
        total = total.astype(bf16)
        return total, swap(total, "ep", k, f"back{k}")

    returned = {}
    own, waiting = [], []
    values = latent.astype(f32)
    received, products, moved = None, None, None
    for group in groups:
        for k in group:
            if k == 0:
                continue
            taken[k] = across(k, arrived[k])
            if received is not None:
                taken[k][-1] = after(taken[k][-1], products[0])
            elif k != first and narrow > 1:
                taken[k][-1] = after(taken[k][-1], packed[first], 1 << 31)
        count = len(group) * narrow * most
        extra = group is groups[-1]
        if extra:
            if received is not None:
                latent_parts[-1] = after(latent_parts[-1], summed, 1 << 30)
            own_grad = sum(part.astype(f32) for part in latent_parts)
            gained = own_grad * latent_gain
            row_sums = jnp.stack(
                [jnp.sum(values * values, axis=1), jnp.sum(gained * values, axis=1)]
            )
        summed, sent = call(
            functools.partial(hidden_kernel, most, extra),
            [
                pltpu.VMEM((count, hidden_width), f32),
                pltpu.VMEM((count + (EXTRA if extra else 0), hidden_width), bf16),
            ],
            *[rows_of_k for k in group for rows_of_k in taken[k]],
            *([row_sums] if extra else []),
            down,
            name="hidden",
            earlier=products[:1] if products else (),
        )
        for k, mine, others in waiting:
            others = [after(other, summed) for other in others]
            returned[k] = give_back(k, mine, others)[1]
        waiting = []
        received = swap(sent, "sub", 1, f"hidden{group[0]}")
        if moved is not None:
            received = after(received, moved)
        products = call(
            functools.partial(back_kernel, most, group),
            [block] * (len(group) * narrow),
            summed,
            received,
            up_by,
            gate_by,
            gate,
            up,
            name="back",
        )
        for at, k in enumerate(group):
            mine, others = products[at * narrow], products[at * narrow + 1 : (at + 1) * narrow]
            if k == 0:
                returned[0], own = mine, others
            elif k != group[0] and not extra:
                waiting.append((k, mine, others))
            else:
                total, returned[k] = give_back(k, mine, others)
                if k == group[0]:
                    moved = total
    own = [swap(after(value, moved), "tp", j + 1, "back0") for j, value in enumerate(own)]
    tail = received[count : count + 4, :tokens].astype(f32)
    row_sums = row_sums + tail[:2] + tail[2:]
    inverse_rms = lax.rsqrt(row_sums[0] / LAT + 1e-06)[:, None]
    d_latent = (
        inverse_rms * gained - values * inverse_rms**3 * row_sums[1][:, None] / LAT
    ).astype(bf16)
    latest = groups[-1][:1] if len(groups) > 1 else []
    distances = [k for k in sorted(returned, reverse=True) if k not in latest]
    (grad_input,) = call(
        functools.partial(unpack_kernel, distances, False),
        [pltpu.VMEM((tokens, width), bf16) if latest else jax.ShapeDtypeStruct((tokens, width), bf16)],
        place,
        *[returned[k] for k in distances],
        *own,
        name="unpack",
    )
    if latest:
        (grad_input,) = call(
            functools.partial(unpack_kernel, latest, True),
            [jax.ShapeDtypeStruct((tokens, width), bf16)],
            place,
            *[returned[k] for k in latest],
            grad_input,
            outs_in=ANY,
            scratch=[pltpu.VMEM((2, tokens, half), bf16), pltpu.SemaphoreType.DMA((2,))],
            name="unpack_latest",
        )
    return (grad_input, d_latent)


def solution(mesh):
    placed = (
        P(("rep", "ep", "tp"), "sub"),
        P(("rep", "ep", "tp"), "sub"),
        P(("rep", "ep", "tp"), None),
        P(("rep", "ep", "tp"), None),
        P("ep", "sub", "tp"),
        P("ep", "sub", "tp"),
        P("ep", "tp", "sub"),
        P(("rep", "ep"), None, None, "tp"),
        P("tp", ("rep", "ep"), "sub"),
        P(("rep", "ep", "tp"), "sub"),
        P("sub"),
    )
    return jax.shard_map(
        local,
        mesh=mesh,
        in_specs=placed,
        out_specs=(P(("rep", "ep", "tp"), "sub"), P(("rep", "ep", "tp"), "sub")),
        check_vma=False,
    )
```

```python
import functools

import jax
import jax.numpy as jnp
from jax import lax
from jax.experimental import pallas as pl
from jax.experimental.pallas import tpu as pltpu
from jax.sharding import PartitionSpec as P

LAT = 512
NT = (((1,), (1,)), ((), ()))
TN = (((0,), (0,)), ((), ()))
VMEM = pl.BlockSpec(memory_space=pltpu.VMEM)
ANY = pl.BlockSpec(memory_space=pl.ANY)
HBM = pl.BlockSpec(memory_space=pltpu.HBM)
EXTRA = 16
LEADING = 2
VMEM_LIMIT = 20 * 1024 * 1024


def dot(a, b, dims, precision=None):
    return lax.dot_general(a, b, dims, precision=precision, preferred_element_type=jnp.float32)


def swap(value, axis, step, what):
    count = lax.axis_size(axis)
    with jax.named_scope(f"{what}_{axis}"):
        return lax.ppermute(value, axis, [(i, i ^ step) for i in range(count)])


def pinned(*arrays):
    return [pltpu.with_memory_space_constraint(array, pltpu.HBM) for array in arrays]


def like(array):
    return pltpu.VMEM(array.shape, array.dtype)


def call(kernel, outs, *args, cost=0, name=None, specs=None, outs_in=VMEM, scratch=(), earlier=()):
    specs = (specs or [VMEM] * len(args)) + [ANY] * len(earlier)
    if earlier:
        taken, body = len(args), kernel

        def kernel(*refs):
            body(*refs[:taken], *refs[taken + len(earlier) :])

    return pl.pallas_call(
        kernel,
        out_shape=outs,
        in_specs=specs,
        out_specs=[outs_in] * len(outs),
        scratch_shapes=scratch,
        compiler_params=pltpu.CompilerParams(vmem_limit_bytes=VMEM_LIMIT),
        cost_estimate=pl.CostEstimate(flops=cost, bytes_accessed=0, transcendentals=0),
        name=name,
    )(*args, *earlier)


def after(value, earlier, cost=0):
    return pl.pallas_call(
        lambda value_ref, earlier_ref, out_ref: None,
        out_shape=jax.ShapeDtypeStruct(value.shape, value.dtype),
        in_specs=[ANY, ANY],
        out_specs=ANY,
        input_output_aliases={0: 0},
        compiler_params=pltpu.CompilerParams(vmem_limit_bytes=1 << 17),
        cost_estimate=pl.CostEstimate(flops=cost, bytes_accessed=0, transcendentals=0),
        name="after",
    )(value, earlier)


def fill(block_ref, most, low, high, weights_ref, scales_ref, grad_ref):
    half, scale_half = grad_ref.shape[1] // 2, scales_ref.shape[0] // 2
    placed = jnp.dot(
        low.astype(jnp.bfloat16), grad_ref[:, :half], preferred_element_type=jnp.float32
    )
    placed += jnp.dot(
        high.astype(jnp.bfloat16), grad_ref[:, half:], preferred_element_type=jnp.float32
    )
    scale = dot(low.astype(jnp.float32), scales_ref[:scale_half], NT, lax.Precision.HIGHEST)
    scale += dot(high.astype(jnp.float32), scales_ref[scale_half:], NT, lax.Precision.HIGHEST)
    weight = jnp.sum(jnp.where(low | high, weights_ref[...], 0.0), axis=1, keepdims=True)
    for b in range(scale_half):
        part = slice(b * 128, (b + 1) * 128)
        block_ref[:, part] = (placed[:, part] * scale[:, b : b + 1] * weight).astype(jnp.bfloat16)


def fetch(sources, targets, sems, first=0):
    copies = [
        pltpu.make_async_copy(source, target, sems.at[first + i])
        for i, (source, target) in enumerate(zip(sources, targets))
    ]
    for copy in copies:
        copy.start()
    return copies


def pack_kernel(most, order, leading, *refs):
    given, refs = refs[:4], refs[4:]
    blocks, (place_ref, *held), (ids_ref, sems) = refs[:leading], refs[leading:-2], refs[-2:]
    held = [ids_ref] + held
    copies = fetch(given, held, sems)
    copies[0].wait()
    weights_ref, scales_ref, grad_ref = held[1:]
    tokens, rows = grad_ref.shape[0], blocks[0].shape[0]
    me = lax.axis_index("ep")
    ids = ids_ref[...]
    expert = lax.broadcasted_iota(jnp.int32, (max(8, len(order)), tokens), 0)
    named = expert == ids
    before = lax.broadcasted_iota(jnp.int32, (tokens, tokens), 0) < lax.broadcasted_iota(
        jnp.int32, (tokens, tokens), 1
    )
    earlier = jnp.dot(
        named.astype(jnp.bfloat16), before.astype(jnp.bfloat16), preferred_element_type=jnp.float32
    )
    position = jnp.sum(jnp.where(named, earlier, 0.0), axis=0, keepdims=True).astype(jnp.int32)
    row = lax.broadcasted_iota(jnp.int32, (rows, tokens), 0)
    found = []
    for k in order:
        local = jnp.where(ids == (me ^ k), position, -2 * rows)
        low, high = row == local, row - most == local
        found.append((low, high))
        place_ref[0, k] = low.astype(jnp.bfloat16)
        place_ref[1, k] = high.astype(jnp.bfloat16)
    for copy in copies[1:]:
        copy.wait()
    for block_ref, (low, high) in zip(blocks, found):
        fill(block_ref, most, low, high, weights_ref, scales_ref, grad_ref)


def pack_more_kernel(most, order, place_ref, weights_ref, scales_ref, grad_ref, partial_ref, *refs):
    blocks, (share_ref, sems) = refs[:-2], refs[-2:]
    lane, count = lax.axis_index("tp"), partial_ref.shape[0]
    shares = fetch(
        [partial_ref.at[lane ^ j] for j in range(count)],
        [share_ref.at[j] for j in range(count)],
        sems,
    )
    for block_ref, k in zip(blocks, order):
        low, high = place_ref[0, k] != 0, place_ref[1, k] != 0
        fill(block_ref, most, low, high, weights_ref, scales_ref, grad_ref)
    for copy in shares:
        copy.wait()


def by_xor(value, most, narrow, lane):
    step = 1
    while step < narrow:
        pieces = [value[i * most : (i + step) * most] for i in range(0, narrow, step)]
        turned = [pieces[i ^ 1] for i in range(len(pieces))]
        value = jnp.where((lane & step) != 0, jnp.concatenate(turned, axis=0), value)
        step *= 2
    return value


def fetch_kernel(most, *refs):
    pre_ref, sems = refs[-2:]
    wide = pre_ref.shape[1]
    narrow = pre_ref.shape[2] // most
    count = (len(refs) - 3) // 2
    given, (up_ref, gate_ref, *held) = refs[:count], refs[count:-2]
    copies = fetch(given, [pre_ref] + held, sems)
    me, lane = lax.axis_index("ep"), lax.axis_index("tp")
    copies[0].wait()
    for k in range(wide):
        gate_pre, up_pre = [
            by_xor(pre_ref[i, me ^ k].astype(jnp.float32), most, narrow, lane) for i in range(2)
        ]
        sig = 1.0 / (1.0 + jnp.exp(-gate_pre))
        up_ref[k] = gate_pre * sig
        gate_ref[k] = up_pre * sig * (1.0 + gate_pre * (1.0 - sig))
    for copy in copies[1:]:
        copy.wait()


def hidden_kernel(most, extra, *refs):
    blocks, (down_ref, sum_ref, sent_ref) = refs[:-3], refs[-3:]
    half = down_ref.shape[1] // 2
    count = sum_ref.shape[0]
    if extra:
        blocks, row_sums = blocks[:-1], blocks[-1][...]
        high = row_sums.astype(jnp.bfloat16).astype(jnp.float32)
        spare = jnp.zeros((EXTRA - 4, row_sums.shape[1]), jnp.float32)
        tail = jnp.concatenate([high, row_sums - high, spare], axis=0)
        sent_ref[count:, :] = jnp.zeros((EXTRA, sent_ref.shape[1]), jnp.bfloat16)
        sent_ref[count:, : row_sums.shape[1]] = tail.astype(jnp.bfloat16)
    values = [b[...].astype(jnp.float32) for b in blocks]
    low = jnp.concatenate([v[:most] for v in values], axis=0).astype(jnp.bfloat16)
    high = jnp.concatenate([v[most : 2 * most] for v in values], axis=0).astype(jnp.bfloat16)
    total = dot(low, down_ref[:, :half], NT) + dot(high, down_ref[:, half:], NT)
    sum_ref[...] = total
    sent_ref[:count, :] = total.astype(jnp.bfloat16)


def back_kernel(most, group, sum_ref, other_ref, up_by_ref, gate_by_ref, gate_ref, up_ref, *outs):
    half = gate_ref.shape[0] // 2
    hidden = sum_ref[...] + other_ref[: sum_ref.shape[0], :].astype(jnp.float32)
    up_by, gate_by = [
        jnp.concatenate([by_ref[k] for k in group], axis=0) for by_ref in (up_by_ref, gate_by_ref)
    ]
    up_grad = (hidden * up_by).astype(jnp.bfloat16)
    gate_grad = (hidden * gate_by).astype(jnp.bfloat16)
    low = dot(gate_grad, gate_ref[:half], NT) + dot(up_grad, up_ref[:half], NT)
    high = dot(gate_grad, gate_ref[half:], NT) + dot(up_grad, up_ref[half:], NT)
    for i, out in enumerate(outs):
        part = slice(i * most, (i + 1) * most)
        pieces = [low[part], high[part]]
        spare = out.shape[0] - 2 * most
        if spare:
            pieces.append(jnp.zeros((spare, half), jnp.float32))
        out[...] = jnp.concatenate(pieces, axis=0).astype(jnp.bfloat16)


def unpack_kernel(distances, started, place_ref, *refs):
    if started:
        refs, held_ref, sems = refs[:-2], refs[-2], refs[-1]
    blocks, others, out_ref = refs[: len(distances)], refs[len(distances) : -1], refs[-1]
    if started:
        others, so_far_ref = others[:-1], others[-1]
    half = out_ref.shape[1] // 2
    copies = []
    for side in range(2):
        columns = slice(side * half, (side + 1) * half)
        total = so_far_ref[:, columns].astype(jnp.float32) if started else 0.0
        for k, block_ref in zip(distances, blocks):
            rows = block_ref[...]
            if k == 0:
                rows = rows.astype(jnp.float32)
                for other_ref in others:
                    rows += other_ref[...].astype(jnp.float32)
                rows = rows.astype(jnp.bfloat16)
            total = total + dot(place_ref[side, k], rows, TN)
        if started:
            held_ref[side] = total.astype(jnp.bfloat16)
            copies.append(
                pltpu.make_async_copy(
                    held_ref.at[side], out_ref.at[:, pl.ds(side * half, half)], sems.at[side]
                )
            )
            copies[-1].start()
        else:
            out_ref[:, columns] = total.astype(jnp.bfloat16)
    for copy in copies:
        copy.wait()


def groups_of(wide):
    if wide < 4:
        return [list(range(wide - 1, -1, -1))]
    left = list(range(wide - 2, 1, -1))
    return [[wide - 1, 1, 0]] + [left[i : i + 2] for i in range(0, len(left), 2)]


def local(
    grad_values,
    grad_scales,
    expert_ids,
    route_weights,
    w_gate,
    w_up,
    w_down,
    pre_acts,
    latent_partials,
    latent,
    latent_gain,
):
    wide, narrow = lax.axis_size("ep"), lax.axis_size("tp")
    tokens, width = grad_values.shape
    half = width // 2
    slots, hidden_width = pre_acts.shape[2:]
    most = slots // (wide * narrow)
    rows = -(-2 * most // 8) * 8
    f32, bf16 = jnp.float32, jnp.bfloat16
    block = pltpu.VMEM((rows, half), bf16)
    groups = groups_of(wide)
    order = [k for group in groups for k in group]
    partials = latent_partials.reshape(narrow, tokens, latent.shape[1])
    *leading, place, weights, scales, grads = call(
        functools.partial(pack_kernel, most, order, LEADING),
        [block] * LEADING
        + [
            pltpu.VMEM((2, wide, rows, tokens), bf16),
            pltpu.VMEM((1, tokens), f32),
            pltpu.VMEM((grad_scales.shape[1], tokens), f32),
            pltpu.VMEM((tokens, width), bf16),
        ],
        *pinned(
            expert_ids.reshape(1, tokens),
            route_weights.reshape(1, tokens),
            grad_scales.T,
            grad_values,
        ),
        specs=[HBM] * 4,
        scratch=[pltpu.VMEM((1, tokens), jnp.int32), pltpu.SemaphoreType.DMA((4,))],
        name="pack",
    )
    *packed, shares = call(
        functools.partial(pack_more_kernel, most, order[LEADING:]),
        [block] * (wide - LEADING) + [like(partials)],
        place,
        weights,
        scales,
        grads,
        *pinned(partials),
        specs=[VMEM] * 4 + [HBM],
        scratch=[pltpu.SemaphoreType.DMA((narrow,))],
        name="pack_more",
    )
    packed = dict(zip(order, leading + packed))

    def across(k, rows_of_k):
        return [rows_of_k] + [swap(rows_of_k, "tp", j, f"rows{k}") for j in range(1, narrow)]

    taken = {0: across(0, packed[0])}
    first = groups[0][0]
    arrived = {}
    for k in order:
        if k:
            given = packed[k] if k in groups[0] else after(packed[k], arrived[first])
            arrived[k] = swap(given, "ep", k, f"rows{k}")
            if len(groups) > 1 and k == groups[1][0]:
                arrived[k] = after(arrived[k], packed[first], 1 << 31)
    fetched = [
        pre_acts.reshape(2, wide, narrow * most, hidden_width),
        w_down[0],
        w_gate[0],
        w_up[0],
        latent,
        latent_gain.reshape(1, -1),
    ]
    factors = pltpu.VMEM((wide, narrow * most, hidden_width), f32)
    up_by, gate_by, down, gate, up, latent, latent_gain = call(
        functools.partial(fetch_kernel, most),
        [factors, factors] + [like(array) for array in fetched[1:]],
        *pinned(*fetched),
        specs=[HBM] * len(fetched),
        scratch=[like(fetched[0]), pltpu.SemaphoreType.DMA((len(fetched),))],
        earlier=[arrived[first]],
        name="fetch",
    )
    latent_parts = [shares[0]] + [
        swap(shares[j], "tp", j, "latent") for j in range(1, narrow)
    ]

    def give_back(k, mine, others):
        others = [swap(other, "tp", j + 1, f"back{k}") for j, other in enumerate(others)]
        total = mine.astype(f32)
        for other in others:
            total += other.astype(f32)
        total = total.astype(bf16)
        return total, swap(total, "ep", k, f"back{k}")

    returned = {}
    own, waiting = [], []
    values = latent.astype(f32)
    received, products, moved = None, None, None
    for group in groups:
        for k in group:
            if k == 0:
                continue
            taken[k] = across(k, arrived[k])
            if received is not None:
                taken[k][-1] = after(taken[k][-1], products[0])
            elif k != first and narrow > 1:
                taken[k][-1] = after(taken[k][-1], packed[first], 1 << 31)
        count = len(group) * narrow * most
        extra = group is groups[-1]
        if extra:
            if received is not None:
                latent_parts[-1] = after(latent_parts[-1], summed, 1 << 28)
            own_grad = sum(part.astype(f32) for part in latent_parts)
            gained = own_grad * latent_gain
            row_sums = jnp.stack(
                [jnp.sum(values * values, axis=1), jnp.sum(gained * values, axis=1)]
            )
        summed, sent = call(
            functools.partial(hidden_kernel, most, extra),
            [
                pltpu.VMEM((count, hidden_width), f32),
                pltpu.VMEM((count + (EXTRA if extra else 0), hidden_width), bf16),
            ],
            *[rows_of_k for k in group for rows_of_k in taken[k]],
            *([row_sums] if extra else []),
            down,
            name="hidden",
            earlier=products[:1] if products else (),
        )
        for k, mine, others in waiting:
            others = [after(other, summed) for other in others]
            returned[k] = give_back(k, mine, others)[1]
        waiting = []
        received = swap(sent, "sub", 1, f"hidden{group[0]}")
        if moved is not None:
            received = after(received, moved)
        products = call(
            functools.partial(back_kernel, most, group),
            [block] * (len(group) * narrow),
            summed,
            received,
            up_by,
            gate_by,
            gate,
            up,
            name="back",
        )
        for at, k in enumerate(group):
            mine, others = products[at * narrow], products[at * narrow + 1 : (at + 1) * narrow]
            if k == 0:
                returned[0], own = mine, others
            elif k != group[0] and not extra:
                waiting.append((k, mine, others))
            else:
                total, returned[k] = give_back(k, mine, others)
                if k == group[0]:
                    moved = total
    own = [swap(after(value, moved), "tp", j + 1, "back0") for j, value in enumerate(own)]
    tail = received[count : count + 4, :tokens].astype(f32)
    row_sums = row_sums + tail[:2] + tail[2:]
    inverse_rms = lax.rsqrt(row_sums[0] / LAT + 1e-06)[:, None]
    d_latent = (
        inverse_rms * gained - values * inverse_rms**3 * row_sums[1][:, None] / LAT
    ).astype(bf16)
    latest = groups[-1][:1] if len(groups) > 1 else []
    distances = [k for k in sorted(returned, reverse=True) if k not in latest]
    (grad_input,) = call(
        functools.partial(unpack_kernel, distances, False),
        [pltpu.VMEM((tokens, width), bf16) if latest else jax.ShapeDtypeStruct((tokens, width), bf16)],
        place,
        *[returned[k] for k in distances],
        *own,
        name="unpack",
    )
    if latest:
        (grad_input,) = call(
            functools.partial(unpack_kernel, latest, True),
            [jax.ShapeDtypeStruct((tokens, width), bf16)],
            place,
            *[returned[k] for k in latest],
            grad_input,
            outs_in=ANY,
            scratch=[pltpu.VMEM((2, tokens, half), bf16), pltpu.SemaphoreType.DMA((2,))],
            name="unpack_latest",
        )
    return (grad_input, d_latent)


def solution(mesh):
    placed = (
        P(("rep", "ep", "tp"), "sub"),
        P(("rep", "ep", "tp"), "sub"),
        P(("rep", "ep", "tp"), None),
        P(("rep", "ep", "tp"), None),
        P("ep", "sub", "tp"),
        P("ep", "sub", "tp"),
        P("ep", "tp", "sub"),
        P(("rep", "ep"), None, None, "tp"),
        P("tp", ("rep", "ep"), "sub"),
        P(("rep", "ep", "tp"), "sub"),
        P("sub"),
    )
    return jax.shard_map(
        local,
        mesh=mesh,
        in_specs=placed,
        out_specs=(P(("rep", "ep", "tp"), "sub"), P(("rep", "ep", "tp"), "sub")),
        check_vma=False,
    )
```

```python
import functools

import jax
import jax.numpy as jnp
from jax import lax
from jax.experimental import pallas as pl
from jax.experimental.pallas import tpu as pltpu
from jax.sharding import PartitionSpec as P

LAT = 512
NT = (((1,), (1,)), ((), ()))
TN = (((0,), (0,)), ((), ()))
VMEM = pl.BlockSpec(memory_space=pltpu.VMEM)
ANY = pl.BlockSpec(memory_space=pl.ANY)
HBM = pl.BlockSpec(memory_space=pltpu.HBM)
EXTRA = 16
LEADING = 2
VMEM_LIMIT = 20 * 1024 * 1024


def dot(a, b, dims, precision=None):
    return lax.dot_general(a, b, dims, precision=precision, preferred_element_type=jnp.float32)


def swap(value, axis, step, what):
    count = lax.axis_size(axis)
    with jax.named_scope(f"{what}_{axis}"):
        return lax.ppermute(value, axis, [(i, i ^ step) for i in range(count)])


def pinned(*arrays):
    return [pltpu.with_memory_space_constraint(array, pltpu.HBM) for array in arrays]


def like(array):
    return pltpu.VMEM(array.shape, array.dtype)


def call(kernel, outs, *args, cost=0, name=None, specs=None, outs_in=VMEM, scratch=(), earlier=()):
    specs = (specs or [VMEM] * len(args)) + [ANY] * len(earlier)
    if earlier:
        taken, body = len(args), kernel

        def kernel(*refs):
            body(*refs[:taken], *refs[taken + len(earlier) :])

    return pl.pallas_call(
        kernel,
        out_shape=outs,
        in_specs=specs,
        out_specs=[outs_in] * len(outs),
        scratch_shapes=scratch,
        compiler_params=pltpu.CompilerParams(vmem_limit_bytes=VMEM_LIMIT),
        cost_estimate=pl.CostEstimate(flops=cost, bytes_accessed=0, transcendentals=0),
        name=name,
    )(*args, *earlier)


def after(value, earlier, cost=0):
    return pl.pallas_call(
        lambda value_ref, earlier_ref, out_ref: None,
        out_shape=jax.ShapeDtypeStruct(value.shape, value.dtype),
        in_specs=[ANY, ANY],
        out_specs=ANY,
        input_output_aliases={0: 0},
        compiler_params=pltpu.CompilerParams(vmem_limit_bytes=1 << 17),
        cost_estimate=pl.CostEstimate(flops=cost, bytes_accessed=0, transcendentals=0),
        name="after",
    )(value, earlier)


def fill(blocks, found, weights_ref, scales_ref, grad_ref):
    half, scale_half = grad_ref.shape[1] // 2, scales_ref.shape[0] // 2
    low, high = [
        jnp.concatenate([pair[side].astype(jnp.float32) for pair in found], axis=0)
        for side in range(2)
    ]
    placed = jnp.dot(
        low.astype(jnp.bfloat16), grad_ref[:, :half], preferred_element_type=jnp.float32
    )
    placed += jnp.dot(
        high.astype(jnp.bfloat16), grad_ref[:, half:], preferred_element_type=jnp.float32
    )
    scale = dot(low, scales_ref[:scale_half], NT, lax.Precision.HIGHEST)
    scale += dot(high, scales_ref[scale_half:], NT, lax.Precision.HIGHEST)
    weight = jnp.sum((low + high) * weights_ref[...], axis=1, keepdims=True)
    rows = blocks[0].shape[0]
    for at, block_ref in enumerate(blocks):
        own = slice(at * rows, (at + 1) * rows)
        for b in range(scale_half):
            part = slice(b * 128, (b + 1) * 128)
            block_ref[:, part] = (placed[own, part] * scale[own, b : b + 1] * weight[own]).astype(
                jnp.bfloat16
            )


def fetch(sources, targets, sems, first=0):
    copies = [
        pltpu.make_async_copy(source, target, sems.at[first + i])
        for i, (source, target) in enumerate(zip(sources, targets))
    ]
    for copy in copies:
        copy.start()
    return copies


def pack_kernel(most, order, leading, *refs):
    given, refs = refs[:4], refs[4:]
    blocks, (place_ref, *held), (ids_ref, sems) = refs[:leading], refs[leading:-2], refs[-2:]
    held = [ids_ref] + held
    copies = fetch(given, held, sems)
    copies[0].wait()
    weights_ref, scales_ref, grad_ref = held[1:]
    tokens, rows = grad_ref.shape[0], blocks[0].shape[0]
    me = lax.axis_index("ep")
    ids = ids_ref[...]
    expert = lax.broadcasted_iota(jnp.int32, (max(8, len(order)), tokens), 0)
    named = expert == ids
    before = lax.broadcasted_iota(jnp.int32, (tokens, tokens), 0) < lax.broadcasted_iota(
        jnp.int32, (tokens, tokens), 1
    )
    earlier = jnp.dot(
        named.astype(jnp.bfloat16), before.astype(jnp.bfloat16), preferred_element_type=jnp.float32
    )
    position = jnp.sum(jnp.where(named, earlier, 0.0), axis=0, keepdims=True).astype(jnp.int32)
    row = lax.broadcasted_iota(jnp.int32, (rows, tokens), 0)
    found = []
    for k in order:
        local = jnp.where(ids == (me ^ k), position, -2 * rows)
        low, high = row == local, row - most == local
        found.append((low, high))
        place_ref[0, k] = low.astype(jnp.bfloat16)
        place_ref[1, k] = high.astype(jnp.bfloat16)
    for copy in copies[1:]:
        copy.wait()
    fill(blocks, found[: len(blocks)], weights_ref, scales_ref, grad_ref)


def pack_more_kernel(most, order, place_ref, weights_ref, scales_ref, grad_ref, partial_ref, *refs):
    blocks, (share_ref, sems) = refs[:-2], refs[-2:]
    lane, count = lax.axis_index("tp"), partial_ref.shape[0]
    shares = fetch(
        [partial_ref.at[lane ^ j] for j in range(count)],
        [share_ref.at[j] for j in range(count)],
        sems,
    )
    found = [(place_ref[0, k], place_ref[1, k]) for k in order]
    fill(blocks, found, weights_ref, scales_ref, grad_ref)
    for copy in shares:
        copy.wait()


def by_xor(value, most, narrow, lane):
    step = 1
    while step < narrow:
        pieces = [value[i * most : (i + step) * most] for i in range(0, narrow, step)]
        turned = [pieces[i ^ 1] for i in range(len(pieces))]
        value = jnp.where((lane & step) != 0, jnp.concatenate(turned, axis=0), value)
        step *= 2
    return value


def fetch_kernel(most, *refs):
    pre_ref, sems = refs[-2:]
    wide = pre_ref.shape[1]
    narrow = pre_ref.shape[2] // most
    count = (len(refs) - 3) // 2
    given, (up_ref, gate_ref, *held) = refs[:count], refs[count:-2]
    copies = fetch(given, [pre_ref] + held, sems)
    me, lane = lax.axis_index("ep"), lax.axis_index("tp")
    copies[0].wait()
    for k in range(wide):
        gate_pre, up_pre = [
            by_xor(pre_ref[i, me ^ k].astype(jnp.float32), most, narrow, lane) for i in range(2)
        ]
        sig = 1.0 / (1.0 + jnp.exp(-gate_pre))
        up_ref[k] = gate_pre * sig
        gate_ref[k] = up_pre * sig * (1.0 + gate_pre * (1.0 - sig))
    for copy in copies[1:]:
        copy.wait()


def hidden_kernel(most, extra, *refs):
    blocks, (down_ref, sum_ref, sent_ref) = refs[:-3], refs[-3:]
    half = down_ref.shape[1] // 2
    count = sum_ref.shape[0]
    if extra:
        blocks, row_sums = blocks[:-1], blocks[-1][...]
        high = row_sums.astype(jnp.bfloat16).astype(jnp.float32)
        spare = jnp.zeros((EXTRA - 4, row_sums.shape[1]), jnp.float32)
        tail = jnp.concatenate([high, row_sums - high, spare], axis=0)
        sent_ref[count:, :] = jnp.zeros((EXTRA, sent_ref.shape[1]), jnp.bfloat16)
        sent_ref[count:, : row_sums.shape[1]] = tail.astype(jnp.bfloat16)
    values = [b[...].astype(jnp.float32) for b in blocks]
    low = jnp.concatenate([v[:most] for v in values], axis=0).astype(jnp.bfloat16)
    high = jnp.concatenate([v[most : 2 * most] for v in values], axis=0).astype(jnp.bfloat16)
    total = dot(low, down_ref[:, :half], NT) + dot(high, down_ref[:, half:], NT)
    sum_ref[...] = total
    sent_ref[:count, :] = total.astype(jnp.bfloat16)


def back_kernel(most, group, sum_ref, other_ref, up_by_ref, gate_by_ref, gate_ref, up_ref, *outs):
    half = gate_ref.shape[0] // 2
    hidden = sum_ref[...] + other_ref[: sum_ref.shape[0], :].astype(jnp.float32)
    up_by, gate_by = [
        jnp.concatenate([by_ref[k] for k in group], axis=0) for by_ref in (up_by_ref, gate_by_ref)
    ]
    up_grad = (hidden * up_by).astype(jnp.bfloat16)
    gate_grad = (hidden * gate_by).astype(jnp.bfloat16)
    low = dot(gate_grad, gate_ref[:half], NT) + dot(up_grad, up_ref[:half], NT)
    high = dot(gate_grad, gate_ref[half:], NT) + dot(up_grad, up_ref[half:], NT)
    for i, out in enumerate(outs):
        part = slice(i * most, (i + 1) * most)
        pieces = [low[part], high[part]]
        spare = out.shape[0] - 2 * most
        if spare:
            pieces.append(jnp.zeros((spare, half), jnp.float32))
        out[...] = jnp.concatenate(pieces, axis=0).astype(jnp.bfloat16)


def unpack_kernel(distances, started, place_ref, *refs):
    if started:
        refs, held_ref, sems = refs[:-2], refs[-2], refs[-1]
    blocks, others, out_ref = refs[: len(distances)], refs[len(distances) : -1], refs[-1]
    if started:
        others, so_far_ref = others[:-1], others[-1]
    half = out_ref.shape[1] // 2
    copies = []
    for side in range(2):
        columns = slice(side * half, (side + 1) * half)
        total = so_far_ref[:, columns].astype(jnp.float32) if started else 0.0
        for k, block_ref in zip(distances, blocks):
            rows = block_ref[...]
            if k == 0:
                rows = rows.astype(jnp.float32)
                for other_ref in others:
                    rows += other_ref[...].astype(jnp.float32)
                rows = rows.astype(jnp.bfloat16)
            total = total + dot(place_ref[side, k], rows, TN)
        if started:
            held_ref[side] = total.astype(jnp.bfloat16)
            copies.append(
                pltpu.make_async_copy(
                    held_ref.at[side], out_ref.at[:, pl.ds(side * half, half)], sems.at[side]
                )
            )
            copies[-1].start()
        else:
            out_ref[:, columns] = total.astype(jnp.bfloat16)
    for copy in copies:
        copy.wait()


def groups_of(wide):
    if wide < 4:
        return [list(range(wide - 1, -1, -1))]
    left = list(range(wide - 2, 1, -1))
    return [[wide - 1, 1, 0]] + [left[i : i + 2] for i in range(0, len(left), 2)]


def local(
    grad_values,
    grad_scales,
    expert_ids,
    route_weights,
    w_gate,
    w_up,
    w_down,
    pre_acts,
    latent_partials,
    latent,
    latent_gain,
):
    wide, narrow = lax.axis_size("ep"), lax.axis_size("tp")
    tokens, width = grad_values.shape
    half = width // 2
    slots, hidden_width = pre_acts.shape[2:]
    most = slots // (wide * narrow)
    rows = -(-2 * most // 8) * 8
    f32, bf16 = jnp.float32, jnp.bfloat16
    block = pltpu.VMEM((rows, half), bf16)
    groups = groups_of(wide)
    order = [k for group in groups for k in group]
    partials = latent_partials.reshape(narrow, tokens, latent.shape[1])
    *leading, place, weights, scales, grads = call(
        functools.partial(pack_kernel, most, order, LEADING),
        [block] * LEADING
        + [
            pltpu.VMEM((2, wide, rows, tokens), bf16),
            pltpu.VMEM((1, tokens), f32),
            pltpu.VMEM((grad_scales.shape[1], tokens), f32),
            pltpu.VMEM((tokens, width), bf16),
        ],
        *pinned(
            expert_ids.reshape(1, tokens),
            route_weights.reshape(1, tokens),
            grad_scales.T,
            grad_values,
        ),
        specs=[HBM] * 4,
        scratch=[pltpu.VMEM((1, tokens), jnp.int32), pltpu.SemaphoreType.DMA((4,))],
        name="pack",
    )
    *packed, shares = call(
        functools.partial(pack_more_kernel, most, order[LEADING:]),
        [block] * (wide - LEADING) + [like(partials)],
        place,
        weights,
        scales,
        grads,
        *pinned(partials),
        specs=[VMEM] * 4 + [HBM],
        scratch=[pltpu.SemaphoreType.DMA((narrow,))],
        name="pack_more",
    )
    packed = dict(zip(order, leading + packed))

    def across(k, rows_of_k):
        return [rows_of_k] + [swap(rows_of_k, "tp", j, f"rows{k}") for j in range(1, narrow)]

    taken = {0: across(0, packed[0])}
    first = groups[0][0]
    arrived = {}
    for k in order:
        if k:
            given = packed[k] if k in groups[0] else after(packed[k], arrived[first])
            arrived[k] = swap(given, "ep", k, f"rows{k}")
            if len(groups) > 1 and k == groups[1][0]:
                arrived[k] = after(arrived[k], packed[first], 1 << 31)
    fetched = [
        pre_acts.reshape(2, wide, narrow * most, hidden_width),
        w_down[0],
        w_gate[0],
        w_up[0],
        latent,
        latent_gain.reshape(1, -1),
    ]
    factors = pltpu.VMEM((wide, narrow * most, hidden_width), f32)
    up_by, gate_by, down, gate, up, latent, latent_gain = call(
        functools.partial(fetch_kernel, most),
        [factors, factors] + [like(array) for array in fetched[1:]],
        *pinned(*fetched),
        specs=[HBM] * len(fetched),
        scratch=[like(fetched[0]), pltpu.SemaphoreType.DMA((len(fetched),))],
        earlier=[arrived[first]],
        name="fetch",
    )
    latent_parts = [shares[0]] + [
        swap(shares[j], "tp", j, "latent") for j in range(1, narrow)
    ]

    def give_back(k, mine, others):
        others = [swap(other, "tp", j + 1, f"back{k}") for j, other in enumerate(others)]
        total = mine.astype(f32)
        for other in others:
            total += other.astype(f32)
        total = total.astype(bf16)
        return total, swap(total, "ep", k, f"back{k}")

    returned = {}
    own, waiting = [], []
    values = latent.astype(f32)
    received, products, moved = None, None, None
    for group in groups:
        for k in group:
            if k == 0:
                continue
            taken[k] = across(k, arrived[k])
            if received is not None:
                taken[k][-1] = after(taken[k][-1], products[0])
            elif k != first and narrow > 1:
                taken[k][-1] = after(taken[k][-1], packed[first], 1 << 31)
        count = len(group) * narrow * most
        extra = group is groups[-1]
        if extra:
            if received is not None:
                latent_parts[-1] = after(latent_parts[-1], summed, 1 << 28)
            own_grad = sum(part.astype(f32) for part in latent_parts)
            gained = own_grad * latent_gain
            row_sums = jnp.stack(
                [jnp.sum(values * values, axis=1), jnp.sum(gained * values, axis=1)]
            )
        summed, sent = call(
            functools.partial(hidden_kernel, most, extra),
            [
                pltpu.VMEM((count, hidden_width), f32),
                pltpu.VMEM((count + (EXTRA if extra else 0), hidden_width), bf16),
            ],
            *[rows_of_k for k in group for rows_of_k in taken[k]],
            *([row_sums] if extra else []),
            down,
            name="hidden",
            earlier=products[:1] if products else (),
        )
        for k, mine, others in waiting:
            others = [after(other, summed) for other in others]
            returned[k] = give_back(k, mine, others)[1]
        waiting = []
        received = swap(sent, "sub", 1, f"hidden{group[0]}")
        if moved is not None:
            received = after(received, moved)
        products = call(
            functools.partial(back_kernel, most, group),
            [block] * (len(group) * narrow),
            summed,
            received,
            up_by,
            gate_by,
            gate,
            up,
            name="back",
        )
        for at, k in enumerate(group):
            mine, others = products[at * narrow], products[at * narrow + 1 : (at + 1) * narrow]
            if k == 0:
                returned[0], own = mine, others
            elif k != group[0] and not extra:
                waiting.append((k, mine, others))
            else:
                total, returned[k] = give_back(k, mine, others)
                if k == group[0]:
                    moved = total
    own = [swap(after(value, moved), "tp", j + 1, "back0") for j, value in enumerate(own)]
    tail = received[count : count + 4, :tokens].astype(f32)
    row_sums = row_sums + tail[:2] + tail[2:]
    inverse_rms = lax.rsqrt(row_sums[0] / LAT + 1e-06)[:, None]
    d_latent = (
        inverse_rms * gained - values * inverse_rms**3 * row_sums[1][:, None] / LAT
    ).astype(bf16)
    latest = groups[-1][:1] if len(groups) > 1 else []
    distances = [k for k in sorted(returned, reverse=True) if k not in latest]
    (grad_input,) = call(
        functools.partial(unpack_kernel, distances, False),
        [pltpu.VMEM((tokens, width), bf16) if latest else jax.ShapeDtypeStruct((tokens, width), bf16)],
        place,
        *[returned[k] for k in distances],
        *own,
        name="unpack",
    )
    if latest:
        (grad_input,) = call(
            functools.partial(unpack_kernel, latest, True),
            [jax.ShapeDtypeStruct((tokens, width), bf16)],
            place,
            *[returned[k] for k in latest],
            grad_input,
            outs_in=ANY,
            scratch=[pltpu.VMEM((2, tokens, half), bf16), pltpu.SemaphoreType.DMA((2,))],
            name="unpack_latest",
        )
    return (grad_input, d_latent)


def solution(mesh):
    placed = (
        P(("rep", "ep", "tp"), "sub"),
        P(("rep", "ep", "tp"), "sub"),
        P(("rep", "ep", "tp"), None),
        P(("rep", "ep", "tp"), None),
        P("ep", "sub", "tp"),
        P("ep", "sub", "tp"),
        P("ep", "tp", "sub"),
        P(("rep", "ep"), None, None, "tp"),
        P("tp", ("rep", "ep"), "sub"),
        P(("rep", "ep", "tp"), "sub"),
        P("sub"),
    )
    return jax.shard_map(
        local,
        mesh=mesh,
        in_specs=placed,
        out_specs=(P(("rep", "ep", "tp"), "sub"), P(("rep", "ep", "tp"), "sub")),
        check_vma=False,
    )
```

```python
import functools

import jax
import jax.numpy as jnp
from jax import lax
from jax.experimental import pallas as pl
from jax.experimental.pallas import tpu as pltpu
from jax.sharding import PartitionSpec as P

LAT = 512
NT = (((1,), (1,)), ((), ()))
TN = (((0,), (0,)), ((), ()))
VMEM = pl.BlockSpec(memory_space=pltpu.VMEM)
ANY = pl.BlockSpec(memory_space=pl.ANY)
HBM = pl.BlockSpec(memory_space=pltpu.HBM)
EXTRA = 16
LEADING = 2
VMEM_LIMIT = 20 * 1024 * 1024


def dot(a, b, dims, precision=None):
    return lax.dot_general(a, b, dims, precision=precision, preferred_element_type=jnp.float32)


def swap(value, axis, step, what):
    count = lax.axis_size(axis)
    with jax.named_scope(f"{what}_{axis}"):
        return lax.ppermute(value, axis, [(i, i ^ step) for i in range(count)])


def pinned(*arrays):
    return [pltpu.with_memory_space_constraint(array, pltpu.HBM) for array in arrays]


def like(array):
    return pltpu.VMEM(array.shape, array.dtype)


def call(kernel, outs, *args, cost=0, name=None, specs=None, outs_in=VMEM, scratch=(), earlier=()):
    specs = (specs or [VMEM] * len(args)) + [ANY] * len(earlier)
    if earlier:
        taken, body = len(args), kernel

        def kernel(*refs):
            body(*refs[:taken], *refs[taken + len(earlier) :])

    return pl.pallas_call(
        kernel,
        out_shape=outs,
        in_specs=specs,
        out_specs=[outs_in] * len(outs),
        scratch_shapes=scratch,
        compiler_params=pltpu.CompilerParams(vmem_limit_bytes=VMEM_LIMIT),
        cost_estimate=pl.CostEstimate(flops=cost, bytes_accessed=0, transcendentals=0),
        name=name,
    )(*args, *earlier)


def after(value, earlier, cost=0):
    return pl.pallas_call(
        lambda value_ref, earlier_ref, out_ref: None,
        out_shape=jax.ShapeDtypeStruct(value.shape, value.dtype),
        in_specs=[ANY, ANY],
        out_specs=ANY,
        input_output_aliases={0: 0},
        compiler_params=pltpu.CompilerParams(vmem_limit_bytes=1 << 17),
        cost_estimate=pl.CostEstimate(flops=cost, bytes_accessed=0, transcendentals=0),
        name="after",
    )(value, earlier)


def fill(blocks, found, weights_ref, scales_ref, grad_ref):
    half, scale_half = grad_ref.shape[1] // 2, scales_ref.shape[0] // 2
    low, high = [
        jnp.concatenate([pair[side].astype(jnp.float32) for pair in found], axis=0)
        for side in range(2)
    ]
    placed = jnp.dot(
        low.astype(jnp.bfloat16), grad_ref[:, :half], preferred_element_type=jnp.float32
    )
    placed += jnp.dot(
        high.astype(jnp.bfloat16), grad_ref[:, half:], preferred_element_type=jnp.float32
    )
    scale = dot(low, scales_ref[:scale_half], NT, lax.Precision.HIGHEST)
    scale += dot(high, scales_ref[scale_half:], NT, lax.Precision.HIGHEST)
    weight = jnp.sum((low + high) * weights_ref[...], axis=1, keepdims=True)
    rows = blocks[0].shape[0]
    for at, block_ref in enumerate(blocks):
        own = slice(at * rows, (at + 1) * rows)
        for b in range(scale_half):
            part = slice(b * 128, (b + 1) * 128)
            block_ref[:, part] = (placed[own, part] * scale[own, b : b + 1] * weight[own]).astype(
                jnp.bfloat16
            )


def fetch(sources, targets, sems, first=0):
    copies = [
        pltpu.make_async_copy(source, target, sems.at[first + i])
        for i, (source, target) in enumerate(zip(sources, targets))
    ]
    for copy in copies:
        copy.start()
    return copies


def pack_kernel(most, order, leading, *refs):
    given, refs = refs[:4], refs[4:]
    blocks, (place_ref, *held), (ids_ref, sems) = refs[:leading], refs[leading:-2], refs[-2:]
    held = [ids_ref] + held
    copies = fetch(given, held, sems)
    copies[0].wait()
    weights_ref, scales_ref, grad_ref = held[1:]
    tokens, rows = grad_ref.shape[0], blocks[0].shape[0]
    me = lax.axis_index("ep")
    ids = ids_ref[...]
    expert = lax.broadcasted_iota(jnp.int32, (max(8, len(order)), tokens), 0)
    named = expert == ids
    before = lax.broadcasted_iota(jnp.int32, (tokens, tokens), 0) < lax.broadcasted_iota(
        jnp.int32, (tokens, tokens), 1
    )
    earlier = jnp.dot(
        named.astype(jnp.bfloat16), before.astype(jnp.bfloat16), preferred_element_type=jnp.float32
    )
    position = jnp.sum(jnp.where(named, earlier, 0.0), axis=0, keepdims=True).astype(jnp.int32)
    row = lax.broadcasted_iota(jnp.int32, (rows, tokens), 0)
    found = []
    for k in order:
        local = jnp.where(ids == (me ^ k), position, -2 * rows)
        low, high = row == local, row - most == local
        found.append((low, high))
        place_ref[0, k] = low.astype(jnp.bfloat16)
        place_ref[1, k] = high.astype(jnp.bfloat16)
    for copy in copies[1:]:
        copy.wait()
    fill(blocks, found[: len(blocks)], weights_ref, scales_ref, grad_ref)


def pack_more_kernel(most, order, place_ref, weights_ref, scales_ref, grad_ref, partial_ref, *refs):
    blocks, (share_ref, sems) = refs[:-2], refs[-2:]
    lane, count = lax.axis_index("tp"), partial_ref.shape[0]
    shares = fetch(
        [partial_ref.at[lane ^ j] for j in range(count)],
        [share_ref.at[j] for j in range(count)],
        sems,
    )
    for block_ref, k in zip(blocks, order):
        fill([block_ref], [(place_ref[0, k], place_ref[1, k])], weights_ref, scales_ref, grad_ref)
    for copy in shares:
        copy.wait()


def by_xor(value, most, narrow, lane):
    step = 1
    while step < narrow:
        pieces = [value[i * most : (i + step) * most] for i in range(0, narrow, step)]
        turned = [pieces[i ^ 1] for i in range(len(pieces))]
        value = jnp.where((lane & step) != 0, jnp.concatenate(turned, axis=0), value)
        step *= 2
    return value


def fetch_kernel(most, *refs):
    pre_ref, sems = refs[-2:]
    wide = pre_ref.shape[1]
    narrow = pre_ref.shape[2] // most
    count = (len(refs) - 3) // 2
    given, (up_ref, gate_ref, *held) = refs[:count], refs[count:-2]
    copies = fetch(given, [pre_ref] + held, sems)
    me, lane = lax.axis_index("ep"), lax.axis_index("tp")
    copies[0].wait()
    for k in range(wide):
        gate_pre, up_pre = [
            by_xor(pre_ref[i, me ^ k].astype(jnp.float32), most, narrow, lane) for i in range(2)
        ]
        sig = 1.0 / (1.0 + jnp.exp(-gate_pre))
        up_ref[k] = gate_pre * sig
        gate_ref[k] = up_pre * sig * (1.0 + gate_pre * (1.0 - sig))
    for copy in copies[1:]:
        copy.wait()


def hidden_kernel(most, extra, *refs):
    blocks, (down_ref, sum_ref, sent_ref) = refs[:-3], refs[-3:]
    half = down_ref.shape[1] // 2
    count = sum_ref.shape[0]
    if extra:
        blocks, row_sums = blocks[:-1], blocks[-1][...]
        high = row_sums.astype(jnp.bfloat16).astype(jnp.float32)
        spare = jnp.zeros((EXTRA - 4, row_sums.shape[1]), jnp.float32)
        tail = jnp.concatenate([high, row_sums - high, spare], axis=0)
        sent_ref[count:, :] = jnp.zeros((EXTRA, sent_ref.shape[1]), jnp.bfloat16)
        sent_ref[count:, : row_sums.shape[1]] = tail.astype(jnp.bfloat16)
    values = [b[...].astype(jnp.float32) for b in blocks]
    low = jnp.concatenate([v[:most] for v in values], axis=0).astype(jnp.bfloat16)
    high = jnp.concatenate([v[most : 2 * most] for v in values], axis=0).astype(jnp.bfloat16)
    total = dot(low, down_ref[:, :half], NT) + dot(high, down_ref[:, half:], NT)
    sum_ref[...] = total
    sent_ref[:count, :] = total.astype(jnp.bfloat16)


def back_kernel(most, group, sum_ref, other_ref, up_by_ref, gate_by_ref, gate_ref, up_ref, *outs):
    half = gate_ref.shape[0] // 2
    hidden = sum_ref[...] + other_ref[: sum_ref.shape[0], :].astype(jnp.float32)
    up_by, gate_by = [
        jnp.concatenate([by_ref[k] for k in group], axis=0) for by_ref in (up_by_ref, gate_by_ref)
    ]
    up_grad = (hidden * up_by).astype(jnp.bfloat16)
    gate_grad = (hidden * gate_by).astype(jnp.bfloat16)
    low = dot(gate_grad, gate_ref[:half], NT) + dot(up_grad, up_ref[:half], NT)
    high = dot(gate_grad, gate_ref[half:], NT) + dot(up_grad, up_ref[half:], NT)
    for i, out in enumerate(outs):
        part = slice(i * most, (i + 1) * most)
        pieces = [low[part], high[part]]
        spare = out.shape[0] - 2 * most
        if spare:
            pieces.append(jnp.zeros((spare, half), jnp.float32))
        out[...] = jnp.concatenate(pieces, axis=0).astype(jnp.bfloat16)


def unpack_kernel(distances, started, place_ref, *refs):
    if started:
        refs, held_ref, sems = refs[:-2], refs[-2], refs[-1]
    blocks, others, out_ref = refs[: len(distances)], refs[len(distances) : -1], refs[-1]
    if started:
        others, so_far_ref = others[:-1], others[-1]
    half = out_ref.shape[1] // 2
    copies = []
    for side in range(2):
        columns = slice(side * half, (side + 1) * half)
        total = so_far_ref[:, columns].astype(jnp.float32) if started else 0.0
        for k, block_ref in zip(distances, blocks):
            rows = block_ref[...]
            if k == 0:
                rows = rows.astype(jnp.float32)
                for other_ref in others:
                    rows += other_ref[...].astype(jnp.float32)
                rows = rows.astype(jnp.bfloat16)
            total = total + dot(place_ref[side, k], rows, TN)
        if started:
            held_ref[side] = total.astype(jnp.bfloat16)
            copies.append(
                pltpu.make_async_copy(
                    held_ref.at[side], out_ref.at[:, pl.ds(side * half, half)], sems.at[side]
                )
            )
            copies[-1].start()
        else:
            out_ref[:, columns] = total.astype(jnp.bfloat16)
    for copy in copies:
        copy.wait()


def groups_of(wide):
    if wide < 4:
        return [list(range(wide - 1, -1, -1))]
    left = list(range(wide - 2, 1, -1))
    return [[wide - 1, 1, 0]] + [left[i : i + 2] for i in range(0, len(left), 2)]


def local(
    grad_values,
    grad_scales,
    expert_ids,
    route_weights,
    w_gate,
    w_up,
    w_down,
    pre_acts,
    latent_partials,
    latent,
    latent_gain,
):
    wide, narrow = lax.axis_size("ep"), lax.axis_size("tp")
    tokens, width = grad_values.shape
    half = width // 2
    slots, hidden_width = pre_acts.shape[2:]
    most = slots // (wide * narrow)
    rows = -(-2 * most // 8) * 8
    f32, bf16 = jnp.float32, jnp.bfloat16
    block = pltpu.VMEM((rows, half), bf16)
    groups = groups_of(wide)
    order = [k for group in groups for k in group]
    partials = latent_partials.reshape(narrow, tokens, latent.shape[1])
    *leading, place, weights, scales, grads = call(
        functools.partial(pack_kernel, most, order, LEADING),
        [block] * LEADING
        + [
            pltpu.VMEM((2, wide, rows, tokens), bf16),
            pltpu.VMEM((1, tokens), f32),
            pltpu.VMEM((grad_scales.shape[1], tokens), f32),
            pltpu.VMEM((tokens, width), bf16),
        ],
        *pinned(
            expert_ids.reshape(1, tokens),
            route_weights.reshape(1, tokens),
            grad_scales.T,
            grad_values,
        ),
        specs=[HBM] * 4,
        scratch=[pltpu.VMEM((1, tokens), jnp.int32), pltpu.SemaphoreType.DMA((4,))],
        name="pack",
    )
    *packed, shares = call(
        functools.partial(pack_more_kernel, most, order[LEADING:]),
        [block] * (wide - LEADING) + [like(partials)],
        place,
        weights,
        scales,
        grads,
        *pinned(partials),
        specs=[VMEM] * 4 + [HBM],
        scratch=[pltpu.SemaphoreType.DMA((narrow,))],
        name="pack_more",
    )
    packed = dict(zip(order, leading + packed))

    def across(k, rows_of_k):
        return [rows_of_k] + [swap(rows_of_k, "tp", j, f"rows{k}") for j in range(1, narrow)]

    taken = {0: across(0, packed[0])}
    first = groups[0][0]
    arrived = {}
    for k in order:
        if k:
            given = packed[k] if k in groups[0] else after(packed[k], arrived[first])
            arrived[k] = swap(given, "ep", k, f"rows{k}")
            if len(groups) > 1 and k == groups[1][0]:
                arrived[k] = after(arrived[k], packed[first], 1 << 31)
    fetched = [
        pre_acts.reshape(2, wide, narrow * most, hidden_width),
        w_down[0],
        w_gate[0],
        w_up[0],
        latent,
        latent_gain.reshape(1, -1),
    ]
    factors = pltpu.VMEM((wide, narrow * most, hidden_width), f32)
    up_by, gate_by, down, gate, up, latent, latent_gain = call(
        functools.partial(fetch_kernel, most),
        [factors, factors] + [like(array) for array in fetched[1:]],
        *pinned(*fetched),
        specs=[HBM] * len(fetched),
        scratch=[like(fetched[0]), pltpu.SemaphoreType.DMA((len(fetched),))],
        earlier=[arrived[first]],
        name="fetch",
    )
    latent_parts = [shares[0]] + [
        swap(shares[j], "tp", j, "latent") for j in range(1, narrow)
    ]

    def give_back(k, mine, others):
        others = [swap(other, "tp", j + 1, f"back{k}") for j, other in enumerate(others)]
        total = mine.astype(f32)
        for other in others:
            total += other.astype(f32)
        total = total.astype(bf16)
        return total, swap(total, "ep", k, f"back{k}")

    returned = {}
    own, waiting = [], []
    values = latent.astype(f32)
    received, products, moved = None, None, None
    for group in groups:
        for k in group:
            if k == 0:
                continue
            taken[k] = across(k, arrived[k])
            if received is not None:
                taken[k][-1] = after(taken[k][-1], products[0])
            elif k != first and narrow > 1:
                taken[k][-1] = after(taken[k][-1], packed[first], 1 << 31)
        count = len(group) * narrow * most
        extra = group is groups[-1]
        if extra:
            if received is not None:
                latent_parts[-1] = after(latent_parts[-1], summed, 1 << 28)
            own_grad = sum(part.astype(f32) for part in latent_parts)
            gained = own_grad * latent_gain
            row_sums = jnp.stack(
                [jnp.sum(values * values, axis=1), jnp.sum(gained * values, axis=1)]
            )
        summed, sent = call(
            functools.partial(hidden_kernel, most, extra),
            [
                pltpu.VMEM((count, hidden_width), f32),
                pltpu.VMEM((count + (EXTRA if extra else 0), hidden_width), bf16),
            ],
            *[rows_of_k for k in group for rows_of_k in taken[k]],
            *([row_sums] if extra else []),
            down,
            name="hidden",
            earlier=products[:1] if products else (),
        )
        for k, mine, others in waiting:
            others = [after(other, summed) for other in others]
            returned[k] = give_back(k, mine, others)[1]
        waiting = []
        received = swap(sent, "sub", 1, f"hidden{group[0]}")
        if moved is not None:
            received = after(received, moved)
        products = call(
            functools.partial(back_kernel, most, group),
            [block] * (len(group) * narrow),
            summed,
            received,
            up_by,
            gate_by,
            gate,
            up,
            name="back",
        )
        for at, k in enumerate(group):
            mine, others = products[at * narrow], products[at * narrow + 1 : (at + 1) * narrow]
            if k == 0:
                returned[0], own = mine, others
            elif k != group[0] and not extra:
                waiting.append((k, mine, others))
            else:
                total, returned[k] = give_back(k, mine, others)
                if k == group[0]:
                    moved = total
    own = [swap(after(value, moved), "tp", j + 1, "back0") for j, value in enumerate(own)]
    tail = received[count : count + 4, :tokens].astype(f32)
    row_sums = row_sums + tail[:2] + tail[2:]
    inverse_rms = lax.rsqrt(row_sums[0] / LAT + 1e-06)[:, None]
    d_latent = (
        inverse_rms * gained - values * inverse_rms**3 * row_sums[1][:, None] / LAT
    ).astype(bf16)
    latest = groups[-1][:1] if len(groups) > 1 else []
    distances = [k for k in sorted(returned, reverse=True) if k not in latest]
    (grad_input,) = call(
        functools.partial(unpack_kernel, distances, False),
        [pltpu.VMEM((tokens, width), bf16) if latest else jax.ShapeDtypeStruct((tokens, width), bf16)],
        place,
        *[returned[k] for k in distances],
        *own,
        name="unpack",
    )
    if latest:
        (grad_input,) = call(
            functools.partial(unpack_kernel, latest, True),
            [jax.ShapeDtypeStruct((tokens, width), bf16)],
            place,
            *[returned[k] for k in latest],
            grad_input,
            outs_in=ANY,
            scratch=[pltpu.VMEM((2, tokens, half), bf16), pltpu.SemaphoreType.DMA((2,))],
            name="unpack_latest",
        )
    return (grad_input, d_latent)


def solution(mesh):
    placed = (
        P(("rep", "ep", "tp"), "sub"),
        P(("rep", "ep", "tp"), "sub"),
        P(("rep", "ep", "tp"), None),
        P(("rep", "ep", "tp"), None),
        P("ep", "sub", "tp"),
        P("ep", "sub", "tp"),
        P("ep", "tp", "sub"),
        P(("rep", "ep"), None, None, "tp"),
        P("tp", ("rep", "ep"), "sub"),
        P(("rep", "ep", "tp"), "sub"),
        P("sub"),
    )
    return jax.shard_map(
        local,
        mesh=mesh,
        in_specs=placed,
        out_specs=(P(("rep", "ep", "tp"), "sub"), P(("rep", "ep", "tp"), "sub")),
        check_vma=False,
    )
```

```python
import functools

import jax
import jax.numpy as jnp
from jax import lax
from jax.experimental import pallas as pl
from jax.experimental.pallas import tpu as pltpu
from jax.sharding import PartitionSpec as P

LAT = 512
NT = (((1,), (1,)), ((), ()))
TN = (((0,), (0,)), ((), ()))
VMEM = pl.BlockSpec(memory_space=pltpu.VMEM)
ANY = pl.BlockSpec(memory_space=pl.ANY)
HBM = pl.BlockSpec(memory_space=pltpu.HBM)
EXTRA = 16
LEADING = 2
VMEM_LIMIT = 20 * 1024 * 1024


def dot(a, b, dims, precision=None):
    return lax.dot_general(a, b, dims, precision=precision, preferred_element_type=jnp.float32)


def swap(value, axis, step, what):
    count = lax.axis_size(axis)
    with jax.named_scope(f"{what}_{axis}"):
        return lax.ppermute(value, axis, [(i, i ^ step) for i in range(count)])


def pinned(*arrays):
    return [pltpu.with_memory_space_constraint(array, pltpu.HBM) for array in arrays]


def like(array):
    return pltpu.VMEM(array.shape, array.dtype)


def call(kernel, outs, *args, cost=0, name=None, specs=None, outs_in=VMEM, scratch=(), earlier=()):
    specs = (specs or [VMEM] * len(args)) + [ANY] * len(earlier)
    if earlier:
        taken, body = len(args), kernel

        def kernel(*refs):
            body(*refs[:taken], *refs[taken + len(earlier) :])

    return pl.pallas_call(
        kernel,
        out_shape=outs,
        in_specs=specs,
        out_specs=[outs_in] * len(outs),
        scratch_shapes=scratch,
        compiler_params=pltpu.CompilerParams(vmem_limit_bytes=VMEM_LIMIT),
        cost_estimate=pl.CostEstimate(flops=cost, bytes_accessed=0, transcendentals=0),
        name=name,
    )(*args, *earlier)


def after(value, earlier, cost=0):
    return pl.pallas_call(
        lambda value_ref, earlier_ref, out_ref: None,
        out_shape=jax.ShapeDtypeStruct(value.shape, value.dtype),
        in_specs=[ANY, ANY],
        out_specs=ANY,
        input_output_aliases={0: 0},
        compiler_params=pltpu.CompilerParams(vmem_limit_bytes=1 << 17),
        cost_estimate=pl.CostEstimate(flops=cost, bytes_accessed=0, transcendentals=0),
        name="after",
    )(value, earlier)


def fill(blocks, found, weights_ref, scales_ref, grad_ref):
    half, scale_half = grad_ref.shape[1] // 2, scales_ref.shape[0] // 2
    low, high = [
        jnp.concatenate([pair[side].astype(jnp.float32) for pair in found], axis=0)
        for side in range(2)
    ]
    placed = jnp.dot(
        low.astype(jnp.bfloat16), grad_ref[:, :half], preferred_element_type=jnp.float32
    )
    placed += jnp.dot(
        high.astype(jnp.bfloat16), grad_ref[:, half:], preferred_element_type=jnp.float32
    )
    scale = dot(low, scales_ref[:scale_half], NT, lax.Precision.HIGHEST)
    scale += dot(high, scales_ref[scale_half:], NT, lax.Precision.HIGHEST)
    scale = scale * jnp.sum((low + high) * weights_ref[...], axis=1, keepdims=True)
    rows = blocks[0].shape[0]
    for at, block_ref in enumerate(blocks):
        own = slice(at * rows, (at + 1) * rows)
        for b in range(scale_half):
            part = slice(b * 128, (b + 1) * 128)
            block_ref[:, part] = (placed[own, part] * scale[own, b : b + 1]).astype(jnp.bfloat16)


def fetch(sources, targets, sems, first=0):
    copies = [
        pltpu.make_async_copy(source, target, sems.at[first + i])
        for i, (source, target) in enumerate(zip(sources, targets))
    ]
    for copy in copies:
        copy.start()
    return copies


def pack_kernel(most, order, leading, *refs):
    given, refs = refs[:4], refs[4:]
    blocks, (place_ref, *held), (ids_ref, sems) = refs[:leading], refs[leading:-2], refs[-2:]
    held = [ids_ref] + held
    copies = fetch(given, held, sems)
    copies[0].wait()
    weights_ref, scales_ref, grad_ref = held[1:]
    tokens, rows = grad_ref.shape[0], blocks[0].shape[0]
    me = lax.axis_index("ep")
    ids = ids_ref[...]
    expert = lax.broadcasted_iota(jnp.int32, (max(8, len(order)), tokens), 0)
    named = expert == ids
    before = lax.broadcasted_iota(jnp.int32, (tokens, tokens), 0) < lax.broadcasted_iota(
        jnp.int32, (tokens, tokens), 1
    )
    earlier = jnp.dot(
        named.astype(jnp.bfloat16), before.astype(jnp.bfloat16), preferred_element_type=jnp.float32
    )
    position = jnp.sum(jnp.where(named, earlier, 0.0), axis=0, keepdims=True).astype(jnp.int32)
    row = lax.broadcasted_iota(jnp.int32, (rows, tokens), 0)
    found = []
    for k in order:
        local = jnp.where(ids == (me ^ k), position, -2 * rows)
        low, high = row == local, row - most == local
        found.append((low, high))
        place_ref[0, k] = low.astype(jnp.bfloat16)
        place_ref[1, k] = high.astype(jnp.bfloat16)
    for copy in copies[1:]:
        copy.wait()
    fill(blocks, found[: len(blocks)], weights_ref, scales_ref, grad_ref)


def pack_more_kernel(most, order, place_ref, weights_ref, scales_ref, grad_ref, partial_ref, *refs):
    blocks, (share_ref, sems) = refs[:-2], refs[-2:]
    lane, count = lax.axis_index("tp"), partial_ref.shape[0]
    shares = fetch(
        [partial_ref.at[lane ^ j] for j in range(count)],
        [share_ref.at[j] for j in range(count)],
        sems,
    )
    for block_ref, k in zip(blocks, order):
        fill([block_ref], [(place_ref[0, k], place_ref[1, k])], weights_ref, scales_ref, grad_ref)
    for copy in shares:
        copy.wait()


def by_xor(value, most, narrow, lane):
    step = 1
    while step < narrow:
        pieces = [value[i * most : (i + step) * most] for i in range(0, narrow, step)]
        turned = [pieces[i ^ 1] for i in range(len(pieces))]
        value = jnp.where((lane & step) != 0, jnp.concatenate(turned, axis=0), value)
        step *= 2
    return value


def fetch_kernel(most, *refs):
    pre_ref, sems = refs[-2:]
    wide = pre_ref.shape[1]
    narrow = pre_ref.shape[2] // most
    count = (len(refs) - 3) // 2
    given, (up_ref, gate_ref, *held) = refs[:count], refs[count:-2]
    copies = fetch(given, [pre_ref] + held, sems)
    me, lane = lax.axis_index("ep"), lax.axis_index("tp")
    copies[0].wait()
    for k in range(wide):
        gate_pre, up_pre = [
            by_xor(pre_ref[i, me ^ k].astype(jnp.float32), most, narrow, lane) for i in range(2)
        ]
        sig = 1.0 / (1.0 + jnp.exp(-gate_pre))
        up_ref[k] = gate_pre * sig
        gate_ref[k] = up_pre * sig * (1.0 + gate_pre * (1.0 - sig))
    for copy in copies[1:]:
        copy.wait()


def hidden_kernel(most, extra, *refs):
    blocks, (down_ref, sum_ref, sent_ref) = refs[:-3], refs[-3:]
    half = down_ref.shape[1] // 2
    count = sum_ref.shape[0]
    if extra:
        blocks, row_sums = blocks[:-1], blocks[-1][...]
        high = row_sums.astype(jnp.bfloat16).astype(jnp.float32)
        spare = jnp.zeros((EXTRA - 4, row_sums.shape[1]), jnp.float32)
        tail = jnp.concatenate([high, row_sums - high, spare], axis=0)
        sent_ref[count:, :] = jnp.zeros((EXTRA, sent_ref.shape[1]), jnp.bfloat16)
        sent_ref[count:, : row_sums.shape[1]] = tail.astype(jnp.bfloat16)
    values = [b[...].astype(jnp.float32) for b in blocks]
    low = jnp.concatenate([v[:most] for v in values], axis=0).astype(jnp.bfloat16)
    high = jnp.concatenate([v[most : 2 * most] for v in values], axis=0).astype(jnp.bfloat16)
    total = dot(low, down_ref[:, :half], NT) + dot(high, down_ref[:, half:], NT)
    sum_ref[...] = total
    sent_ref[:count, :] = total.astype(jnp.bfloat16)


def back_kernel(most, group, sum_ref, other_ref, up_by_ref, gate_by_ref, gate_ref, up_ref, *outs):
    half = gate_ref.shape[0] // 2
    hidden = sum_ref[...] + other_ref[: sum_ref.shape[0], :].astype(jnp.float32)
    up_by, gate_by = [
        jnp.concatenate([by_ref[k] for k in group], axis=0) for by_ref in (up_by_ref, gate_by_ref)
    ]
    up_grad = (hidden * up_by).astype(jnp.bfloat16)
    gate_grad = (hidden * gate_by).astype(jnp.bfloat16)
    low = dot(gate_grad, gate_ref[:half], NT) + dot(up_grad, up_ref[:half], NT)
    high = dot(gate_grad, gate_ref[half:], NT) + dot(up_grad, up_ref[half:], NT)
    for i, out in enumerate(outs):
        part = slice(i * most, (i + 1) * most)
        pieces = [low[part], high[part]]
        spare = out.shape[0] - 2 * most
        if spare:
            pieces.append(jnp.zeros((spare, half), jnp.float32))
        out[...] = jnp.concatenate(pieces, axis=0).astype(jnp.bfloat16)


def unpack_kernel(distances, started, place_ref, *refs):
    if started:
        refs, held_ref, sems = refs[:-2], refs[-2], refs[-1]
    blocks, others, out_ref = refs[: len(distances)], refs[len(distances) : -1], refs[-1]
    if started:
        others, so_far_ref = others[:-1], others[-1]
    half = out_ref.shape[1] // 2
    copies = []
    for side in range(2):
        columns = slice(side * half, (side + 1) * half)
        total = so_far_ref[:, columns].astype(jnp.float32) if started else 0.0
        for k, block_ref in zip(distances, blocks):
            rows = block_ref[...]
            if k == 0:
                rows = rows.astype(jnp.float32)
                for other_ref in others:
                    rows += other_ref[...].astype(jnp.float32)
                rows = rows.astype(jnp.bfloat16)
            total = total + dot(place_ref[side, k], rows, TN)
        if started:
            held_ref[side] = total.astype(jnp.bfloat16)
            copies.append(
                pltpu.make_async_copy(
                    held_ref.at[side], out_ref.at[:, pl.ds(side * half, half)], sems.at[side]
                )
            )
            copies[-1].start()
        else:
            out_ref[:, columns] = total.astype(jnp.bfloat16)
    for copy in copies:
        copy.wait()


def groups_of(wide):
    if wide < 4:
        return [list(range(wide - 1, -1, -1))]
    left = list(range(wide - 2, 1, -1))
    return [[wide - 1, 1, 0]] + [left[i : i + 2] for i in range(0, len(left), 2)]


def local(
    grad_values,
    grad_scales,
    expert_ids,
    route_weights,
    w_gate,
    w_up,
    w_down,
    pre_acts,
    latent_partials,
    latent,
    latent_gain,
):
    wide, narrow = lax.axis_size("ep"), lax.axis_size("tp")
    tokens, width = grad_values.shape
    half = width // 2
    slots, hidden_width = pre_acts.shape[2:]
    most = slots // (wide * narrow)
    rows = -(-2 * most // 8) * 8
    f32, bf16 = jnp.float32, jnp.bfloat16
    block = pltpu.VMEM((rows, half), bf16)
    groups = groups_of(wide)
    order = [k for group in groups for k in group]
    partials = latent_partials.reshape(narrow, tokens, latent.shape[1])
    *leading, place, weights, scales, grads = call(
        functools.partial(pack_kernel, most, order, LEADING),
        [block] * LEADING
        + [
            pltpu.VMEM((2, wide, rows, tokens), bf16),
            pltpu.VMEM((1, tokens), f32),
            pltpu.VMEM((grad_scales.shape[1], tokens), f32),
            pltpu.VMEM((tokens, width), bf16),
        ],
        *pinned(
            expert_ids.reshape(1, tokens),
            route_weights.reshape(1, tokens),
            grad_scales.T,
            grad_values,
        ),
        specs=[HBM] * 4,
        scratch=[pltpu.VMEM((1, tokens), jnp.int32), pltpu.SemaphoreType.DMA((4,))],
        name="pack",
    )
    *packed, shares = call(
        functools.partial(pack_more_kernel, most, order[LEADING:]),
        [block] * (wide - LEADING) + [like(partials)],
        place,
        weights,
        scales,
        grads,
        *pinned(partials),
        specs=[VMEM] * 4 + [HBM],
        scratch=[pltpu.SemaphoreType.DMA((narrow,))],
        name="pack_more",
    )
    packed = dict(zip(order, leading + packed))

    def across(k, rows_of_k):
        return [rows_of_k] + [swap(rows_of_k, "tp", j, f"rows{k}") for j in range(1, narrow)]

    taken = {0: across(0, packed[0])}
    first = groups[0][0]
    arrived = {}
    for k in order:
        if k:
            given = packed[k] if k in groups[0] else after(packed[k], arrived[first])
            arrived[k] = swap(given, "ep", k, f"rows{k}")
            if len(groups) > 1 and k == groups[1][0]:
                arrived[k] = after(arrived[k], packed[first], 1 << 31)
    fetched = [
        pre_acts.reshape(2, wide, narrow * most, hidden_width),
        w_down[0],
        w_gate[0],
        w_up[0],
        latent,
        latent_gain.reshape(1, -1),
    ]
    factors = pltpu.VMEM((wide, narrow * most, hidden_width), f32)
    up_by, gate_by, down, gate, up, latent, latent_gain = call(
        functools.partial(fetch_kernel, most),
        [factors, factors] + [like(array) for array in fetched[1:]],
        *pinned(*fetched),
        specs=[HBM] * len(fetched),
        scratch=[like(fetched[0]), pltpu.SemaphoreType.DMA((len(fetched),))],
        earlier=[arrived[first]],
        name="fetch",
    )
    latent_parts = [shares[0]] + [
        swap(shares[j], "tp", j, "latent") for j in range(1, narrow)
    ]

    def give_back(k, mine, others):
        others = [swap(other, "tp", j + 1, f"back{k}") for j, other in enumerate(others)]
        total = mine.astype(f32)
        for other in others:
            total += other.astype(f32)
        total = total.astype(bf16)
        return total, swap(total, "ep", k, f"back{k}")

    returned = {}
    own, waiting = [], []
    values = latent.astype(f32)
    received, products, moved = None, None, None
    for group in groups:
        for k in group:
            if k == 0:
                continue
            taken[k] = across(k, arrived[k])
            if received is not None:
                taken[k][-1] = after(taken[k][-1], products[0])
            elif k != first and narrow > 1:
                taken[k][-1] = after(taken[k][-1], packed[first], 1 << 31)
        count = len(group) * narrow * most
        extra = group is groups[-1]
        if extra:
            if received is not None:
                latent_parts[-1] = after(latent_parts[-1], summed, 1 << 28)
            own_grad = sum(part.astype(f32) for part in latent_parts)
            gained = own_grad * latent_gain
            row_sums = jnp.stack(
                [jnp.sum(values * values, axis=1), jnp.sum(gained * values, axis=1)]
            )
        summed, sent = call(
            functools.partial(hidden_kernel, most, extra),
            [
                pltpu.VMEM((count, hidden_width), f32),
                pltpu.VMEM((count + (EXTRA if extra else 0), hidden_width), bf16),
            ],
            *[rows_of_k for k in group for rows_of_k in taken[k]],
            *([row_sums] if extra else []),
            down,
            name="hidden",
            earlier=products[:1] if products else (),
        )
        for k, mine, others in waiting:
            others = [after(other, summed) for other in others]
            returned[k] = give_back(k, mine, others)[1]
        waiting = []
        received = swap(sent, "sub", 1, f"hidden{group[0]}")
        if moved is not None:
            received = after(received, moved)
        products = call(
            functools.partial(back_kernel, most, group),
            [block] * (len(group) * narrow),
            summed,
            received,
            up_by,
            gate_by,
            gate,
            up,
            name="back",
        )
        for at, k in enumerate(group):
            mine, others = products[at * narrow], products[at * narrow + 1 : (at + 1) * narrow]
            if k == 0:
                returned[0], own = mine, others
            elif k != group[0] and not extra:
                waiting.append((k, mine, others))
            else:
                total, returned[k] = give_back(k, mine, others)
                if k == group[0]:
                    moved = total
    own = [swap(after(value, moved), "tp", j + 1, "back0") for j, value in enumerate(own)]
    tail = received[count : count + 4, :tokens].astype(f32)
    row_sums = row_sums + tail[:2] + tail[2:]
    inverse_rms = lax.rsqrt(row_sums[0] / LAT + 1e-06)[:, None]
    d_latent = (
        inverse_rms * gained - values * inverse_rms**3 * row_sums[1][:, None] / LAT
    ).astype(bf16)
    latest = groups[-1][:1] if len(groups) > 1 else []
    distances = [k for k in sorted(returned, reverse=True) if k not in latest]
    (grad_input,) = call(
        functools.partial(unpack_kernel, distances, False),
        [pltpu.VMEM((tokens, width), bf16) if latest else jax.ShapeDtypeStruct((tokens, width), bf16)],
        place,
        *[returned[k] for k in distances],
        *own,
        name="unpack",
    )
    if latest:
        (grad_input,) = call(
            functools.partial(unpack_kernel, latest, True),
            [jax.ShapeDtypeStruct((tokens, width), bf16)],
            place,
            *[returned[k] for k in latest],
            grad_input,
            outs_in=ANY,
            scratch=[pltpu.VMEM((2, tokens, half), bf16), pltpu.SemaphoreType.DMA((2,))],
            name="unpack_latest",
        )
    return (grad_input, d_latent)


def solution(mesh):
    placed = (
        P(("rep", "ep", "tp"), "sub"),
        P(("rep", "ep", "tp"), "sub"),
        P(("rep", "ep", "tp"), None),
        P(("rep", "ep", "tp"), None),
        P("ep", "sub", "tp"),
        P("ep", "sub", "tp"),
        P("ep", "tp", "sub"),
        P(("rep", "ep"), None, None, "tp"),
        P("tp", ("rep", "ep"), "sub"),
        P(("rep", "ep", "tp"), "sub"),
        P("sub"),
    )
    return jax.shard_map(
        local,
        mesh=mesh,
        in_specs=placed,
        out_specs=(P(("rep", "ep", "tp"), "sub"), P(("rep", "ep", "tp"), "sub")),
        check_vma=False,
    )
```
